32 devices in a mesh: dp: 4 (over y, core), seq: 8 (over z, x).
Axes of the slice: x: 2, y: 2, z: 4, core: 2. Of those that a mesh axis runs over, the one named last changes fastest.
Arguments:
- tokens: bfloat16 [8, 2048, 1024], P('dp', 'seq'), may hold values from -6 to 6
- first_gain: float32 [1024], replicated, may hold values from 0.25 to 1.75
- first_shift: float32 [1024], replicated, may hold values from -1.5 to 1.5
- project_weight: bfloat16 [1024, 3072], replicated, may hold values from -0.1875 to 0.1875
- query_bias: float32 [1024], replicated, may hold values from -1.5 to 1.5
- value_bias: float32 [1024], replicated, may hold values from -1.5 to 1.5
- output_weight: bfloat16 [1024, 1024], replicated, may hold values from -1 to 1
- output_bias: float32 [1024], replicated, may hold values from -1.5 to 1.5
- second_gain: float32 [1024], replicated, may hold values from 0.25 to 1.75
- second_shift: float32 [1024], replicated, may hold values from -1.5 to 1.5
- up_weight: bfloat16 [1024, 4096], replicated, may hold values from -0.1875 to 0.1875
- up_bias: float32 [4096], replicated, may hold values from -1.5 to 1.5
- down_weight: bfloat16 [4096, 1024], replicated, may hold values from -0.09375 to 0.09375
- down_bias: float32 [1024], replicated, may hold values from -1.5 to 1.5
- doc_offsets: int32 [8, 4], P('dp'), may hold values from 0 to 2048, as said below
- exit_layers: int32 [8, 2048], P('dp'), may hold values from 1 to 24, as said below
- layer_index: int32 [1], replicated, may hold values from 6 to 11
- upstream: bfloat16 [8, 2048, 1024], P('dp', 'seq'), may hold values from -6 to 6
Outputs:
- result: bfloat16 [8, 2048, 1024], P('dp', 'seq')
- token_grad: bfloat16 [8, 2048, 1024], P('dp', 'seq')
- first_gain_grad: float32 [1024], P(('dp', 'seq'))
- first_shift_grad: float32 [1024], P(('dp', 'seq'))
- project_weight_grad: float32 [1024, 3072], P(('dp', 'seq'))
- query_bias_grad: float32 [1024], P(('dp', 'seq'))
- value_bias_grad: float32 [1024], P(('dp', 'seq'))
- output_weight_grad: float32 [1024, 1024], P(('dp', 'seq'))
- output_bias_grad: float32 [1024], P(('dp', 'seq'))
- second_gain_grad: float32 [1024], P(('dp', 'seq'))
- second_shift_grad: float32 [1024], P(('dp', 'seq'))
- up_weight_grad: float32 [1024, 4096], P(('dp', 'seq'))
- up_bias_grad: float32 [4096], P(('dp', 'seq'))
- down_weight_grad: float32 [4096, 1024], P(('dp', 'seq'))
- down_bias_grad: float32 [1024], P(('dp', 'seq'))
The draws below stay inside these ranges and needn't reach their ends.
Inputs may be any that keep to these rules, and one draw needn't show every extreme that they name: `doc_offsets`: each row's offsets start at 0 and never fall; document j runs from offset j to offset j + 1 (the last to 2048); an offset of 2048 marks an empty document. In every aligned group of 2 rows one row has a document that begins within the first device's tokens of the row and ends within the last device's tokens. `exit_layers`: the first token of every document has exit layer 24.
All inputs are finite; a program needn't handle non-finite values.
Results may differ from the reference program's by a relative error of at most 0.011.
Values may be sent and summed in bfloat16 or wider, within the bound.
A program may use at most 192 MiB of HBM per device.

```python
import jax
import jax.numpy as jnp
from jax import lax

D = 1024
HEADS = 16
HEAD_DIM = 64
FF = 4096
NLAYERS = 24
SEQ_LEN = 2048
DOCS = 4
TOK_DEV = 512
ROWS_GRP = 2
ROWS = 8


def doc_starts(key):
    cuts = jax.random.randint(key, (ROWS, DOCS - 1), 1, SEQ_LEN)
    cuts = jnp.sort(cuts, axis=1)
    group_count = ROWS // ROWS_GRP
    chosen = jax.random.randint(jax.random.fold_in(key, 11), (group_count,), 0, ROWS_GRP)
    row_ids = jnp.arange(ROWS, dtype=jnp.int32)
    single = row_ids % ROWS_GRP == jnp.repeat(chosen, ROWS_GRP)
    shard_len = TOK_DEV // ROWS_GRP
    early_cut = jax.random.randint(jax.random.fold_in(key, 13), (ROWS,), 1, shard_len)
    late_cut = jax.random.randint(jax.random.fold_in(key, 17), (ROWS,), SEQ_LEN - shard_len + 1, SEQ_LEN)
    columns = jnp.arange(DOCS - 1, dtype=jnp.int32)[None, :]
    spanning = jnp.where(columns == 0, early_cut[:, None], jnp.where(columns == 1, late_cut[:, None], SEQ_LEN))
    cuts = jnp.where(single[:, None], spanning, cuts)
    return jnp.concatenate([jnp.zeros((ROWS, 1), jnp.int32), cuts.astype(jnp.int32)], axis=1)


def draw_doc_offsets(key, part):
    starts = doc_starts(key)
    return starts


def draw_exit_layers(key, part):
    starts = doc_starts(key)
    key = jax.random.fold_in(key, 7)
    places = jnp.arange(SEQ_LEN, dtype=jnp.int32)
    reached = starts[:, :, None] <= places[None, None, :]
    begin = jnp.max(jnp.where(reached, starts[:, :, None], 0), axis=1)
    within = places[None, :] - begin
    ceiling = NLAYERS - within * NLAYERS // (2 * SEQ_LEN)
    drawn = jax.random.randint(key, (ROWS, SEQ_LEN), 1, ceiling + 1)
    return jnp.where(within == 0, NLAYERS, drawn).astype(jnp.int32)


def levels(own_key, dims, shards, least, largest):
    factor_of, own = 1.0, jax.random.fold_in(own_key, 6)
    for dim, parts in shards:
        draws = jnp.exp(jax.random.uniform(jax.random.fold_in(own, dim), (parts,), jnp.float32, least / len(shards), largest / len(shards)))
        factor_of = factor_of * jnp.repeat(draws, dims[dim] // parts).reshape([-1 if axis == dim else 1 for axis in range(len(dims))])
    return factor_of


def normal_values(own_key, dims, width, limit, cuts=(), kind=jnp.bfloat16):
    array = width * jax.random.normal(own_key, dims, jnp.float32)
    if cuts:
        array = array * levels(own_key, dims, cuts, -0.22, 0.18)
    return jnp.clip(array, -limit, limit).astype(kind)


def setup_inputs(seed: int = 0) -> dict:
    arg_keys = jax.random.split(jax.random.key(seed), 19)
    tokens = normal_values(arg_keys[0], (ROWS, SEQ_LEN, D), 1.0, 6.0, ((0, 4), (1, 8)))
    first_gain = jnp.clip(1.0 + 0.15 * jax.random.normal(arg_keys[1], (D,), jnp.float32), 0.25, 1.75)
    first_shift = normal_values(arg_keys[2], (D,), 0.3, 1.5, (), jnp.float32)
    project_weight = normal_values(arg_keys[3], (D, 3 * D), D ** -0.5, 0.1875)
    query_bias = normal_values(arg_keys[4], (D,), 0.3, 1.5, (), jnp.float32)
    value_bias = normal_values(arg_keys[5], (D,), 0.3, 1.5, (), jnp.float32)
    output_weight = normal_values(arg_keys[6], (D, D), (D // 32) ** -0.5, 1.0)
    output_bias = normal_values(arg_keys[7], (D,), 0.3, 1.5, (), jnp.float32)
    second_gain = jnp.clip(1.0 + 0.15 * jax.random.normal(arg_keys[8], (D,), jnp.float32), 0.25, 1.75)
    second_shift = normal_values(arg_keys[9], (D,), 0.3, 1.5, (), jnp.float32)
    up_weight = normal_values(arg_keys[10], (D, FF), D ** -0.5, 0.1875)
    up_bias = normal_values(arg_keys[11], (FF,), 0.3, 1.5, (), jnp.float32)
    down_weight = normal_values(arg_keys[12], (FF, D), FF ** -0.5, 0.09375)
    down_bias = normal_values(arg_keys[13], (D,), 0.3, 1.5, (), jnp.float32)
    doc_offsets = draw_doc_offsets(jax.random.fold_in(arg_keys[18], 71), 0)
    exit_layers = draw_exit_layers(jax.random.fold_in(arg_keys[18], 71), 0)
    layer_index = jax.random.randint(arg_keys[16], (1,), NLAYERS // 4, NLAYERS // 2).astype(jnp.int32)
    upstream = normal_values(arg_keys[17], (ROWS, SEQ_LEN, D), 1.0, 6.0, ((0, 4), (1, 8)))
    return dict(tokens=tokens, first_gain=first_gain, first_shift=first_shift, project_weight=project_weight, query_bias=query_bias, value_bias=value_bias, output_weight=output_weight, output_bias=output_bias, second_gain=second_gain, second_shift=second_shift, up_weight=up_weight, up_bias=up_bias, down_weight=down_weight, down_bias=down_bias, doc_offsets=doc_offsets, exit_layers=exit_layers, layer_index=layer_index, upstream=upstream)


@jax.custom_vjp
def low(v):
    return lax.optimization_barrier(v.astype(jnp.bfloat16)).astype(jnp.float32)

@jax.custom_vjp
def low_back(v):
    return v

def low_keep(v):
    return (low(v), None)

def low_pass(kept, grad):
    return (grad,)

def back_keep(v):
    return (v, None)

def back_low(kept, grad):
    return (low(grad),)
low.defvjp(low_keep, low_pass)
low_back.defvjp(back_keep, back_low)

def layer_norm(inputs, gain_vec, bias_vec):
    average = lax.optimization_barrier(jnp.mean(inputs, axis=-1, keepdims=True))
    centred = inputs - average
    spread = lax.optimization_barrier(jnp.mean(centred * centred, axis=-1, keepdims=True))
    return centred * lax.rsqrt(spread + 1e-05) * gain_vec + bias_vec

def product(operand, weights_mat):
    return jnp.dot(operand, weights_mat, precision=lax.Precision.HIGHEST, preferred_element_type=jnp.float32)

def attend(queries, key_rows, value_rows, doc_row, live_row):
    places = jnp.arange(SEQ_LEN, dtype=jnp.int32)
    scores = jnp.einsum('qhd,khd->hqk', queries, key_rows, precision=lax.Precision.HIGHEST) * HEAD_DIM ** (-0.5)
    scores = low_back(scores)
    allowed = (doc_row[:, None] == doc_row[None, :]) & (places[None, :] <= places[:, None]) & live_row[None, :]
    masked = jnp.where(allowed[None], scores, -1e+30)
    highest = lax.optimization_barrier(jnp.max(masked, axis=2, keepdims=True))
    weights = jnp.exp(masked - highest)
    weights_low = low(weights / lax.optimization_barrier(jnp.sum(weights, axis=2, keepdims=True)))
    return jnp.einsum('hqk,khd->qhd', weights_low, value_rows, precision=lax.Precision.HIGHEST)

def reference(tokens, first_gain, first_shift, project_weight, query_bias, value_bias, output_weight, output_bias, second_gain, second_shift, up_weight, up_bias, down_weight, down_bias, doc_offsets, exit_layers, layer_index, upstream):
    places = jnp.arange(SEQ_LEN, dtype=jnp.int32)
    doc_ids = lax.optimization_barrier(jnp.sum((doc_offsets[:, 1:, None] <= places[None, None, :]).astype(jnp.int32), axis=1))
    active = exit_layers > layer_index[0]

    def whole(residual, first_gain, first_shift, project_weight, query_bias, value_bias, output_weight, output_bias, second_gain, second_shift, up_weight, up_bias, down_weight, down_bias):

        def one_row(packed):
            row_data, doc_row, live_row = packed
            keep_mask = live_row.astype(row_data.dtype)[:, None]
            normed = low(layer_norm(row_data, first_gain, first_shift))
            mixed = product(normed, project_weight)
            queries = low(low_back(mixed[:, :D] + query_bias))
            key_rows = low(low_back(mixed[:, D:2 * D]))
            value_rows = low(low_back(mixed[:, 2 * D:] + value_bias))
            head_shape = (SEQ_LEN, HEADS, HEAD_DIM)
            context = attend(queries.reshape(head_shape), key_rows.reshape(head_shape), value_rows.reshape(head_shape), doc_row, live_row)
            context = low(low_back(context.reshape(SEQ_LEN, D)))
            attended = low_back(product(context, output_weight) + output_bias)
            middle = row_data + keep_mask * attended
            normed_two = low(layer_norm(middle, second_gain, second_shift))
            raised = low_back(product(normed_two, up_weight) + up_bias)
            hidden = low(jax.nn.gelu(raised, approximate=True))
            return middle + keep_mask * (product(hidden, down_weight) + down_bias)
        return lax.map(jax.checkpoint(one_row), (residual, doc_ids, active))
    single = jnp.float32
    result, pullback = jax.vjp(whole, tokens.astype(single), first_gain.astype(single), first_shift.astype(single), project_weight.astype(single), query_bias.astype(single), value_bias.astype(single), output_weight.astype(single), output_bias.astype(single), second_gain.astype(single), second_shift.astype(single), up_weight.astype(single), up_bias.astype(single), down_weight.astype(single), down_bias.astype(single))
    grads = pullback(upstream.astype(single))
    return (result.astype(jnp.bfloat16), grads[0].astype(jnp.bfloat16), grads[1], grads[2], grads[3], grads[4], grads[5], grads[6], grads[7], grads[8], grads[9], grads[10], grads[11], grads[12], grads[13])
```

```python
import functools

import jax
import jax.numpy as jnp
from jax import lax
from jax.experimental import pallas as pl
from jax.experimental.pallas import tpu as pltpu
from jax.sharding import PartitionSpec as P

HEAD_DIM = 64
SCALE = HEAD_DIM**-0.5
TILE = 256
FAR = 2**30
NEG = -1e30
EPS = 1e-05
VMEM_LIMIT = 56 * 2**20
F32 = jnp.float32
BF16 = jnp.bfloat16

NT = (((1,), (1,)), ((), ()))
NN = (((1,), (0,)), ((), ()))


def dot(a, b, dims=NN):
    return lax.dot_general(a, b, dims, preferred_element_type=F32)


def any_spec():
    return pl.BlockSpec(memory_space=pltpu.VMEM)


def params(**kw):
    return pltpu.CompilerParams(vmem_limit_bytes=VMEM_LIMIT, **kw)


def centre_rows(x):
    centred = x - jnp.mean(x, axis=-1, keepdims=True)
    spread = jnp.mean(centred * centred, axis=-1, keepdims=True)
    rs = lax.rsqrt(spread + EPS)
    return centred * rs, rs


def qkv_kernel(group, me_ref, x_ref, gain_ref, shift_ref, w_ref, bias_ref, normed_ref, *outs):
    step = pl.program_id(0)

    @pl.when(step == 0)
    def _():
        n, _ = centre_rows(x_ref[...].astype(F32))
        normed_ref[...] = (n * gain_ref[...] + shift_ref[...]).astype(BF16)

    value = (dot(normed_ref[...], w_ref[0]) + bias_ref[0]).astype(BF16)
    for m in range(group):

        @pl.when(step == m)
        def _(m=m):
            outs[m][...] = value


def qkv_chunks(me, x, gain, shift, w_parts, bias_parts):
    group, width, cols = w_parts.shape
    rows = x.shape[0]
    whole = lambda m, me_ref: (0, 0)
    out = pl.pallas_call(
        functools.partial(qkv_kernel, group),
        grid_spec=pltpu.PrefetchScalarGridSpec(
            num_scalar_prefetch=1,
            grid=(group,),
            in_specs=[
                pl.BlockSpec((rows, width), whole),
                pl.BlockSpec((1, width), whole),
                pl.BlockSpec((1, width), whole),
                pl.BlockSpec((1, width, cols), lambda m, me_ref: (m ^ me_ref[0], 0, 0)),
                pl.BlockSpec((1, 1, cols), lambda m, me_ref: (m ^ me_ref[0], 0, 0)),
            ],
            out_specs=[pl.BlockSpec((rows, width), whole)]
            + [pl.BlockSpec((rows, cols), whole)] * group,
        ),
        out_shape=[jax.ShapeDtypeStruct((rows, width), BF16)]
        + [jax.ShapeDtypeStruct((rows, cols), BF16)] * group,
        compiler_params=params(),
        cost_estimate=pl.CostEstimate(
            flops=2 * rows * width * cols * group,
            bytes_accessed=2 * group * cols * (width + rows),
            transcendentals=0,
        ),
        name="norm_project",
    )(me, x, gain[None], shift[None], w_parts, bias_parts)
    return out[0], out[1:]


def head_mask(rows, wide, head):
    lane = lax.broadcasted_iota(jnp.int32, (rows, wide), 1)
    return lane // HEAD_DIM == head


def only_head(block, head, heads):
    if heads == 1:
        return block
    return jnp.where(head_mask(*block.shape, head), block, jnp.zeros_like(block))


def transposed(block):
    return block.astype(F32).T.astype(BF16)


def visible(key_pos, starts, spots, diagonal):
    seen = key_pos >= starts
    if diagonal:
        seen = seen & (key_pos <= spots)
    return seen


def attend_kernel(group, cap, tiles, heads, sc_ref, *refs):
    parts, refs = refs[:group], refs[group:]
    kp_ref, starts_ref, spots_ref = refs[:3]
    outs, refs = refs[3 : 3 + group], refs[3 + group :]
    lse_ref, q_s, k_s, v_s, vt_s, o_s = refs
    wide = heads * HEAD_DIM
    me = sc_ref[0]
    row = pl.program_id(0)
    for m in range(group):
        here = pl.ds(pl.multiple_of((me ^ m) * cap, cap), cap)
        q_s[here, :] = parts[m][:, :wide] * SCALE
        k_s[here, :] = parts[m][:, wide : 2 * wide]
        v_s[here, :] = parts[m][:, 2 * wide :]
    for t in range(tiles):
        vt_s[t] = transposed(v_s[t * TILE : (t + 1) * TILE, :])

    def one_tile(i, _):
        at = pl.ds(pl.multiple_of(i * TILE, TILE), TILE)
        queries = q_s[at, :]
        split = [only_head(queries, h, heads) for h in range(heads)]
        starts = starts_ref[0, i]
        spots = spots_ref[0, i]

        def step(j, carry, diagonal):
            there = pl.ds(pl.multiple_of(j * TILE, TILE), TILE)
            seen = visible(kp_ref[0, there, :], starts, spots, diagonal)
            keys = k_s[there, :]
            new = []
            for h in range(heads):
                top, total, acc = carry[h]
                s = jnp.where(seen, dot(keys, split[h], NT), NEG)
                top2 = jnp.maximum(top, jnp.max(s, axis=0, keepdims=True))
                p = jnp.exp(s - top2)
                fade = jnp.exp(top - top2)
                total = total * fade + jnp.sum(p, axis=0, keepdims=True)
                vt = vt_s[j, h * HEAD_DIM : (h + 1) * HEAD_DIM, :]
                acc = acc * fade + dot(vt, p.astype(BF16))
                new.append((top2, total, acc))
            return tuple(new)

        first = tuple(
            (
                jnp.full((1, TILE), NEG, F32),
                jnp.zeros((1, TILE), F32),
                jnp.zeros((HEAD_DIM, TILE), F32),
            )
            for _ in range(heads)
        )
        low = sc_ref[1 + row * tiles + i]
        carry = lax.fori_loop(low, i, lambda j, c: step(j, c, False), first)
        carry = step(i, carry, True)
        pieces = []
        for h in range(heads):
            top, total, acc = carry[h]
            pieces.append(acc * (1.0 / total))
            lse_ref[0, i, h : h + 1, :] = top + jnp.log(total)
        o_s[at, :] = jnp.concatenate(pieces, axis=0).T.astype(BF16)
        return 0

    lax.fori_loop(0, tiles, one_tile, 0)
    for m in range(group):
        outs[m][...] = o_s[pl.ds(pl.multiple_of((me ^ m) * cap, cap), cap), :]


def attend(scalars, parts, key_pos, starts, spots, cap, heads):
    group = len(parts)
    rows = parts[0].shape[0] // cap
    cols = parts[0].shape[1]
    length = group * cap
    tiles = length // TILE
    wide = heads * HEAD_DIM
    pair = rows * heads * length * length // 2 * HEAD_DIM
    by_row = lambda r, sc: (r, 0)
    out = pl.pallas_call(
        functools.partial(attend_kernel, group, cap, tiles, heads),
        grid_spec=pltpu.PrefetchScalarGridSpec(
            num_scalar_prefetch=1,
            grid=(rows,),
            in_specs=[pl.BlockSpec((cap, cols), by_row)] * group
            + [
                pl.BlockSpec((1, length, 1), lambda r, sc: (r, 0, 0)),
                pl.BlockSpec((1, tiles, 1, TILE), lambda r, sc: (r, 0, 0, 0)),
                pl.BlockSpec((1, tiles, 1, TILE), lambda r, sc: (r, 0, 0, 0)),
            ],
            out_specs=[pl.BlockSpec((cap, wide), by_row)] * group
            + [pl.BlockSpec((1, tiles, heads, TILE), lambda r, sc: (r, 0, 0, 0))],
            scratch_shapes=[
                pltpu.VMEM((length, wide), BF16),
                pltpu.VMEM((length, wide), BF16),
                pltpu.VMEM((length, wide), BF16),
                pltpu.VMEM((tiles, wide, TILE), BF16),
                pltpu.VMEM((length, wide), BF16),
            ],
        ),
        out_shape=[jax.ShapeDtypeStruct((rows * cap, wide), BF16)] * group
        + [jax.ShapeDtypeStruct((rows, tiles, heads, TILE), F32)],
        compiler_params=params(),
        cost_estimate=pl.CostEstimate(
            flops=4 * 4 * pair, bytes_accessed=8 * rows * length * wide, transcendentals=pair // 32
        ),
        name="attend",
    )(scalars, *parts, key_pos, starts, spots)
    return out[:group], out[group]


def attend_back_kernel(group, cap, tiles, heads, sc_ref, *refs):
    parts, refs = refs[:group], refs[group:]
    ctx, refs = refs[:group], refs[group:]
    grads, refs = refs[:group], refs[group:]
    kp_ref, starts_ref, spots_ref, lse_ref = refs[:4]
    outs, refs = refs[4 : 4 + group], refs[4 + group :]
    q_s, k_s, v_s, kt_s, g_s, o_s, dq_s, dk_s, dv_s = refs
    wide = heads * HEAD_DIM
    me = sc_ref[0]
    row = pl.program_id(0)
    for m in range(group):
        here = pl.ds(pl.multiple_of((me ^ m) * cap, cap), cap)
        q_s[here, :] = parts[m][:, :wide] * SCALE
        k_s[here, :] = parts[m][:, wide : 2 * wide]
        v_s[here, :] = parts[m][:, 2 * wide :]
        g_s[here, :] = grads[m][...]
        o_s[here, :] = ctx[m][...]
    for t in range(tiles):
        kt_s[t] = transposed(k_s[t * TILE : (t + 1) * TILE, :])
    dk_s[...] = jnp.zeros_like(dk_s)
    dv_s[...] = jnp.zeros_like(dv_s)

    def one_tile(i, _):
        at = pl.ds(pl.multiple_of(i * TILE, TILE), TILE)
        queries = q_s[at, :]
        grad = g_s[at, :]
        starts = starts_ref[0, i]
        spots = spots_ref[0, i]
        product = (grad.astype(F32) * o_s[at, :].astype(F32)).T
        split_q = [only_head(queries, h, heads) for h in range(heads)]
        split_g = [only_head(grad, h, heads) for h in range(heads)]
        delta = [
            jnp.sum(product[h * HEAD_DIM : (h + 1) * HEAD_DIM], axis=0, keepdims=True)
            for h in range(heads)
        ]
        lse = [lse_ref[0, i, h : h + 1, :] for h in range(heads)]

        def step(j, carry, diagonal):
            there = pl.ds(pl.multiple_of(j * TILE, TILE), TILE)
            seen = visible(kp_ref[0, there, :], starts, spots, diagonal)
            keys = k_s[there, :]
            values = v_s[there, :]
            new = []
            dk = dk_s[there, :]
            dv = dv_s[there, :]
            for h in range(heads):
                s = dot(keys, split_q[h], NT)
                p = jnp.where(seen, jnp.exp(s - lse[h]), 0.0)
                dp = dot(values, split_g[h], NT)
                ds = (p * (dp - delta[h])).astype(BF16)
                dv = dv + dot(p.astype(BF16), split_g[h])
                dk = dk + dot(ds, split_q[h])
                kt = kt_s[j, h * HEAD_DIM : (h + 1) * HEAD_DIM, :]
                new.append(carry[h] + dot(kt, ds))
            dk_s[there, :] = dk
            dv_s[there, :] = dv
            return tuple(new)

        first = tuple(jnp.zeros((HEAD_DIM, TILE), F32) for _ in range(heads))
        low = sc_ref[1 + row * tiles + i]
        carry = lax.fori_loop(low, i, lambda j, c: step(j, c, False), first)
        carry = step(i, carry, True)
        dq_s[at, :] = (jnp.concatenate(carry, axis=0).T * SCALE).astype(BF16)
        return 0

    lax.fori_loop(0, tiles, one_tile, 0)
    for m in range(group):
        here = pl.ds(pl.multiple_of((me ^ m) * cap, cap), cap)
        outs[m][:, :wide] = dq_s[here, :]
        outs[m][:, wide : 2 * wide] = dk_s[here, :].astype(BF16)
        outs[m][:, 2 * wide :] = dv_s[here, :].astype(BF16)


def attend_back(scalars, parts, ctx, grads, key_pos, starts, spots, lse, cap, heads):
    group = len(parts)
    rows = parts[0].shape[0] // cap
    cols = parts[0].shape[1]
    length = group * cap
    tiles = length // TILE
    wide = heads * HEAD_DIM
    pair = rows * heads * length * length // 2 * HEAD_DIM
    by_row = lambda r, sc: (r, 0)
    return pl.pallas_call(
        functools.partial(attend_back_kernel, group, cap, tiles, heads),
        grid_spec=pltpu.PrefetchScalarGridSpec(
            num_scalar_prefetch=1,
            grid=(rows,),
            in_specs=[pl.BlockSpec((cap, cols), by_row)] * group
            + [pl.BlockSpec((cap, wide), by_row)] * (2 * group)
            + [
                pl.BlockSpec((1, length, 1), lambda r, sc: (r, 0, 0)),
                pl.BlockSpec((1, tiles, 1, TILE), lambda r, sc: (r, 0, 0, 0)),
                pl.BlockSpec((1, tiles, 1, TILE), lambda r, sc: (r, 0, 0, 0)),
                pl.BlockSpec((1, tiles, heads, TILE), lambda r, sc: (r, 0, 0, 0)),
            ],
            out_specs=[pl.BlockSpec((cap, cols), by_row)] * group,
            scratch_shapes=[pltpu.VMEM((length, wide), BF16)] * 3
            + [pltpu.VMEM((tiles, wide, TILE), BF16)]
            + [pltpu.VMEM((length, wide), BF16)] * 3
            + [pltpu.VMEM((length, wide), F32)] * 2,
        ),
        out_shape=[jax.ShapeDtypeStruct((rows * cap, cols), BF16)] * group,
        compiler_params=params(),
        cost_estimate=pl.CostEstimate(
            flops=10 * 4 * pair, bytes_accessed=20 * rows * length * wide, transcendentals=pair // 32
        ),
        name="attend_back",
    )(scalars, *parts, *ctx, *grads, key_pos, starts, spots, lse)


def gather_parts(me, parts, ordered):
    for m in range(len(parts)):
        ordered[me ^ m] = parts[m][...]


def output_kernel(group, sc_ref, *refs):
    parts, refs = refs[:group], refs[group:]
    x_ref, w_ref, bias_ref, gain_ref, shift_ref, ctx_ref, mid_ref, normed_ref, ordered = refs
    wide = parts[0].shape[1]
    gather_parts(sc_ref[0], parts, ordered)
    for s in range(group):
        ctx_ref[:, s * wide : (s + 1) * wide] = ordered[s]
    mid = x_ref[...].astype(F32) + dot(ctx_ref[...], w_ref[...]) + bias_ref[...]
    mid_ref[...] = mid
    n, _ = centre_rows(mid)
    normed_ref[...] = (n * gain_ref[...] + shift_ref[...]).astype(BF16)


def output_project(me, parts, x, w, bias, gain, shift):
    group = len(parts)
    rows, width = x.shape
    wide = parts[0].shape[1]
    return pl.pallas_call(
        functools.partial(output_kernel, group),
        in_specs=[pl.BlockSpec(memory_space=pltpu.SMEM)] + [any_spec()] * (group + 5),
        out_specs=[any_spec()] * 3,
        out_shape=[
            jax.ShapeDtypeStruct((rows, width), BF16),
            jax.ShapeDtypeStruct((rows, width), F32),
            jax.ShapeDtypeStruct((rows, width), BF16),
        ],
        scratch_shapes=[pltpu.VMEM((group, rows, wide), BF16)],
        compiler_params=params(),
        cost_estimate=pl.CostEstimate(
            flops=2 * rows * width * width,
            bytes_accessed=2 * width * width + 12 * rows * width,
            transcendentals=0,
        ),
        name="output_project",
    )(me, *parts, x, w, bias[None], gain[None], shift[None])


def mid_back_kernel(
    group, sc_ref, n2_ref, mid_ref, g_ref, gain_ref, w_ref, mg_ref, ag_ref, gg_ref, gs_ref, bo_ref, *rest
):
    outs, ordered = rest[:group], rest[group]
    n, rs = centre_rows(mid_ref[...])
    n2 = n2_ref[...]
    gg_ref[...] = jnp.sum(n2 * n, axis=0, keepdims=True)
    gs_ref[...] = jnp.sum(n2, axis=0, keepdims=True)
    e = n2 * gain_ref[...]
    part = rs * (
        e - jnp.mean(e, axis=-1, keepdims=True) - n * jnp.mean(e * n, axis=-1, keepdims=True)
    )
    mid_grad = g_ref[...].astype(F32) + part
    mg_ref[...] = mid_grad
    attn = mid_grad.astype(BF16)
    ag_ref[...] = attn
    bo_ref[...] = jnp.sum(attn.astype(F32), axis=0, keepdims=True)
    full = dot(attn, w_ref[...], NT).astype(BF16)
    wide = outs[0].shape[1]
    for s in range(group):
        ordered[s] = full[:, s * wide : (s + 1) * wide]
    for m in range(group):
        outs[m][...] = ordered[sc_ref[0] ^ m]


def mid_back(me, n2_grad, mid, g, gain, w, group):
    rows, width = mid.shape
    wide = width // group
    vec = jax.ShapeDtypeStruct((1, width), F32)
    out = pl.pallas_call(
        functools.partial(mid_back_kernel, group),
        in_specs=[pl.BlockSpec(memory_space=pltpu.SMEM)] + [any_spec()] * 5,
        out_specs=[any_spec()] * (5 + group),
        out_shape=[
            jax.ShapeDtypeStruct((rows, width), F32),
            jax.ShapeDtypeStruct((rows, width), BF16),
            vec,
            vec,
            vec,
        ]
        + [jax.ShapeDtypeStruct((rows, wide), BF16)] * group,
        scratch_shapes=[pltpu.VMEM((group, rows, wide), BF16)],
        compiler_params=params(),
        cost_estimate=pl.CostEstimate(
            flops=2 * rows * width * width,
            bytes_accessed=2 * width * width + 18 * rows * width,
            transcendentals=0,
        ),
        name="mid_back",
    )(me, n2_grad, mid, g, gain[None], w)
    return out[0], out[1], out[2][0], out[3][0], out[4][0], out[5:]


def input_back_kernel(group, sc_ref, *refs):
    parts, refs = refs[:group], refs[group:]
    w_ref, x_ref, mg_ref, gain_ref, flat_ref, tg_ref, gg_ref, gs_ref, gb_ref, ordered, acc = refs
    s = pl.program_id(0)
    cols = parts[0].shape[1]

    @pl.when(s == 0)
    def _():
        gather_parts(sc_ref[0], parts, ordered)
        for k in range(group):
            flat_ref[:, k * cols : (k + 1) * cols] = ordered[k]
            gb_ref[:, k * cols : (k + 1) * cols] = jnp.sum(
                ordered[k].astype(F32), axis=0, keepdims=True
            )
        acc[...] = jnp.zeros_like(acc)

    acc[...] += dot(ordered[s], w_ref[0], NT)

    @pl.when(s == group - 1)
    def _():
        n, rs = centre_rows(x_ref[...].astype(F32))
        n1 = acc[...]
        gg_ref[...] = jnp.sum(n1 * n, axis=0, keepdims=True)
        gs_ref[...] = jnp.sum(n1, axis=0, keepdims=True)
        e = n1 * gain_ref[...]
        part = rs * (
            e - jnp.mean(e, axis=-1, keepdims=True) - n * jnp.mean(e * n, axis=-1, keepdims=True)
        )
        tg_ref[...] = (mg_ref[...] + part).astype(BF16)


def input_back(me, parts, w_parts, x, mid_grad, gain):
    group, width, cols = w_parts.shape
    rows = x.shape[0]
    whole = lambda s, sc: (0, 0)
    vec = jax.ShapeDtypeStruct((1, width), F32)
    out = pl.pallas_call(
        functools.partial(input_back_kernel, group),
        grid_spec=pltpu.PrefetchScalarGridSpec(
            num_scalar_prefetch=1,
            grid=(group,),
            in_specs=[pl.BlockSpec((rows, cols), whole)] * group
            + [
                pl.BlockSpec((1, width, cols), lambda s, sc: (s, 0, 0)),
                pl.BlockSpec((rows, width), whole),
                pl.BlockSpec((rows, width), whole),
                pl.BlockSpec((1, width), whole),
            ],
            out_specs=[
                pl.BlockSpec((rows, group * cols), whole),
                pl.BlockSpec((rows, width), whole),
                pl.BlockSpec((1, width), whole),
                pl.BlockSpec((1, width), whole),
                pl.BlockSpec((1, group * cols), whole),
            ],
            scratch_shapes=[
                pltpu.VMEM((group, rows, cols), BF16),
                pltpu.VMEM((rows, width), F32),
            ],
        ),
        out_shape=[
            jax.ShapeDtypeStruct((rows, group * cols), BF16),
            jax.ShapeDtypeStruct((rows, width), BF16),
            vec,
            vec,
            jax.ShapeDtypeStruct((1, group * cols), F32),
        ],
        compiler_params=params(),
        cost_estimate=pl.CostEstimate(
            flops=2 * rows * width * cols * group,
            bytes_accessed=2 * group * cols * (width + 2 * rows) + 8 * rows * width,
            transcendentals=0,
        ),
        name="input_back",
    )(me, *parts, w_parts, x, mid_grad, gain[None])
    return out[0], out[1], out[2][0], out[3][0], out[4][0]


def partner(axis, mask):
    return [(i, i ^ mask) for i in range(lax.axis_size(axis))]


def exchange(chunks):
    return [chunks[0]] + [
        lax.ppermute(chunks[m], "seq", partner("seq", m)) for m in range(1, len(chunks))
    ]


def bits_of(size):
    return size.bit_length() - 1


def halve(block, axis, bit, dim):
    mine = (lax.axis_index(axis) >> bit) & 1
    keep = lax.dynamic_index_in_dim(block, mine, dim, keepdims=False)
    send = lax.dynamic_index_in_dim(block, 1 - mine, dim, keepdims=False)
    got = lax.ppermute(send, axis, partner(axis, 1 << bit))
    return keep.astype(F32) + got.astype(F32)


def reduce_shares(a, b, order):
    tokens, rows = a.shape
    cols = b.shape[1]
    outer, inner = lax.axis_size("dp") // 2, lax.axis_size("seq")
    share = rows // (2 * outer * inner)
    split = a.reshape(tokens, outer, 2, inner * share)
    core = lax.axis_index("dp") & 1
    send = lax.dynamic_index_in_dim(split, 1 - core, 2, keepdims=False).reshape(tokens, rows // 2)
    keep = lax.dynamic_index_in_dim(split, core, 2, keepdims=False).reshape(tokens, rows // 2)
    got = lax.ppermute(
        dot(send, b, (((0,), (0,)), ((), ()))).astype(BF16), "dp", partner("dp", 1)
    )
    total = (dot(keep, b, (((0,), (0,)), ((), ()))) + got.astype(F32)).astype(BF16)
    return halving(total, order, share, cols)


def halving(total, order, share, cols):
    outer, inner = lax.axis_size("dp") // 2, lax.axis_size("seq")
    axes = [("dp", 1 + k) for k in reversed(range(bits_of(outer)))]
    axes += [("seq", k) for k in reversed(range(bits_of(inner)))]
    total = total.reshape((2,) * len(axes) + (share, cols))
    left = list(axes)
    for pick in order(axes):
        dim = left.index(pick)
        total = halve(total, *pick, dim).astype(F32 if len(left) == 1 else BF16)
        left.remove(pick)
    return total


def dp_first(axes):
    return sorted(axes, key=lambda a: (a[0] != "dp", a[1]))


def seq_first(axes):
    low = [a for a in axes if a == ("seq", 0)]
    rest = sorted((a for a in axes if a != ("seq", 0)), key=lambda a: (a[0] != "dp", a[1]))
    return low + rest


def reduce_vectors(vectors):
    outer, inner = lax.axis_size("dp") // 2, lax.axis_size("seq")
    devices = 2 * outer * inner
    flat = jnp.concatenate([v.reshape(devices, -1) for v in vectors], axis=1)
    axes = [("dp", k) for k in reversed(range(bits_of(2 * outer)))]
    axes += [("seq", k) for k in reversed(range(bits_of(inner)))]
    total = flat.reshape((2,) * len(axes) + flat.shape[1:])
    for axis, bit in axes:
        total = halve(total, axis, bit, 0)
    out, at = [], 0
    for v in vectors:
        wide = v.shape[0] // devices
        out.append(total[at : at + wide])
        at += wide
    return out


def gelu_tanh(inputs):
    return jax.nn.gelu(inputs, approximate=True)


def token_sum(values):
    return jnp.sum(values.astype(F32), axis=0)


def layer(
    cap,
    tokens,
    first_gain,
    first_shift,
    project_weight,
    query_bias,
    value_bias,
    output_weight,
    output_bias,
    second_gain,
    second_shift,
    up_weight,
    up_bias,
    down_weight,
    down_bias,
    doc_offsets,
    active,
    upstream,
):
    group = lax.axis_size("seq")
    rows, shard, width = tokens.shape
    length = active.shape[1]
    wide = width // group
    heads = wide // HEAD_DIM
    me = lax.axis_index("seq")
    me1 = me[None].astype(jnp.int32)
    count = rows * cap

    place = jnp.arange(length, dtype=jnp.int32)
    begun = jnp.where(doc_offsets[:, :, None] <= place, doc_offsets[:, :, None], 0)
    starts = jnp.max(begun, axis=1)
    live = active.reshape(rows, group, shard)
    rank = jnp.cumsum(live.astype(jnp.int32), axis=2) - 1
    slot = jnp.arange(cap, dtype=jnp.int32)[:, None]
    chosen = (rank[:, :, None, :] == slot) & live[:, :, None, :]
    filled = jnp.any(chosen, axis=3)
    place = place.reshape(1, group, 1, shard)
    key_pos = jnp.sum(jnp.where(chosen, place, 0), axis=3)
    key_pos = jnp.where(filled, key_pos, -1).reshape(rows, group * cap)
    begin = jnp.sum(jnp.where(chosen, starts.reshape(rows, group, 1, shard), 0), axis=3)
    begin = jnp.where(filled, begin, FAR).reshape(rows, group * cap)
    tiles = group * cap // TILE
    last_key = jnp.max(key_pos.reshape(rows, tiles, TILE), axis=2)
    first_start = jnp.min(begin.reshape(rows, tiles, TILE), axis=2)
    number = jnp.arange(tiles, dtype=jnp.int32)
    needed = (last_key[:, None, :] >= first_start[:, :, None]) & (number < number[:, None])
    low = jnp.min(jnp.where(needed, number, number[:, None]), axis=2)
    scalars = jnp.concatenate([me1, low.reshape(-1)])
    kp = key_pos[:, :, None]
    spots = key_pos.reshape(rows, tiles, 1, TILE)
    begin = begin.reshape(rows, tiles, 1, TILE)
    pick = lax.dynamic_index_in_dim(chosen, me, 1, keepdims=False).astype(BF16)
    live_here = lax.dynamic_index_in_dim(live, me, 1, keepdims=False)[:, :, None]

    def pack(values):
        return (
            jnp.einsum("rct,rtd->rcd", pick, values, preferred_element_type=F32)
            .astype(BF16)
            .reshape(count, width)
        )

    def unpack(packed, values):
        spread = jnp.einsum(
            "rct,rcd->rtd", pick, packed.reshape(rows, cap, width), preferred_element_type=F32
        ).astype(BF16)
        return jnp.where(live_here, spread, values)

    x = pack(tokens)
    g = pack(upstream)

    w_parts = project_weight.reshape(width, 3, group, wide).transpose(2, 0, 1, 3)
    w_parts = w_parts.reshape(group, width, 3 * wide)
    biases = jnp.stack([query_bias, jnp.zeros_like(query_bias), value_bias])
    bias_parts = biases.reshape(3, group, wide).transpose(1, 0, 2).reshape(group, 1, 3 * wide)

    normed, chunks = qkv_chunks(me1, x, first_gain, first_shift, w_parts, bias_parts)
    head_parts = exchange(chunks)
    ctx_chunks, lse = attend(scalars, head_parts, kp, begin, spots, cap, heads)
    ctx_parts = exchange(ctx_chunks)
    context, middle, normed_two = output_project(
        me1, ctx_parts, x, output_weight, output_bias, second_gain, second_shift
    )

    raised = dot(normed_two, up_weight) + up_bias
    activated, gelu_back = jax.vjp(gelu_tanh, raised)
    hidden = activated.astype(BF16)
    hidden_grad = dot(g, down_weight, NT)
    raised_grad = gelu_back(hidden_grad)[0].astype(BF16)
    normed_two_grad = dot(raised_grad, up_weight, NT)
    middle_grad, attended_grad, grad_second_gain, grad_second_shift, grad_output_bias, grads = (
        mid_back(me1, normed_two_grad, middle, g, second_gain, output_weight, group)
    )
    grad_parts = exchange(grads)
    down_share = reduce_shares(hidden, g, dp_first)
    up_share = reduce_shares(normed_two, raised_grad, seq_first)
    lowered = dot(hidden, down_weight) + down_bias
    result = unpack((middle + lowered).astype(BF16), tokens)
    output_share = reduce_shares(context, attended_grad, dp_first)

    back_chunks = attend_back(
        scalars, head_parts, ctx_chunks, grad_parts, kp, begin, spots, lse, cap, heads
    )
    back_parts = exchange(back_chunks)
    flat_grad, token_grad, grad_first_gain, grad_first_shift, grad_biases = input_back(
        me1, back_parts, w_parts, x, middle_grad, first_gain
    )
    project_share = reduce_shares(normed, flat_grad, seq_first)
    project_share = (
        project_share.reshape(-1, group, 3, wide).transpose(0, 2, 1, 3).reshape(-1, 3 * width)
    )
    grad_biases = grad_biases.reshape(group, 3, wide).transpose(1, 0, 2).reshape(3, width)
    (
        first_gain_share,
        first_shift_share,
        query_share,
        value_share,
        output_bias_share,
        second_gain_share,
        second_shift_share,
        up_bias_share,
        down_bias_share,
    ) = reduce_vectors(
        [
            grad_first_gain,
            grad_first_shift,
            grad_biases[0],
            grad_biases[2],
            grad_output_bias,
            grad_second_gain,
            grad_second_shift,
            token_sum(raised_grad),
            token_sum(g),
        ]
    )
    return (
        result,
        unpack(token_grad, upstream),
        first_gain_share,
        first_shift_share,
        project_share,
        query_share,
        value_share,
        output_share,
        output_bias_share,
        second_gain_share,
        second_shift_share,
        up_share,
        up_bias_share,
        down_share,
        down_bias_share,
    )


def per_device(*args):
    *most, doc_offsets, exit_layers, layer_index, upstream = args
    shard = most[0].shape[1]
    active = exit_layers > layer_index[0]
    return layer(shard, *most, doc_offsets, active, upstream)


def solution(mesh):
    rows = P("dp", "seq", None)
    shares = P(("dp", "seq"))
    wide_shares = P(("dp", "seq"), None)
    in_specs = (rows,) + (P(),) * 13 + (P("dp", None), P("dp", None), P(), rows)
    out_specs = (
        rows,
        rows,
        shares,
        shares,
        wide_shares,
        shares,
        shares,
        wide_shares,
        shares,
        shares,
        shares,
        wide_shares,
        shares,
        wide_shares,
        shares,
    )
    return jax.shard_map(
        per_device, mesh=mesh, in_specs=in_specs, out_specs=out_specs, check_vma=False
    )
```

```python
import functools
import math

import jax
import jax.numpy as jnp
from jax import lax
from jax.experimental import pallas as pl
from jax.experimental.pallas import tpu as pltpu
from jax.sharding import PartitionSpec as P

HEAD_DIM = 64
SCALE = HEAD_DIM**-0.5
TILE = 256
PAIR = 2 * TILE
NEG = -1e30
EPS = 1e-05
VMEM_LIMIT = 60 * 2**20
F32 = jnp.float32
BF16 = jnp.bfloat16

NT = (((1,), (1,)), ((), ()))
NN = (((1,), (0,)), ((), ()))
TN = (((0,), (0,)), ((), ()))


def dot(a, b, dims=NN):
    return lax.dot_general(a, b, dims, preferred_element_type=F32)


def any_spec():
    return pl.BlockSpec(memory_space=pltpu.VMEM)


def params(**kw):
    return pltpu.CompilerParams(vmem_limit_bytes=VMEM_LIMIT, **kw)


def centre_rows(x):
    centred = x - jnp.mean(x, axis=-1, keepdims=True)
    spread = jnp.mean(centred * centred, axis=-1, keepdims=True)
    rs = lax.rsqrt(spread + EPS)
    return centred * rs, rs


def smem():
    return pl.BlockSpec(memory_space=pltpu.SMEM)


def flip(index, mask):
    bit = 1
    out = index
    while bit <= mask:
        if mask & bit:
            out = out + bit * (1 - 2 * ((index // bit) % 2))
        bit *= 2
    return out


class Links:
    def __init__(self, send_sem, recv_sem):
        self.send_sem, self.recv_sem, self.used, self.sent = send_sem, recv_sem, 0, []

    def reserve(self, count):
        first, self.used = self.used, self.used + count
        return first

    def start(self, src, dst, slot, there, device):
        copy = pltpu.make_async_remote_copy(
            src_ref=src,
            dst_ref=dst,
            send_sem=self.send_sem.at[slot],
            recv_sem=self.recv_sem.at[there],
            device_id=device,
            device_id_type=pl.DeviceIdType.MESH,
        )
        copy.start()
        self.sent.append(copy)

    def arrived(self, ref, slot, device):
        pltpu.make_async_remote_copy(
            src_ref=ref,
            dst_ref=ref,
            send_sem=self.send_sem.at[slot],
            recv_sem=self.recv_sem.at[slot],
            device_id=device,
            device_id_type=pl.DeviceIdType.MESH,
        ).wait_recv()

    def drain(self):
        for copy in self.sent:
            copy.wait_send()


def greet(seq_masks, dp_masks):
    me, dp = lax.axis_index("seq"), lax.axis_index("dp")
    barrier = pltpu.get_barrier_semaphore()
    others = [{"seq": flip(me, m)} for m in seq_masks] + [{"dp": flip(dp, m)} for m in dp_masks]
    for device in others:
        pl.semaphore_signal(barrier, inc=1, device_id=device, device_id_type=pl.DeviceIdType.MESH)
    pl.semaphore_wait(barrier, len(others))


class Grid:
    def __init__(self):
        self.dp, self.seq = lax.axis_size("dp"), lax.axis_size("seq")
        self.y = self.dp // 2
        self.x = min(self.y, self.seq)
        self.z = self.seq // self.x
        self.size = {"y": self.y, "x": self.x, "z": self.z}

    def device(self, axis, r):
        me, dp = lax.axis_index("seq"), lax.axis_index("dp")
        if axis == "y":
            return {"dp": flip(dp, 2 * r)}
        return {"seq": flip(me, self.mask(axis, r))}

    def mask(self, axis, r):
        return {"y": 0, "x": r, "z": r * self.x}[axis]


def total_of(first, others, kind):
    total = first.astype(F32)
    for other in others:
        total = total + other.astype(F32)
    return total.astype(kind)


def add_into(total, others):
    for i in range(total.shape[0]):
        for j in range(total.shape[1]):
            total[i, j] = total_of(total[i, j], [other[i, j] for other in others], total.dtype)


class Summed:
    def __init__(self, links, grid, axis, block, got):
        self.links, self.grid, self.axis, self.block, self.got = links, grid, axis, block, got
        self.size = grid.size[axis]
        self.slot = links.reserve(self.size - 1)

    def send(self):
        for r in range(1, self.size):
            slot = self.slot + r - 1
            self.links.start(
                self.block.at[r], self.got.at[r - 1], slot, slot, self.grid.device(self.axis, r)
            )

    def receive(self, store, kind=BF16):
        for r in range(1, self.size):
            self.links.arrived(
                self.got.at[r - 1], self.slot + r - 1, self.grid.device(self.axis, r)
            )
        for i in range(store.shape[0]):
            store[i] = total_of(
                self.block[0, i], [self.got[r - 1, i] for r in range(1, self.size)], kind
            )

    def receive_last(self, store):
        for r in range(1, self.size):
            self.links.arrived(
                self.got.at[r - 1], self.slot + r - 1, self.grid.device(self.axis, r)
            )
        store[...] = total_of(self.block[0], [self.got[r - 1] for r in range(1, self.size)], F32)


class LineSum:
    def __init__(self, links, grid, block, right, left):
        self.links, self.grid, self.block = links, grid, block
        self.got = {1: right, -1: left}
        self.size = grid.z
        self.place = lax.axis_index("seq") // grid.x
        self.slot = {1: links.reserve(self.size), -1: links.reserve(self.size)}

    def next(self, way):
        return {"seq": lax.axis_index("seq") + way * self.grid.x}

    def copy(self, way, goal, src):
        slot = self.slot[way] + goal
        return pltpu.make_async_remote_copy(
            src_ref=src,
            dst_ref=self.got[way].at[goal],
            send_sem=self.links.send_sem.at[slot],
            recv_sem=self.links.recv_sem.at[slot],
            device_id=self.next(way),
            device_id_type=pl.DeviceIdType.MESH,
        )

    def source(self, way, goal, first):
        if first:
            return self.block.at[flip(self.place, goal)]
        return self.got[way].at[goal]

    def hop(self, k):
        for way, at in ((1, k), (-1, self.size - 1 - k)):
            goals = range(at + 1, self.size) if way == 1 else range(at - 1, -1, -1)

            @pl.when(self.place == at)
            def _(way=way, goals=goals):
                for goal in goals:
                    if k:
                        self.arrived(way, goal)
                        got = self.got[way]
                        own = self.block.at[flip(self.place, goal)]
                        for i in range(got.shape[1]):
                            got[goal, i] = total_of(own[i], [got[goal, i]], BF16)
                    self.copy(way, goal, self.source(way, goal, k == 0)).start()

    def arrived(self, way, goal):
        self.copy(way, goal, self.got[way].at[goal]).wait_recv()

    def finish(self, store, cols):
        for at in range(self.size):

            @pl.when(self.place == at)
            def _(at=at):
                ways = [way for way in (1, -1) if (at > 0 if way == 1 else at < self.size - 1)]
                for way in ways:
                    self.arrived(way, at)
                store[:, cols] = total_of(self.block[0], [self.got[w][at] for w in ways], F32)
                for way, k in ((1, at), (-1, self.size - 1 - at)):
                    goals = range(at + 1, self.size) if way == 1 else range(at - 1, -1, -1)
                    for goal in goals:
                        self.copy(way, goal, self.source(way, goal, k == 0)).wait_send()


class SlotSum:
    def __init__(self, links, grid, axis, slots, block, got, inner=False):
        self.links, self.grid, self.axis, self.got = links, grid, axis, got
        self.block = (lambda m, r: block.at[m, :, r]) if inner else (lambda m, r: block.at[m, r])
        self.size = grid.size[axis]
        self.first = links.reserve(slots * (self.size - 1))

    def id(self, m, r):
        return self.first + m * (self.size - 1) + r - 1

    def send(self, m):
        for r in range(1, self.size):
            there = m ^ self.grid.mask(self.axis, r)
            self.links.start(
                self.block(m, r),
                self.got.at[there, r - 1],
                self.id(m, r),
                self.id(there, r),
                self.grid.device(self.axis, r),
            )

    def receive(self, m):
        for r in range(1, self.size):
            self.links.arrived(
                self.got.at[m, r - 1], self.id(m, r), self.grid.device(self.axis, r)
            )
        return total_of(
            self.block(m, 0)[...], [self.got[m, r - 1] for r in range(1, self.size)], F32
        )


def split_weight(weight, group):
    width = weight.shape[0]
    wide = width // group
    if wide % 128 == 0:
        return weight
    return weight.reshape(width, 3, group, wide).transpose(1, 2, 0, 3)


def weight_view(weight, part, source, width, wide):
    if wide % 128 == 0:
        return weight.at[:, pl.ds(pl.multiple_of(part * width + source * wide, 128), wide)]
    return weight.at[part, source]


def first_kernel(wide, *refs):
    x_ref, gain_ref, shift_ref, weight, bias_ref, normed_ref, landed = refs[:7]
    w_s, stage, send_sem, recv_sem, load_sem, own_sem = refs[7:]
    group = lax.axis_size("seq")
    me = lax.axis_index("seq")
    width = x_ref.shape[1]
    links = Links(send_sem, recv_sem)
    first = links.reserve(group)
    order = list(range(group - 1, -1, -1))
    loads = {}
    for m in order:
        source = flip(me, m)
        loads[m] = []
        for part in range(3):
            loads[m].append(
                pltpu.make_async_copy(
                    weight_view(weight, part, source, width, wide),
                    w_s.at[m, part],
                    load_sem.at[3 * m + part],
                )
            )
            loads[m][-1].start()
    n, _ = centre_rows(x_ref[...].astype(F32))
    normed_ref[...] = (n * gain_ref[...] + shift_ref[...]).astype(BF16)
    greet(range(1, group), [])
    own = pltpu.make_async_copy(stage.at[0], landed.at[0], own_sem)
    for m in order:
        for copy in loads[m]:
            copy.wait()
        joined = jnp.concatenate([w_s[m, part] for part in range(3)], axis=1)
        stage[m] = (dot(normed_ref[...], joined) + bias_ref[flip(me, m)]).astype(BF16)
        if m:
            links.start(stage.at[m], landed.at[m], first + m, first + m, {"seq": flip(me, m)})
        else:
            own.start()
    for m in range(1, group):
        links.arrived(landed.at[m], first + m, {"seq": flip(me, m)})
    links.drain()
    own.wait()


def project(x, gain, shift, weight, bias_parts):
    rows, width = x.shape
    group = bias_parts.shape[0]
    wide = width // group
    cols = 3 * wide
    here = any_spec()
    anywhere = pl.BlockSpec(memory_space=pl.ANY)
    return pl.pallas_call(
        functools.partial(first_kernel, wide),
        in_specs=[here, here, here, anywhere, here],
        out_specs=[here, anywhere],
        out_shape=[
            jax.ShapeDtypeStruct((rows, width), BF16),
            jax.ShapeDtypeStruct((group, rows, cols), BF16),
        ],
        scratch_shapes=[
            pltpu.VMEM((group, 3, width, wide), BF16),
            pltpu.VMEM((group, rows, cols), BF16),
            pltpu.SemaphoreType.DMA((group,)),
            pltpu.SemaphoreType.DMA((group,)),
            pltpu.SemaphoreType.DMA((3 * group,)),
            pltpu.SemaphoreType.DMA,
        ],
        compiler_params=params(collective_id=2, has_side_effects=True),
        cost_estimate=pl.CostEstimate(
            flops=2 * rows * width * cols * group,
            bytes_accessed=2 * group * cols * (width + rows),
            transcendentals=0,
        ),
        name="norm_project",
    )(x, gain[None], shift[None], weight, bias_parts)


def only_head(block, head, heads):
    if heads == 1:
        return block
    lane = lax.broadcasted_iota(jnp.int32, block.shape, 1)
    return jnp.where(lane // HEAD_DIM == head, block, jnp.zeros_like(block))


def transposed(block):
    return block.astype(F32).T.astype(BF16)


def causal(size, offset):
    key = lax.broadcasted_iota(jnp.int32, (size, TILE), 0)
    query = lax.broadcasted_iota(jnp.int32, (size, TILE), 1)
    return key <= query + offset


def sweep(tiles, low_of, start, step, finish):
    def before(i, whole_blocks):
        low = low_of(i)
        return lax.fori_loop(
            low, whole_blocks, lambda b, c: step(i, b * PAIR, PAIR, None, c), start(i)
        )

    def even(i, half):
        finish(i, step(i, i * TILE, TILE, 0, before(i, half)))

    def odd(i, half):
        finish(i, step(i, half * PAIR, PAIR, TILE, before(i, half)))

    def both(half, _):
        even(2 * half, half)
        odd(2 * half + 1, half)
        return 0

    lax.fori_loop(0, tiles // 2, both, 0)
    if tiles % 2:
        even(tiles - 1, tiles // 2)


def span(at, size):
    return pl.ds(at if isinstance(at, int) else pl.multiple_of(at, TILE), size)


def load_heads(me, cap, parts, q_s, k_s, v_s):
    wide = v_s.shape[1]
    for m in range(parts.shape[0]):
        here = pl.ds(pl.multiple_of((me ^ m) * cap, 32), cap)
        q_s[here, :] = parts[m, :, :wide] * SCALE
        k_s[here, :wide] = parts[m, :, wide : 2 * wide]
        v_s[here, :] = parts[m, :, 2 * wide :]


def query_rows(queries, docs, heads):
    out = []
    for h in range(heads):
        mine = only_head(queries, h, heads).astype(F32)
        out.append(jnp.concatenate([mine, docs.astype(F32)], axis=1).T.astype(BF16))
    return out


def attend_kernel(group, cap, tiles, heads, sc_ref, *refs):
    parts, q_docs, k_docs, out_ref, lse_ref, q_s, k_s, v_s, vt_s, o_s = refs
    wide = heads * HEAD_DIM
    me = sc_ref[0]
    row = pl.program_id(0)
    load_heads(me, cap, parts, q_s, k_s, v_s)
    k_s[:, wide:] = k_docs[0]
    for t in range(tiles):
        vt_s[:, t * TILE : (t + 1) * TILE] = transposed(v_s[t * TILE : (t + 1) * TILE, :])

    def start(i):
        blank = (
            jnp.full((1, TILE), NEG, F32),
            jnp.zeros((1, TILE), F32),
            jnp.zeros((HEAD_DIM, TILE), F32),
        )
        at = span(i * TILE, TILE)
        return tuple(query_rows(q_s[at, :], q_docs[0, at, :], heads)), (blank,) * heads

    def step(i, at, size, diagonal, carry):
        queries, states = carry
        there = span(at, size)
        keys = k_s[there, :]
        new = []
        for h in range(heads):
            top, total, acc = states[h]
            s = dot(keys, queries[h])
            if diagonal is not None:
                s = jnp.where(causal(size, diagonal), s, NEG)
            top2 = jnp.maximum(top, jnp.max(s, axis=0, keepdims=True))
            p = jnp.exp(s - top2)
            fade = jnp.exp(top - top2)
            total = total * fade + jnp.sum(p, axis=0, keepdims=True)
            vt = vt_s[h * HEAD_DIM : (h + 1) * HEAD_DIM, there]
            acc = acc * fade + dot(vt, p.astype(BF16))
            new.append((top2, total, acc))
        return queries, tuple(new)

    def finish(i, carry):
        pieces = []
        for h in range(heads):
            top, total, acc = carry[1][h]
            pieces.append(acc * (1.0 / total))
            lse_ref[0, i, h : h + 1, :] = top + jnp.log(total)
        o_s[span(i * TILE, TILE), :] = jnp.concatenate(pieces, axis=0).T.astype(BF16)

    sweep(tiles, lambda i: sc_ref[1 + row * tiles + i], start, step, finish)
    for m in range(group):
        out_ref[m] = o_s[pl.ds(pl.multiple_of((me ^ m) * cap, 32), cap), :]


def attend(scalars, parts, q_docs, k_docs, cap, heads):
    group, tokens, cols = parts.shape
    rows = tokens // cap
    length = group * cap
    tiles = length // TILE
    wide = heads * HEAD_DIM
    deep = wide + q_docs.shape[2]
    pair = rows * heads * length * length // 2
    by_row = lambda r, sc: (0, r, 0)
    all_row = lambda r, sc: (r, 0, 0)
    return pl.pallas_call(
        functools.partial(attend_kernel, group, cap, tiles, heads),
        grid_spec=pltpu.PrefetchScalarGridSpec(
            num_scalar_prefetch=1,
            grid=(rows,),
            in_specs=[pl.BlockSpec((group, cap, cols), by_row)]
            + [pl.BlockSpec((1,) + q_docs.shape[1:], all_row)] * 2,
            out_specs=[
                pl.BlockSpec((group, cap, wide), by_row),
                pl.BlockSpec((1, tiles, heads, TILE), lambda r, sc: (r, 0, 0, 0)),
            ],
            scratch_shapes=[
                pltpu.VMEM((length, wide), BF16),
                pltpu.VMEM((length, deep), BF16),
                pltpu.VMEM((length, wide), BF16),
                pltpu.VMEM((wide, length), BF16),
                pltpu.VMEM((length, wide), BF16),
            ],
        ),
        out_shape=[
            jax.ShapeDtypeStruct((group, rows * cap, wide), BF16),
            jax.ShapeDtypeStruct((rows, tiles, heads, TILE), F32),
        ],
        compiler_params=params(),
        cost_estimate=pl.CostEstimate(
            flops=4 * 256 * pair, bytes_accessed=8 * rows * length * wide, transcendentals=pair
        ),
        name="attend",
    )(scalars, parts, q_docs, k_docs)


def attend_back_kernel(group, cap, tiles, heads, sc_ref, *refs):
    parts, ctx, grads, q_docs, k_docs, lse_ref, out_ref = refs[:7]
    refs = refs[7:]
    q_s, k_s, v_s, kt_s, g_s, o_s, dq_s, dk_s, dv_s = refs
    wide = heads * HEAD_DIM
    me = sc_ref[0]
    row = pl.program_id(0)
    load_heads(me, cap, parts, q_s, k_s, v_s)
    k_s[:, wide:] = k_docs[0]
    for m in range(group):
        here = pl.ds(pl.multiple_of((me ^ m) * cap, 32), cap)
        g_s[here, :] = grads[m]
        o_s[here, :] = ctx[m]
    for t in range(tiles):
        kt_s[:, t * TILE : (t + 1) * TILE] = transposed(k_s[t * TILE : (t + 1) * TILE, :wide])
    dk_s[...] = jnp.zeros_like(dk_s)
    dv_s[...] = jnp.zeros_like(dv_s)

    def start(i):
        at = span(i * TILE, TILE)
        queries = q_s[at, :]
        grad = g_s[at, :]
        product = (grad.astype(F32) * o_s[at, :].astype(F32)).T
        delta = tuple(
            jnp.sum(product[h * HEAD_DIM : (h + 1) * HEAD_DIM], axis=0, keepdims=True)
            for h in range(heads)
        )
        split_q = tuple(only_head(queries, h, heads) for h in range(heads))
        split_g = tuple(only_head(grad, h, heads) for h in range(heads))
        turned_q = tuple(query_rows(queries, q_docs[0, at, :], heads))
        turned_g = tuple(transposed(part) for part in split_g)
        fixed = (split_q, split_g, turned_q, turned_g, delta)
        return fixed, tuple(jnp.zeros((HEAD_DIM, TILE), F32) for _ in range(heads))

    def step(i, at, size, diagonal, carry):
        fixed, sums = carry
        split_q, split_g, turned_q, turned_g, delta = fixed
        there = span(at, size)
        keys = k_s[there, :]
        values = v_s[there, :]
        new, ps, dss = [], [], []
        for h in range(heads):
            s = dot(keys, turned_q[h]) - lse_ref[0, i, h : h + 1, :]
            if diagonal is not None:
                s = jnp.where(causal(size, diagonal), s, NEG)
            p = jnp.exp(s)
            dp = dot(values, turned_g[h])
            ds = (p * (dp - delta[h])).astype(BF16)
            ps.append(p.astype(BF16))
            dss.append(ds)
            kt = kt_s[h * HEAD_DIM : (h + 1) * HEAD_DIM, there]
            new.append(sums[h] + dot(kt, ds))
        dv = dot(ps[0], split_g[0])
        dk = dot(dss[0], split_q[0])
        for h in range(1, heads):
            dv = dv + dot(ps[h], split_g[h])
            dk = dk + dot(dss[h], split_q[h])
        dv_s[there, :] += dv
        dk_s[there, :] += dk
        return fixed, tuple(new)

    def finish(i, carry):
        dq_s[span(i * TILE, TILE), :] = (jnp.concatenate(carry[1], axis=0).T * SCALE).astype(BF16)

    sweep(tiles, lambda i: sc_ref[1 + row * tiles + i], start, step, finish)
    for m in range(group):
        here = pl.ds(pl.multiple_of((me ^ m) * cap, 32), cap)
        out_ref[m, :, :wide] = dq_s[here, :]
        out_ref[m, :, wide : 2 * wide] = dk_s[here, :].astype(BF16)
        out_ref[m, :, 2 * wide :] = dv_s[here, :].astype(BF16)


def attend_back(scalars, parts, ctx, grads, q_docs, k_docs, lse, cap, heads):
    group, tokens, cols = parts.shape
    rows = tokens // cap
    length = group * cap
    tiles = length // TILE
    wide = heads * HEAD_DIM
    deep = wide + q_docs.shape[2]
    pair = rows * heads * length * length // 2
    by_row = lambda r, sc: (0, r, 0)
    all_row = lambda r, sc: (r, 0, 0)
    return pl.pallas_call(
        functools.partial(attend_back_kernel, group, cap, tiles, heads),
        grid_spec=pltpu.PrefetchScalarGridSpec(
            num_scalar_prefetch=1,
            grid=(rows,),
            in_specs=[pl.BlockSpec((group, cap, cols), by_row)]
            + [pl.BlockSpec((group, cap, wide), by_row)] * 2
            + [pl.BlockSpec((1,) + q_docs.shape[1:], all_row)] * 2
            + [pl.BlockSpec((1, tiles, heads, TILE), lambda r, sc: (r, 0, 0, 0))],
            out_specs=pl.BlockSpec((group, cap, cols), by_row),
            scratch_shapes=[
                pltpu.VMEM((length, wide), BF16),
                pltpu.VMEM((length, deep), BF16),
                pltpu.VMEM((length, wide), BF16),
                pltpu.VMEM((wide, length), BF16),
            ]
            + [pltpu.VMEM((length, wide), BF16)] * 3
            + [pltpu.VMEM((length, wide), F32)] * 2,
        ),
        out_shape=jax.ShapeDtypeStruct((group, rows * cap, cols), BF16),
        compiler_params=params(),
        cost_estimate=pl.CostEstimate(
            flops=10 * 256 * pair, bytes_accessed=20 * rows * length * wide, transcendentals=pair
        ),
        name="attend_back",
    )(scalars, parts, ctx, grads, q_docs, k_docs, lse)


def norm_back(upper, n, rs, gain):
    e = upper * gain
    return rs * (
        e - jnp.mean(e, axis=-1, keepdims=True) - n * jnp.mean(e * n, axis=-1, keepdims=True)
    )


GELU_A = 0.7978845608028654
GELU_B = 0.044715


VECTORS = 10


def mid_kernel(wide, *refs):
    grid = Grid()
    group, ys, xs, zs = grid.seq, grid.y, grid.x, grid.z
    refs = list(refs)

    def take(n):
        out = refs[:n]
        del refs[:n]
        return out

    ctx_hbm, x_ref, g_ref, ow_hbm, uw_hbm, dw_hbm, ob, gain, shift, ub, db = take(11)
    grads, result_ref, mg_ref, early = take(4)
    down_out, up_out, out_out = take(2 * ys), take(xs + ys), take(zs)
    gots = take(3)
    landed, ctx, ow, uw, dw, hid, rise, mid_s, n2_s, normed, attn, chunk = take(12)
    flat_ring, tall_ring, flat_got, tall_got = take(4)
    send_sem, recv_sem, load_sem, ring_sem, got_sem = take(5)

    me, dp = lax.axis_index("seq"), lax.axis_index("dp")
    core, row = dp % 2, dp // 2
    links = Links(send_sem, recv_sem)
    tokens, width = x_ref.shape
    hidden = hid.shape[1]
    block = min(512, hidden)
    partner_core = {"dp": flip(dp, 1)}
    loads = [
        pltpu.make_async_copy(src, dst, load_sem.at[k])
        for k, (src, dst) in enumerate(
            ((dw_hbm, dw), (ow_hbm, ow), (uw_hbm, uw), (ctx_hbm.at[0], landed.at[0]))
        )
    ]
    for copy in loads:
        copy.start()
    greet(range(1, group), [1])
    first = links.reserve(group)
    for m in range(group - 1, 0, -1):
        links.start(ctx_hbm.at[m], landed.at[m], first + m, first + m, {"seq": flip(me, m)})

    early[...] = jnp.zeros_like(early)
    early[5:6, :] = jnp.sum(g_ref[...].astype(F32), axis=0, keepdims=True)
    loads[0].wait()

    def lanes(f, size):
        return pl.ds(pl.multiple_of(f * size, size), size)

    def before(f, _):
        here = lanes(f, block)
        rise[:, here] = dot(g_ref[...], dw[here, :], NT).astype(BF16)
        return 0

    lax.fori_loop(0, hidden // block, before, 0)
    for copy in loads[1:]:
        copy.wait()
    for m in range(1, group):
        links.arrived(landed.at[m], first + m, {"seq": flip(me, m)})
    for s in range(group):
        chunk[s] = landed[flip(me, s)]
    for s in range(group):
        ctx[:, s * wide : (s + 1) * wide] = chunk[s]
    mid = x_ref[...].astype(F32) + dot(ctx[...], ow[...]) + ob[...]
    mid_s[...] = mid
    n, _ = centre_rows(mid)
    normed[...] = (n * gain[...] + shift[...]).astype(BF16)
    n2_s[...] = jnp.zeros_like(n2_s)

    def through(f, _):
        here = lanes(f, block)
        u = dot(normed[...], uw[:, here]) + ub[:, here]
        square = u * u
        t = jnp.tanh(GELU_A * u * (1.0 + GELU_B * square))
        half = 0.5 * (1.0 + t)
        hid[:, here] = (u * half).astype(BF16)
        slope = half + 0.5 * GELU_A * u * (1.0 - t * t) * (1.0 + 3.0 * GELU_B * square)
        up = (rise[:, here].astype(F32) * slope).astype(BF16)
        rise[:, here] = up
        n2_s[...] += dot(up, uw[:, here], NT)
        return 0

    lax.fori_loop(0, hidden // block, through, 0)
    n, rs = centre_rows(mid_s[...])
    n2 = n2_s[...]
    early[3:4, :] = jnp.sum(n2 * n, axis=0, keepdims=True)
    early[4:5, :] = jnp.sum(n2, axis=0, keepdims=True)
    mid_grad = g_ref[...].astype(F32) + norm_back(n2, n, rs, gain[...])
    mg_ref[...] = mid_grad
    attn[...] = mid_grad.astype(BF16)
    full = dot(attn[...], ow[...], NT).astype(BF16)
    for s in range(group):
        chunk[flip(me, s)] = full[:, s * wide : (s + 1) * wide]
    second = links.reserve(group)
    for m in range(group - 1, 0, -1):
        links.start(chunk.at[m], grads.at[m], second + m, second + m, {"seq": flip(me, m)})
    own = pltpu.make_async_copy(chunk.at[0], grads.at[0], load_sem.at[0])
    own.start()

    rings = {"flat": flat_ring, "tall": tall_ring}
    loaded = {"flat": flat_got, "tall": tall_got}
    busy = {"flat": [None] * flat_ring.shape[0], "tall": [None] * tall_ring.shape[0]}
    places = {"flat": 0, "tall": flat_ring.shape[0]}
    made = {"flat": 0, "tall": 0}
    arriving = {}

    def ordered(ring, spot, total, parts, share, got):
        for s in range(parts):
            rel = flip(me % parts, s)
            piece = total[s * share : (s + 1) * share]
            if got is not None:
                piece = piece + got[rel % xs, rel // xs].astype(F32)
            ring[spot, rel % xs, rel // xs] = piece.astype(BF16)

    def outputs(item, o, z, cols, ring):
        if item == 0:
            half = down_out[0].shape[-1]
            for h in range(2):
                yield ring.at[:, :, :, h * half : (h + 1) * half], down_out[2 * o + h].at[:, z]
        elif item == 1:
            half = up_out[0].shape[-1]
            h, at = cols.start // half, cols.start % half
            here = slice(at, at + cols.stop - cols.start)
            if h:
                yield ring, up_out[xs + o].at[:, :, :, here]
            else:
                for x in range(xs):
                    yield ring.at[x], up_out[x].at[o, :, :, here]
        else:
            for z in range(zs):
                yield ring.at[:, z], out_out[z].at[o]

    def weight_grad(kind, item, a, b):
        share = a.shape[1] // (2 * ys * group)
        parts = min(group, max(256 // share, xs))
        sub = group // parts
        depth = parts // xs
        cols = b.shape[1]
        piece = min(1024, cols)
        ring, got = rings[kind], loaded[kind]
        units = [(o, k, p) for o in reversed(range(ys)) for k in range(sub) for p in range(0, cols, piece)]

        def rows_of(c, o, k):
            at = (flip(row, o) * 2 + flip(core, c)) * group * share
            at = at + flip(me // parts, k) * parts * share
            return transposed(a[:, pl.ds(pl.multiple_of(at, 128), parts * share)])

        def place(o, k, p):
            return (o, slice(None), slice(k * depth, (k + 1) * depth), slice(None), slice(p, p + piece))

        def spot_of():
            spot = made[kind] % ring.shape[0]
            made[kind] += 1
            for wait in busy[kind][spot] or ():
                wait()
            return spot

        for n, (o, k, p) in enumerate(units):
            if p == 0:
                left = rows_of(1, o, k)
            total = dot(left, b[:, p : p + piece])
            spot = spot_of()
            ordered(ring, spot, total, parts, share, None)
            slot = links.reserve(1)
            copy = pltpu.make_async_remote_copy(
                src_ref=ring.at[spot],
                dst_ref=gots[item].at[place(o, k, p)],
                send_sem=send_sem.at[slot],
                recv_sem=recv_sem.at[slot],
                device_id=partner_core,
                device_id_type=pl.DeviceIdType.MESH,
            )
            copy.start()
            busy[kind][spot] = [copy.wait_send]
            arriving[n] = slot

        def fetch(n):
            src = gots[item].at[place(*units[n])]
            links.arrived(src, arriving[n], partner_core)
            copy = pltpu.make_async_copy(src, got.at[n % 2], got_sem.at[2 * item + n % 2])
            copy.start()
            return copy

        coming = fetch(0)
        for n, (o, k, p) in enumerate(units):
            if p == 0:
                left = rows_of(0, o, k)
            total = dot(left, b[:, p : p + piece])
            coming.wait()
            if n + 1 < len(units):
                coming = fetch(n + 1)
            spot = spot_of()
            ordered(ring, spot, total, parts, share, got.at[n % 2])
            busy[kind][spot] = []
            z = slice(k * depth, (k + 1) * depth)
            for h, (src, dst) in enumerate(outputs(item, o, z, slice(p, p + piece), ring.at[spot])):
                sem = ring_sem.at[(places[kind] + spot) * max(2, xs, zs) + h]
                copy = pltpu.make_async_copy(src, dst, sem)
                copy.start()
                busy[kind][spot].append(copy.wait)

    weight_grad("tall", 0, hid, g_ref)
    weight_grad("flat", 1, normed, rise)
    weight_grad("flat", 2, ctx, attn)
    result_ref[...] = (mid_s[...] + (dot(hid[...], dw[...]) + db[...])).astype(BF16)
    early[2:3, :] = jnp.sum(attn[...].astype(F32), axis=0, keepdims=True)
    for k in range(hidden // width):
        part = rise[:, k * width : (k + 1) * width].astype(F32)
        early[6 + k : 7 + k, :] = jnp.sum(part, axis=0, keepdims=True)
    for m in range(1, group):
        links.arrived(grads.at[m], second + m, {"seq": flip(me, m)})
    for spots in busy.values():
        for waits in spots:
            for wait in waits or ():
                wait()
    own.wait()
    links.drain()


def feed_forward(ctx, x, g, ow, ob, gain, shift, uw, ub, dw, db):
    grid = Grid()
    group, ys, xs, zs = grid.seq, grid.y, grid.x, grid.z
    rows, width = x.shape
    wide = width // group
    hidden = uw.shape[1]
    here = any_spec()
    anywhere = pl.BlockSpec(memory_space=pl.ANY)
    shape = jax.ShapeDtypeStruct
    low, high = width // (grid.dp * group), hidden // (grid.dp * group)
    vectors = VECTORS + group
    vectors += -vectors % 8
    sums = [
        shape((ys, xs, zs, high, width), BF16),
        shape((ys, xs, zs, low, hidden), BF16),
        shape((ys, xs, zs, low, width), BF16),
    ]
    parts = lambda share: min(group, max(256 // share, xs))
    ring = lambda share, n: pltpu.VMEM((n, xs, parts(share) // xs, share, width), BF16)
    blocks = ys * (group // parts(high)) + ys * (hidden // width) + ys
    vmem = lambda dims, kind=BF16: pltpu.VMEM(dims, kind)
    return pl.pallas_call(
        functools.partial(mid_kernel, wide),
        in_specs=[anywhere, here, here, anywhere, anywhere, anywhere] + [here] * 5,
        out_specs=[anywhere, here, here, here] + [anywhere] * (3 * ys + xs + zs + 3),
        out_shape=[
            shape((group, rows, wide), BF16),
            shape((rows, width), BF16),
            shape((rows, width), F32),
            shape((vectors, width), F32),
        ]
        + [shape((xs, zs, high, width // 2), BF16)] * (2 * ys)
        + [shape((ys, zs, low, hidden // 2), BF16)] * xs
        + [shape((xs, zs, low, hidden // 2), BF16)] * ys
        + [shape((ys, xs, low, width), BF16)] * zs
        + sums,
        scratch_shapes=[
            vmem((group, rows, wide)),
            vmem((rows, width)),
            vmem((width, width)),
            vmem((width, hidden)),
            vmem((hidden, width)),
            vmem((rows, hidden)),
            vmem((rows, hidden)),
            vmem((rows, width), F32),
            vmem((rows, width), F32),
            vmem((rows, width)),
            vmem((rows, width)),
            vmem((group, rows, wide)),
            ring(low, 4),
            ring(high, 4),
            ring(low, 2),
            ring(high, 2),
            pltpu.SemaphoreType.DMA((2 * group + blocks,)),
            pltpu.SemaphoreType.DMA((2 * group + blocks,)),
            pltpu.SemaphoreType.DMA((4,)),
            pltpu.SemaphoreType.DMA((8 * max(2, xs, zs),)),
            pltpu.SemaphoreType.DMA((6,)),
        ],
        compiler_params=params(collective_id=3, has_side_effects=True),
        cost_estimate=pl.CostEstimate(
            flops=8 * rows * width * width + 12 * rows * width * hidden,
            bytes_accessed=4 * width * width + 8 * width * hidden,
            transcendentals=rows * hidden,
        ),
        name="feed_forward",
    )(ctx, x, g, ow, uw, dw, ob[None], gain[None], shift[None], ub[None], db[None])


def partner(axis, mask):
    return [(i, i ^ mask) for i in range(lax.axis_size(axis))]


def exchange(axis, blocks):
    grid = Grid()
    out = [blocks[0]]
    for r in range(1, grid.size[axis]):
        name, mask = ("dp", 2 * r) if axis == "y" else ("seq", grid.mask(axis, r))
        out.append(lax.ppermute(blocks[r], name, partner(name, mask)))
    return out


def item_counts(ys, xs, zs):
    return (ys - 1) + 5, (xs - 1) + 5, 7, 7, (zs - 1) + 4


def tail_kernel(wide, *refs):
    grid = Grid()
    group, ys, xs, zs = grid.seq, grid.y, grid.x, grid.z
    refs = list(refs)

    def take(n):
        out = refs[:n]
        del refs[:n]
        return out

    back, weight, normed_ref, x_hbm, mg_hbm, gain_ref, early_ref = take(7)
    down_in, down_rest = take(ys), take(ys)
    up_in, up_rest = take(xs), take(ys)
    out_in = take(zs)
    tg_ref, project_ref, down_ref, up_ref, out_ref, vec_ref = take(6)
    landed, w_s, x_s, mg_s, acc, turned, order = take(7)
    send_a, send_b, keep_a, keep_b, pair_a, pair_b = take(6)
    got_a1, got_b1, mid_a, mid_b, got_a2, got_b2, z_a, z_b, got_za, got_zb = take(10)
    items = [take(count) for count in item_counts(ys, xs, zs)]
    vec_s, vec_g = take(2)
    send_sem, recv_sem, load_sem = take(3)

    me, dp = lax.axis_index("seq"), lax.axis_index("dp")
    core, row = dp % 2, dp // 2
    links = Links(send_sem, recv_sem)
    tokens, width = normed_ref.shape
    share = project_ref.shape[1]
    partner_core = {"dp": flip(dp, 1)}
    loads = []

    def load(src, dst):
        copy = pltpu.make_async_copy(src, dst, load_sem.at[len(loads)])
        copy.start()
        loads.append(copy)
        return copy

    greet(range(1, group), [1] + [2 * r for r in range(1, ys)])

    first = links.reserve(group)
    for m in range(1, group):
        links.start(back.at[m], landed.at[m], first + m, first + m, {"seq": flip(me, m)})
    own = load(back.at[0], landed.at[0])
    down_a, up_a, down_b, up_b, out_a = items
    loaded = [
        [load(src, dst) for src, dst in zip(up_in, [up_a[xs - 1]] + up_a[: xs - 1])],
        [load(src, dst) for src, dst in zip(down_in, [down_a[ys - 1]] + down_a[: ys - 1])],
        [load(src, dst) for src, dst in zip(out_in, [out_a[zs - 1]] + out_a[: zs - 1])],
        [load(src, down_b[0].at[o]) for o, src in enumerate(down_rest)],
        [load(src, up_b[0].at[o]) for o, src in enumerate(up_rest)],
    ]

    def load_weight(m):
        source = flip(me, m)
        out = []
        for part in range(3):
            src = weight_view(weight, part, source, width, wide)
            out.append(load(src, w_s.at[m % ahead, part]))
        return out

    ahead = w_s.shape[0]
    own_w = [load_weight(m) for m in range(ahead)]
    own_x = load(x_hbm, x_s)
    own_mg = load(mg_hbm, mg_s)

    def summed(axis, block, got):
        return Summed(links, grid, axis, block, got)

    up_a1 = summed("y", up_a[xs - 1], up_a[xs])
    up_a2 = LineSum(links, grid, *up_a[xs + 1 :])
    down_a1 = summed("x", down_a[ys - 1], down_a[ys])
    down_a2 = LineSum(links, grid, *down_a[ys + 1 :])
    down_b1, down_b2 = summed("y", down_b[0], down_b[1]), summed("x", down_b[2], down_b[3])
    down_b3 = LineSum(links, grid, *down_b[4:])
    up_b1, up_b2 = summed("y", up_b[0], up_b[1]), summed("x", up_b[2], up_b[3])
    up_b3 = LineSum(links, grid, *up_b[4:])
    out_1 = summed("y", out_a[zs - 1], out_a[zs])
    out_2 = summed("x", out_a[zs + 1], out_a[zs + 2])
    lines = (up_a2, down_a2, up_b3, down_b3)
    for copies in loaded[3:]:
        for copy in copies:
            copy.wait()
    down_b1.send()
    up_b1.send()
    for copies, item, count, stage in (
        (loaded[0], up_a, xs, up_a1),
        (loaded[1], down_a, ys, down_a1),
        (loaded[2], out_a, zs, out_1),
    ):
        for copy in copies:
            copy.wait()
        add_into(item[count - 1], item[: count - 1])
        stage.send()

    for k in range(0, width, 256):
        turned[k : k + 256, :] = normed_ref[:, k : k + 256].astype(F32).T
    for c in range(2):
        for o in range(ys):
            for x in range(xs):
                for z in range(zs):
                    there = (flip(row, o) * 2 + flip(core, c)) * group + flip(me, z * xs + x)
                    rows = turned[pl.ds(pl.multiple_of(there * share, share), share), :]
                    order[c, o, x, z] = rows.astype(BF16)
    half = ys * group * share
    acc[...] = jnp.zeros_like(acc)
    vec_s[0] = early_ref[...]
    own.wait()

    pair_first = links.reserve(2 * group)
    a1 = SlotSum(links, grid, "y", group, keep_a, got_a1)
    a2 = SlotSum(links, grid, "x", group, mid_a, got_a2)
    b1 = SlotSum(links, grid, "x", group, keep_b, got_b1, inner=True)
    b2 = SlotSum(links, grid, "y", group, mid_b, got_b2)
    cut = 2 * wide

    def multiply(m):
        if m:
            links.arrived(landed.at[m], first + m, {"seq": flip(me, m)})
        source = flip(me, m)
        for k, (send, keep, pair, cols) in enumerate(
            (
                (send_a, keep_a, pair_a, slice(0, cut)),
                (send_b, keep_b, pair_b, slice(cut, 3 * wide)),
            )
        ):
            grad = landed[m, :, cols]
            left = order[1].reshape(half, tokens)
            send[m] = dot(left, grad).reshape(send.shape[1:]).astype(BF16)
            slot = pair_first + 2 * m + k
            links.start(send.at[m], pair.at[m], slot, slot, partner_core)
            left = order[0].reshape(half, tokens)
            keep[m] = dot(left, grad).reshape(keep.shape[1:]).astype(BF16)
        block = landed[m]
        for copy in own_w[m]:
            copy.wait()
        pieces = [w_s[m % ahead, part] for part in range(3)]
        acc[...] += dot(block, jnp.concatenate(pieces, axis=1), NT)
        if m + ahead < group:
            own_w.append(load_weight(m + ahead))
        sums = jnp.sum(block.astype(F32), axis=0, keepdims=True)
        vec_s[0, pl.ds(VECTORS + source, 1), : 3 * wide] = sums

    def paired(m):
        for k, (keep, pair, nxt) in enumerate(((keep_a, pair_a, a1), (keep_b, pair_b, b1))):
            links.arrived(pair.at[m], pair_first + 2 * m + k, partner_core)
            keep[m] = total_of(keep[m], [pair[m]], BF16)
            nxt.send(m)

    def second(m):
        mid_a[m] = a1.receive(m).astype(BF16)
        a2.send(m)
        mid_b[m] = b1.receive(m).astype(BF16)
        b2.send(m)

    def third(m):
        total = a2.receive(m).astype(BF16)
        for z in range(zs):
            z_a[z, m] = total[z]
        total = b2.receive(m).astype(BF16)
        for z in range(zs):
            z_b[z, m] = total[z]

    def input_grads():
        own_x.wait()
        own_mg.wait()
        n, rs = centre_rows(x_s[...].astype(F32))
        n1 = acc[...]
        tg_ref[...] = (mg_s[...] + norm_back(n1, n, rs, gain_ref[...])).astype(BF16)
        vec_s[0, 0:1, :] = jnp.sum(n1 * n, axis=0, keepdims=True)
        vec_s[0, 1:2, :] = jnp.sum(n1, axis=0, keepdims=True)

    vec_first = links.reserve(1 + (ys - 1) + (xs - 1) + (zs - 1))
    hops = [[partner_core]]
    for axis in ("y", "x", "z"):
        hops.append([grid.device(axis, r) for r in range(1, grid.size[axis])])

    def vec_send(k):
        at = vec_first + sum(len(h) for h in hops[:k])
        for r, device in enumerate(hops[k]):
            links.start(vec_s.at[k], vec_g.at[at + r - vec_first], at + r, at + r, device)

    def vec_receive(k):
        at = vec_first + sum(len(h) for h in hops[:k])
        got = []
        for r, device in enumerate(hops[k]):
            links.arrived(vec_g.at[at + r - vec_first], at + r, device)
            got.append(vec_g[at + r - vec_first])
        total = total_of(vec_s[k], got, F32)
        if k + 1 < len(hops):
            vec_s[k + 1] = total
            vec_send(k + 1)
        else:
            vec_ref[...] = total

    for m in range(group):
        multiply(m)
        if m:
            paired(m - 1)
        if m == group // 2:
            down_b1.receive(down_b[2])
            down_b2.send()
    paired(group - 1)
    down_a1.receive(down_a[ys + 1])
    down_a2.hop(0)
    up_b1.receive(up_b[2])
    up_b2.send()
    up_a1.receive(up_a[xs + 1])
    up_a2.hop(0)
    input_grads()
    vec_send(0)
    out_1.receive(out_a[zs + 1])
    out_2.send()
    down_b2.receive(down_b[4])
    down_b3.hop(0)
    for k in range(1, zs - 1):
        down_a2.hop(k)
        up_a2.hop(k)
    vec_receive(0)
    for m in range(group):
        second(m)
        if m == group // 2:
            for k in range(1, zs - 1):
                down_b3.hop(k)
    vec_receive(1)
    up_b2.receive(up_b[4])
    up_b3.hop(0)
    for m in range(group):
        third(m)
        if m == group // 2:
            for k in range(1, zs - 1):
                up_b3.hop(k)

    z_first = links.reserve(2 * (zs - 1))
    for r in range(1, zs):
        for k, (block, got) in enumerate(((z_a, got_za), (z_b, got_zb))):
            slot = z_first + 2 * (r - 1) + k
            links.start(block.at[r], got.at[r - 1], slot, slot, grid.device("z", r))
    vec_receive(2)
    half = down_ref.shape[1] // 2
    out_2.receive_last(out_ref)
    up_a2.finish(up_ref, slice(0, up_ref.shape[1] // 2))
    down_a2.finish(down_ref, slice(0, half))
    up_b3.finish(up_ref, slice(up_ref.shape[1] // 2, up_ref.shape[1]))
    down_b3.finish(down_ref, slice(half, 2 * half))
    vec_receive(3)
    for r in range(1, zs):
        for k, got in enumerate((got_za, got_zb)):
            links.arrived(got.at[r - 1], z_first + 2 * (r - 1) + k, grid.device("z", r))
    for m in range(group):
        source = flip(me, m)
        for block, got, cols in (
            (z_a, got_za, slice(0, cut)),
            (z_b, got_zb, slice(cut, 3 * wide)),
        ):
            others = [got[r - 1, m ^ grid.mask("z", r)] for r in range(1, zs)]
            project_ref[source, :, cols] = total_of(block[0, m], others, F32)
    links.drain()


def tail(back, normed, weight, x, mid_grad, gain, early, down, up, out):
    grid = Grid()
    group, ys, xs, zs = grid.seq, grid.y, grid.x, grid.z
    rows, width = x.shape
    wide = width // group
    shape = jax.ShapeDtypeStruct
    any_place = pl.BlockSpec(memory_space=pl.ANY)
    here = any_spec()
    share = width // (grid.dp * grid.seq)
    (down, down_rest), (up, up_rest) = down, up
    down_block, up_block, out_block = down[0].shape, up[0].shape, out[0].shape
    vmem = lambda dims, kind=BF16: pltpu.VMEM(tuple(dims), kind)
    a_full, b_full = (share, 2 * wide), (share, wide)
    copies = (
        group
        + 2 * group
        + 2 * group * (ys - 1)
        + 2 * group * (xs - 1)
        + 4 * (xs - 1)
        + 4 * (ys - 1)
        + 8 * zs
        + (1 + (ys - 1) + (xs - 1) + (zs - 1))
        + 2 * (zs - 1)
    )
    hops = 1 + (ys - 1) + (xs - 1) + (zs - 1)
    scratch = (
        [
            vmem((group, rows, 3 * wide)),
            vmem((min(4, group), 3, width, wide)),
            vmem((rows, width)),
            vmem((rows, width), F32),
            vmem((rows, width), F32),
            vmem((width, rows), F32),
            vmem((2, ys, xs, zs, share, rows)),
        ]
        + [vmem((group, ys, xs, zs) + a_full), vmem((group, ys, xs, zs) + b_full)] * 3
        + [
            vmem((group, ys - 1, xs, zs) + a_full),
            vmem((group, xs - 1, ys, zs) + b_full),
            vmem((group, xs, zs) + a_full),
            vmem((group, ys, zs) + b_full),
            vmem((group, xs - 1, zs) + a_full),
            vmem((group, ys - 1, zs) + b_full),
            vmem((zs, group) + a_full),
            vmem((zs, group) + b_full),
            vmem((zs - 1, group) + a_full),
            vmem((zs - 1, group) + b_full),
        ]
        + [vmem(down_block)] * ys
        + [vmem((xs - 1,) + down_block[1:])]
        + [vmem(down_block[1:])] * 3
        + [vmem(up_block)] * xs
        + [vmem((ys - 1,) + up_block[1:])]
        + [vmem(up_block[1:])] * 3
        + [
            vmem((ys,) + down_block),
            vmem((ys - 1,) + down_block),
            vmem(down_block),
            vmem((xs - 1,) + down_block[1:]),
        ]
        + [vmem(down_block[1:])] * 3
        + [
            vmem((ys,) + up_rest[0].shape),
            vmem((ys - 1,) + up_rest[0].shape),
            vmem(up_rest[0].shape),
            vmem((xs - 1,) + up_block[1:]),
        ]
        + [vmem(up_block[1:])] * 3
        + [vmem(out_block)] * zs
        + [
            vmem((ys - 1,) + out_block[1:]),
            vmem(out_block[1:]),
            vmem((xs - 1,) + out_block[2:]),
        ]
        + [
            vmem((4,) + early.shape, F32),
            vmem((hops,) + early.shape, F32),
            pltpu.SemaphoreType.DMA((copies,)),
            pltpu.SemaphoreType.DMA((copies,)),
            pltpu.SemaphoreType.DMA((3 + 3 * ys + xs + zs + 3 * group,)),
        ]
    )
    return pl.pallas_call(
        functools.partial(tail_kernel, wide),
        in_specs=[any_place, any_place, here, any_place, any_place, here, here]
        + [any_place] * (3 * ys + xs + zs),
        out_specs=[here] * 6,
        out_shape=[
            shape((rows, width), BF16),
            shape((group, share, 3 * wide), F32),
            shape((down_block[2], width), F32),
            shape((up_block[2], 2 * up_block[3]), F32),
            shape(out_block[2:], F32),
            shape(early.shape, F32),
        ],
        scratch_shapes=scratch,
        compiler_params=params(collective_id=1, has_side_effects=True),
        cost_estimate=pl.CostEstimate(
            flops=12 * rows * width * width, bytes_accessed=2**25, transcendentals=0
        ),
        name="tail",
    )(back, weight, normed, x, mid_grad, gain[None], early, *down, *down_rest, *up, *up_rest, *out)


def layer(
    cap,
    tokens,
    first_gain,
    first_shift,
    project_weight,
    query_bias,
    value_bias,
    output_weight,
    output_bias,
    second_gain,
    second_shift,
    up_weight,
    up_bias,
    down_weight,
    down_bias,
    doc_offsets,
    active,
    upstream,
):
    group = lax.axis_size("seq")
    outer = lax.axis_size("dp") // 2
    rows, shard, width = tokens.shape
    length = active.shape[1]
    docs = doc_offsets.shape[1]
    wide = width // group
    heads = wide // HEAD_DIM
    me = lax.axis_index("seq").astype(jnp.int32)
    dp = lax.axis_index("dp").astype(jnp.int32)
    count = rows * cap

    place = jnp.arange(length, dtype=jnp.int32)
    ids = jnp.sum((doc_offsets[:, 1:, None] <= place).astype(jnp.int32), axis=1)
    live = active.reshape(rows, group, shard)
    rank = jnp.cumsum(live.astype(jnp.int32), axis=2) - 1
    slot = jnp.arange(cap, dtype=jnp.int32)[:, None]
    chosen = (rank[:, :, None, :] == slot) & live[:, :, None, :]
    ids = jnp.sum(
        jnp.where(chosen, ids.reshape(rows, group, 1, shard) + 1, 0), axis=3
    ).reshape(rows, group * cap)
    padded = -docs % 128
    unit = ids[:, :, None] == 1 + jnp.arange(docs + padded, dtype=jnp.int32)
    q_docs = unit.astype(BF16)
    k_docs = jnp.where(unit | (jnp.arange(docs + padded) >= docs), 0.0, NEG).astype(BF16)
    tiles = group * cap // TILE
    last = jnp.max(ids.reshape(rows, tiles, TILE), axis=2)
    first = jnp.min(jnp.where(ids == 0, docs + 1, ids).reshape(rows, tiles, TILE), axis=2)
    number = jnp.arange(tiles, dtype=jnp.int32)
    needed = (last[:, None, :] >= first[:, :, None]) & (number < number[:, None])
    low = jnp.min(jnp.where(needed, number, number[:, None]), axis=2) // 2
    scalars = jnp.concatenate([me[None], low.reshape(-1)])
    pick = lax.dynamic_index_in_dim(chosen, me, 1, keepdims=False).astype(BF16)
    live_here = lax.dynamic_index_in_dim(live, me, 1, keepdims=False)[:, :, None]

    def pack(values):
        return (
            jnp.einsum("rct,rtd->rcd", pick, values, preferred_element_type=F32)
            .astype(BF16)
            .reshape(count, width)
        )

    def unpack(packed, values):
        spread = jnp.einsum(
            "rct,rcd->rtd", pick, packed.reshape(rows, cap, width), preferred_element_type=F32
        ).astype(BF16)
        return jnp.where(live_here, spread, values)

    x = pack(tokens)
    g = pack(upstream)

    biases = jnp.stack([query_bias, jnp.zeros_like(query_bias), value_bias])
    bias_parts = biases.reshape(3, group, wide).transpose(1, 0, 2).reshape(group, 1, 3 * wide)

    weight = split_weight(project_weight, group)
    normed, head_parts = project(x, first_gain, first_shift, weight, bias_parts)
    ctx_chunks, lse = attend(scalars, head_parts, q_docs, k_docs, cap, heads)
    grad_parts, result, middle_grad, early, *halves = feed_forward(
        ctx_chunks,
        x,
        g,
        output_weight,
        output_bias,
        second_gain,
        second_shift,
        up_weight,
        up_bias,
        down_weight,
        down_bias,
    )
    ys, xs = Grid().y, Grid().x
    down, up, out = halves[: 2 * ys], halves[2 * ys : 3 * ys + xs], halves[3 * ys + xs : -3]
    down_parts = exchange("y", down[0::2]), down[1::2]
    up_parts = exchange("x", up[:xs]), up[xs:]
    out_parts = exchange("z", out)
    back = attend_back(
        scalars, head_parts, ctx_chunks, grad_parts, q_docs, k_docs, lse, cap, heads
    )
    token_grad, project_share, down_share, up_share, out_share, sums = tail(
        back, normed, weight, x, middle_grad, first_gain, early, down_parts, up_parts, out_parts
    )
    project_share = project_share.reshape(group, -1, 3, wide).transpose(1, 2, 0, 3)
    devices = 2 * outer * group
    index = dp * group + me
    mine = lambda v: lax.dynamic_index_in_dim(v, index, 1, keepdims=False)
    singles = mine(sums[:6].reshape(6, devices, -1))
    up_bias_share = mine(sums[6:VECTORS].reshape(1, devices, -1))[0]
    by_part = sums[VECTORS : VECTORS + group, : 3 * wide].reshape(group, 3, wide).transpose(1, 0, 2)
    by_part = mine(by_part.reshape(3, devices, -1))
    return (
        unpack(result, tokens),
        unpack(token_grad, upstream),
        singles[0],
        singles[1],
        project_share.reshape(-1, 3 * width),
        by_part[0],
        by_part[2],
        out_share,
        singles[2],
        singles[3],
        singles[4],
        up_share,
        up_bias_share,
        down_share,
        singles[5],
    )


def per_device(*args):
    *most, doc_offsets, exit_layers, layer_index, upstream = args
    shard = most[0].shape[1]
    active = exit_layers > layer_index[0]
    return layer(shard, *most, doc_offsets, active, upstream)


def solution(mesh):
    rows = P("dp", "seq", None)
    shares = P(("dp", "seq"))
    wide_shares = P(("dp", "seq"), None)
    in_specs = (rows,) + (P(),) * 13 + (P("dp", None), P("dp", None), P(), rows)
    out_specs = (
        rows,
        rows,
        shares,
        shares,
        wide_shares,
        shares,
        shares,
        wide_shares,
        shares,
        shares,
        shares,
        wide_shares,
        shares,
        wide_shares,
        shares,
    )
    return jax.shard_map(
        per_device, mesh=mesh, in_specs=in_specs, out_specs=out_specs, check_vma=False
    )
```

```python
import functools
import math

import jax
import jax.numpy as jnp
from jax import lax
from jax.experimental import pallas as pl
from jax.experimental.pallas import tpu as pltpu
from jax.sharding import PartitionSpec as P

HEAD_DIM = 64
SCALE = HEAD_DIM**-0.5
TILE = 256
PAIR = 2 * TILE
NEG = -1e30
EPS = 1e-05
VMEM_LIMIT = 60 * 2**20
F32 = jnp.float32
BF16 = jnp.bfloat16

NT = (((1,), (1,)), ((), ()))
NN = (((1,), (0,)), ((), ()))
TN = (((0,), (0,)), ((), ()))


def dot(a, b, dims=NN):
    return lax.dot_general(a, b, dims, preferred_element_type=F32)


def any_spec():
    return pl.BlockSpec(memory_space=pltpu.VMEM)


def params(**kw):
    return pltpu.CompilerParams(vmem_limit_bytes=VMEM_LIMIT, **kw)


def centre_rows(x):
    centred = x - jnp.mean(x, axis=-1, keepdims=True)
    spread = jnp.mean(centred * centred, axis=-1, keepdims=True)
    rs = lax.rsqrt(spread + EPS)
    return centred * rs, rs


def smem():
    return pl.BlockSpec(memory_space=pltpu.SMEM)


def flip(index, mask, size=64):
    bit = 1
    out = index
    while bit < size:
        if not isinstance(mask, int):
            ours, theirs = (index // bit) % 2, (mask // bit) % 2
            out = out + bit * (theirs - 2 * ours * theirs)
        elif mask & bit:
            out = out + bit * (1 - 2 * ((index // bit) % 2))
        bit *= 2
    return out


def loop(first, last, body):
    def turn(i, _):
        body(i)
        return 0

    lax.fori_loop(first, last, turn, 0)


class Links:
    def __init__(self, send_sem, recv_sem):
        self.send_sem, self.recv_sem, self.used, self.sent = send_sem, recv_sem, 0, []

    def reserve(self, count):
        first, self.used = self.used, self.used + count
        return first

    def start(self, src, dst, slot, there, device, later=True):
        copy = pltpu.make_async_remote_copy(
            src_ref=src,
            dst_ref=dst,
            send_sem=self.send_sem.at[slot],
            recv_sem=self.recv_sem.at[there],
            device_id=device,
            device_id_type=pl.DeviceIdType.MESH,
        )
        copy.start()
        if later:
            self.sent.append(copy)

    def left(self, src, slot, device):
        pltpu.make_async_remote_copy(
            src_ref=src,
            dst_ref=src,
            send_sem=self.send_sem.at[slot],
            recv_sem=self.recv_sem.at[slot],
            device_id=device,
            device_id_type=pl.DeviceIdType.MESH,
        ).wait_send()

    def arrived(self, ref, slot, device):
        pltpu.make_async_remote_copy(
            src_ref=ref,
            dst_ref=ref,
            send_sem=self.send_sem.at[slot],
            recv_sem=self.recv_sem.at[slot],
            device_id=device,
            device_id_type=pl.DeviceIdType.MESH,
        ).wait_recv()

    def drain(self):
        for copy in self.sent:
            copy.wait_send()


def greet(seq_masks, dp_masks):
    me, dp = lax.axis_index("seq"), lax.axis_index("dp")
    barrier = pltpu.get_barrier_semaphore()
    others = [{"seq": flip(me, m)} for m in seq_masks] + [{"dp": flip(dp, m)} for m in dp_masks]
    for device in others:
        pl.semaphore_signal(barrier, inc=1, device_id=device, device_id_type=pl.DeviceIdType.MESH)
    pl.semaphore_wait(barrier, len(others))


class Grid:
    def __init__(self):
        self.dp, self.seq = lax.axis_size("dp"), lax.axis_size("seq")
        self.y = self.dp // 2
        self.x = min(self.y, self.seq)
        self.z = self.seq // self.x
        self.size = {"y": self.y, "x": self.x, "z": self.z}

    def device(self, axis, r):
        me, dp = lax.axis_index("seq"), lax.axis_index("dp")
        if axis == "y":
            return {"dp": flip(dp, 2 * r)}
        return {"seq": flip(me, self.mask(axis, r))}

    def mask(self, axis, r):
        return {"y": 0, "x": r, "z": r * self.x}[axis]


def total_of(first, others, kind):
    total = first.astype(F32)
    for other in others:
        total = total + other.astype(F32)
    return total.astype(kind)


def add_into(total, others):
    inner = total.shape[1]

    def one(k):
        i, j = k // inner, k % inner
        total[i, j] = total_of(total[i, j], [other[i, j] for other in others], total.dtype)

    loop(0, total.shape[0] * inner, one)


class Summed:
    def __init__(self, links, grid, axis, block, got):
        self.links, self.grid, self.axis, self.block, self.got = links, grid, axis, block, got
        self.size = grid.size[axis]
        self.slot = links.reserve(self.size - 1)

    def send(self):
        for r in range(1, self.size):
            slot = self.slot + r - 1
            self.links.start(
                self.block.at[r], self.got.at[r - 1], slot, slot, self.grid.device(self.axis, r)
            )

    def receive(self, store, kind=BF16):
        for r in range(1, self.size):
            self.links.arrived(
                self.got.at[r - 1], self.slot + r - 1, self.grid.device(self.axis, r)
            )
        inner = store.shape[1]

        def one(k):
            i, j = k // inner, k % inner
            others = [self.got[r - 1, i, j] for r in range(1, self.size)]
            store[i, j] = total_of(self.block[0, i, j], others, kind)

        if len(store.shape) == 4:
            loop(0, store.shape[0] * inner, one)
        else:
            store[...] = total_of(self.block[0], [self.got[r - 1] for r in range(1, self.size)], kind)

    def receive_last(self, store):
        for r in range(1, self.size):
            self.links.arrived(
                self.got.at[r - 1], self.slot + r - 1, self.grid.device(self.axis, r)
            )
        store[...] = total_of(self.block[0], [self.got[r - 1] for r in range(1, self.size)], F32)


class LineSum:
    def __init__(self, links, grid, block, right, left):
        self.links, self.grid, self.block = links, grid, block
        self.got = {1: right, -1: left}
        self.size = grid.z
        self.place = lax.axis_index("seq") // grid.x
        self.slot = {1: links.reserve(self.size), -1: links.reserve(self.size)}

    def next(self, way):
        return {"seq": lax.axis_index("seq") + way * self.grid.x}

    def copy(self, way, goal, src):
        slot = self.slot[way] + goal
        return pltpu.make_async_remote_copy(
            src_ref=src,
            dst_ref=self.got[way].at[goal],
            send_sem=self.links.send_sem.at[slot],
            recv_sem=self.links.recv_sem.at[slot],
            device_id=self.next(way),
            device_id_type=pl.DeviceIdType.MESH,
        )

    def source(self, way, goal, first):
        if first:
            return self.block.at[flip(self.place, goal)]
        return self.got[way].at[goal]

    def hop(self, k):
        for way, at in ((1, k), (-1, self.size - 1 - k)):
            goals = range(self.size - 1, at, -1) if way == 1 else range(at)

            @pl.when(self.place == at)
            def _(way=way, goals=goals):
                for goal in goals:
                    if k:
                        self.arrived(way, goal)
                        got = self.got[way]
                        own = self.block.at[flip(self.place, goal)]
                        for i in range(got.shape[1]):
                            got[goal, i] = total_of(own[i], [got[goal, i]], BF16)
                    self.copy(way, goal, self.source(way, goal, k == 0)).start()

    def arrived(self, way, goal):
        self.copy(way, goal, self.got[way].at[goal]).wait_recv()

    def finish(self, store, cols):
        store[:, cols] = self.block[0].astype(F32)
        for way, limit in ((1, self.place > 0), (-1, self.place < self.size - 1)):

            @pl.when(limit)
            def _(way=way):
                self.arrived(way, self.place)
                store[:, cols] = store[:, cols] + self.got[way][self.place].astype(F32)

        for way in (1, -1):
            for goal in range(self.size):

                @pl.when(self.place < goal if way == 1 else self.place > goal)
                def _(way=way, goal=goal):
                    self.copy(way, goal, self.got[way].at[goal]).wait_send()


class SlotSum:
    def __init__(self, links, grid, axis, slots, block, got, inner=False):
        self.links, self.grid, self.axis, self.got = links, grid, axis, got
        self.block = (lambda m, r: block.at[m, :, r]) if inner else (lambda m, r: block.at[m, r])
        self.size, self.slots = grid.size[axis], slots
        self.first = links.reserve(slots * (self.size - 1))

    def id(self, m, r):
        return self.first + m * (self.size - 1) + r - 1

    def send(self, m):
        for r in range(1, self.size):
            there = flip(m, self.grid.mask(self.axis, r), self.slots)
            self.links.start(
                self.block(m, r),
                self.got.at[there, r - 1],
                self.id(m, r),
                self.id(there, r),
                self.grid.device(self.axis, r),
                later=False,
            )

    def receive(self, m):
        for r in range(1, self.size):
            self.links.arrived(
                self.got.at[m, r - 1], self.id(m, r), self.grid.device(self.axis, r)
            )
        return total_of(
            self.block(m, 0)[...], [self.got[m, r - 1] for r in range(1, self.size)], F32
        )

    def drain(self, m):
        for r in range(1, self.size):
            self.links.left(self.block(m, r), self.id(m, r), self.grid.device(self.axis, r))


def split_weight(weight, group):
    width = weight.shape[0]
    wide = width // group
    if wide % 128 == 0:
        return weight
    return weight.reshape(width, 3, group, wide).transpose(1, 2, 0, 3)


def weight_view(weight, part, source, width, wide):
    if wide % 128 == 0:
        return weight.at[:, pl.ds(pl.multiple_of(part * width + source * wide, 128), wide)]
    return weight.at[part, source]


def first_kernel(wide, *refs):
    x_ref, gain_ref, shift_ref, weight, bias_ref, normed_ref, landed = refs[:7]
    w_s, stage, send_sem, recv_sem, load_sem, own_sem = refs[7:]
    group = lax.axis_size("seq")
    me = lax.axis_index("seq")
    width = x_ref.shape[1]
    links = Links(send_sem, recv_sem)
    first = links.reserve(group)
    order = list(range(group - 1, -1, -1))
    loads = {}
    for m in order:
        source = flip(me, m)
        loads[m] = []
        for part in range(3):
            loads[m].append(
                pltpu.make_async_copy(
                    weight_view(weight, part, source, width, wide),
                    w_s.at[m, part],
                    load_sem.at[3 * m + part],
                )
            )
            loads[m][-1].start()
    n, _ = centre_rows(x_ref[...].astype(F32))
    normed_ref[...] = (n * gain_ref[...] + shift_ref[...]).astype(BF16)
    greet(range(1, group), [])
    own = pltpu.make_async_copy(stage.at[0], landed.at[0], own_sem)
    for m in order:
        for copy in loads[m]:
            copy.wait()
        joined = jnp.concatenate([w_s[m, part] for part in range(3)], axis=1)
        stage[m] = (dot(normed_ref[...], joined) + bias_ref[flip(me, m)]).astype(BF16)
        if m:
            links.start(stage.at[m], landed.at[m], first + m, first + m, {"seq": flip(me, m)})
        else:
            own.start()
    for m in range(1, group):
        links.arrived(landed.at[m], first + m, {"seq": flip(me, m)})
    links.drain()
    own.wait()


def project(branch, x, gain, shift, weight, bias_parts):
    rows, width = x.shape
    group = bias_parts.shape[0]
    wide = width // group
    cols = 3 * wide
    here = any_spec()
    anywhere = pl.BlockSpec(memory_space=pl.ANY)
    return pl.pallas_call(
        functools.partial(first_kernel, wide),
        in_specs=[here, here, here, anywhere, here],
        out_specs=[here, anywhere],
        out_shape=[
            jax.ShapeDtypeStruct((rows, width), BF16),
            jax.ShapeDtypeStruct((group, rows, cols), BF16),
        ],
        scratch_shapes=[
            pltpu.VMEM((group, 3, width, wide), BF16),
            pltpu.VMEM((group, rows, cols), BF16),
            pltpu.SemaphoreType.DMA((group,)),
            pltpu.SemaphoreType.DMA((group,)),
            pltpu.SemaphoreType.DMA((3 * group,)),
            pltpu.SemaphoreType.DMA,
        ],
        compiler_params=params(collective_id=3 * branch + 1, has_side_effects=True),
        cost_estimate=pl.CostEstimate(
            flops=2 * rows * width * cols * group,
            bytes_accessed=2 * group * cols * (width + rows),
            transcendentals=0,
        ),
        name="norm_project",
    )(x, gain[None], shift[None], weight, bias_parts)


def only_head(block, head, heads):
    if heads == 1:
        return block
    lane = lax.broadcasted_iota(jnp.int32, block.shape, 1)
    return jnp.where(lane // HEAD_DIM == head, block, jnp.zeros_like(block))


def transposed(block):
    return block.astype(F32).T.astype(BF16)


def causal(size, offset):
    key = lax.broadcasted_iota(jnp.int32, (size, TILE), 0)
    query = lax.broadcasted_iota(jnp.int32, (size, TILE), 1)
    return key <= query + offset


def sweep(tiles, low_of, start, step, finish):
    def before(i, whole_blocks):
        low = low_of(i)
        return lax.fori_loop(
            low, whole_blocks, lambda b, c: step(i, b * PAIR, PAIR, None, c), start(i)
        )

    def even(i, half):
        finish(i, step(i, i * TILE, TILE, 0, before(i, half)))

    def odd(i, half):
        finish(i, step(i, half * PAIR, PAIR, TILE, before(i, half)))

    def both(half, _):
        even(2 * half, half)
        odd(2 * half + 1, half)
        return 0

    lax.fori_loop(0, tiles // 2, both, 0)
    if tiles % 2:
        even(tiles - 1, tiles // 2)


def span(at, size):
    return pl.ds(at if isinstance(at, int) else pl.multiple_of(at, TILE), size)


def blank_rest(used, *arrays):
    if used < arrays[0].shape[0]:
        for array in arrays:
            array[used:, :] = jnp.zeros((array.shape[0] - used, array.shape[1]), array.dtype)


def load_heads(me, cap, parts, q_s, k_s, v_s):
    wide = v_s.shape[1]
    blank_rest(parts.shape[0] * cap, q_s, k_s, v_s)
    for m in range(parts.shape[0]):
        here = pl.ds(pl.multiple_of((me ^ m) * cap, math.gcd(cap, 128)), cap)
        q_s[here, :] = parts[m, :, :wide] * SCALE
        k_s[here, :wide] = parts[m, :, wide : 2 * wide]
        v_s[here, :] = parts[m, :, 2 * wide :]


def query_rows(queries, docs, heads):
    out = []
    for h in range(heads):
        mine = only_head(queries, h, heads).astype(F32)
        out.append(jnp.concatenate([mine, docs.astype(F32)], axis=1).T.astype(BF16))
    return out


def attend_kernel(group, cap, tiles, heads, sc_ref, *refs):
    parts, q_docs, k_docs, out_ref, lse_ref, q_s, k_s, v_s, vt_s, o_s = refs
    wide = heads * HEAD_DIM
    me = sc_ref[0]
    row = pl.program_id(0)
    load_heads(me, cap, parts, q_s, k_s, v_s)
    k_s[:, wide:] = k_docs[0]
    for t in range(tiles):
        vt_s[:, t * TILE : (t + 1) * TILE] = transposed(v_s[t * TILE : (t + 1) * TILE, :])

    def start(i):
        blank = (
            jnp.full((1, TILE), NEG, F32),
            jnp.zeros((1, TILE), F32),
            jnp.zeros((HEAD_DIM, TILE), F32),
        )
        at = span(i * TILE, TILE)
        return tuple(query_rows(q_s[at, :], q_docs[0, at, :], heads)), (blank,) * heads

    def step(i, at, size, diagonal, carry):
        queries, states = carry
        there = span(at, size)
        keys = k_s[there, :]
        new = []
        for h in range(heads):
            top, total, acc = states[h]
            s = dot(keys, queries[h])
            if diagonal is not None:
                s = jnp.where(causal(size, diagonal), s, NEG)
            top2 = jnp.maximum(top, jnp.max(s, axis=0, keepdims=True))
            p = jnp.exp(s - top2)
            fade = jnp.exp(top - top2)
            total = total * fade + jnp.sum(p, axis=0, keepdims=True)
            vt = vt_s[h * HEAD_DIM : (h + 1) * HEAD_DIM, there]
            acc = acc * fade + dot(vt, p.astype(BF16))
            new.append((top2, total, acc))
        return queries, tuple(new)

    def finish(i, carry):
        pieces = []
        for h in range(heads):
            top, total, acc = carry[1][h]
            pieces.append(acc * (1.0 / total))
            lse_ref[0, i, h : h + 1, :] = top + jnp.log(total)
        o_s[span(i * TILE, TILE), :] = jnp.concatenate(pieces, axis=0).T.astype(BF16)

    sweep(tiles, lambda i: sc_ref[1 + row * tiles + i], start, step, finish)
    for m in range(group):
        out_ref[m] = o_s[pl.ds(pl.multiple_of((me ^ m) * cap, math.gcd(cap, 128)), cap), :]


def attend(scalars, parts, q_docs, k_docs, cap, heads):
    group, tokens, cols = parts.shape
    rows = tokens // cap
    tiles = pl.cdiv(group * cap, TILE)
    length = tiles * TILE
    wide = heads * HEAD_DIM
    deep = wide + q_docs.shape[2]
    pair = rows * heads * length * length // 2
    by_row = lambda r, sc: (0, r, 0)
    all_row = lambda r, sc: (r, 0, 0)
    return pl.pallas_call(
        functools.partial(attend_kernel, group, cap, tiles, heads),
        grid_spec=pltpu.PrefetchScalarGridSpec(
            num_scalar_prefetch=1,
            grid=(rows,),
            in_specs=[pl.BlockSpec((group, cap, cols), by_row)]
            + [pl.BlockSpec((1,) + q_docs.shape[1:], all_row)] * 2,
            out_specs=[
                pl.BlockSpec((group, cap, wide), by_row),
                pl.BlockSpec((1, tiles, heads, TILE), lambda r, sc: (r, 0, 0, 0)),
            ],
            scratch_shapes=[
                pltpu.VMEM((length, wide), BF16),
                pltpu.VMEM((length, deep), BF16),
                pltpu.VMEM((length, wide), BF16),
                pltpu.VMEM((wide, length), BF16),
                pltpu.VMEM((length, wide), BF16),
            ],
        ),
        out_shape=[
            jax.ShapeDtypeStruct((group, rows * cap, wide), BF16),
            jax.ShapeDtypeStruct((rows, tiles, heads, TILE), F32),
        ],
        compiler_params=params(),
        cost_estimate=pl.CostEstimate(
            flops=4 * 256 * pair, bytes_accessed=8 * rows * length * wide, transcendentals=pair
        ),
        name="attend",
    )(scalars, parts, q_docs, k_docs)


def attend_back_kernel(group, cap, tiles, heads, sc_ref, *refs):
    parts, ctx, grads, q_docs, k_docs, lse_ref, out_ref = refs[:7]
    refs = refs[7:]
    q_s, k_s, v_s, kt_s, g_s, o_s, dq_s, dk_s, dv_s = refs
    wide = heads * HEAD_DIM
    me = sc_ref[0]
    row = pl.program_id(0)
    load_heads(me, cap, parts, q_s, k_s, v_s)
    k_s[:, wide:] = k_docs[0]
    blank_rest(group * cap, g_s, o_s)
    for m in range(group):
        here = pl.ds(pl.multiple_of((me ^ m) * cap, math.gcd(cap, 128)), cap)
        g_s[here, :] = grads[m]
        o_s[here, :] = ctx[m]
    for t in range(tiles):
        kt_s[:, t * TILE : (t + 1) * TILE] = transposed(k_s[t * TILE : (t + 1) * TILE, :wide])
    dk_s[...] = jnp.zeros_like(dk_s)
    dv_s[...] = jnp.zeros_like(dv_s)

    def start(i):
        at = span(i * TILE, TILE)
        queries = q_s[at, :]
        grad = g_s[at, :]
        product = (grad.astype(F32) * o_s[at, :].astype(F32)).T
        delta = tuple(
            jnp.sum(product[h * HEAD_DIM : (h + 1) * HEAD_DIM], axis=0, keepdims=True)
            for h in range(heads)
        )
        split_q = tuple(only_head(queries, h, heads) for h in range(heads))
        split_g = tuple(only_head(grad, h, heads) for h in range(heads))
        turned_q = tuple(query_rows(queries, q_docs[0, at, :], heads))
        turned_g = tuple(transposed(part) for part in split_g)
        fixed = (split_q, split_g, turned_q, turned_g, delta)
        return fixed, tuple(jnp.zeros((HEAD_DIM, TILE), F32) for _ in range(heads))

    def step(i, at, size, diagonal, carry):
        fixed, sums = carry
        split_q, split_g, turned_q, turned_g, delta = fixed
        there = span(at, size)
        keys = k_s[there, :]
        values = v_s[there, :]
        new, ps, dss = [], [], []
        for h in range(heads):
            s = dot(keys, turned_q[h]) - lse_ref[0, i, h : h + 1, :]
            if diagonal is not None:
                s = jnp.where(causal(size, diagonal), s, NEG)
            p = jnp.exp(s)
            dp = dot(values, turned_g[h])
            ds = (p * (dp - delta[h])).astype(BF16)
            ps.append(p.astype(BF16))
            dss.append(ds)
            kt = kt_s[h * HEAD_DIM : (h + 1) * HEAD_DIM, there]
            new.append(sums[h] + dot(kt, ds))
        dv = dot(ps[0], split_g[0])
        dk = dot(dss[0], split_q[0])
        for h in range(1, heads):
            dv = dv + dot(ps[h], split_g[h])
            dk = dk + dot(dss[h], split_q[h])
        dv_s[there, :] += dv
        dk_s[there, :] += dk
        return fixed, tuple(new)

    def finish(i, carry):
        dq_s[span(i * TILE, TILE), :] = (jnp.concatenate(carry[1], axis=0).T * SCALE).astype(BF16)

    sweep(tiles, lambda i: sc_ref[1 + row * tiles + i], start, step, finish)
    for m in range(group):
        here = pl.ds(pl.multiple_of((me ^ m) * cap, math.gcd(cap, 128)), cap)
        out_ref[m, :, :wide] = dq_s[here, :]
        out_ref[m, :, wide : 2 * wide] = dk_s[here, :].astype(BF16)
        out_ref[m, :, 2 * wide :] = dv_s[here, :].astype(BF16)


def attend_back(scalars, parts, ctx, grads, q_docs, k_docs, lse, cap, heads):
    group, tokens, cols = parts.shape
    rows = tokens // cap
    tiles = pl.cdiv(group * cap, TILE)
    length = tiles * TILE
    wide = heads * HEAD_DIM
    deep = wide + q_docs.shape[2]
    pair = rows * heads * length * length // 2
    by_row = lambda r, sc: (0, r, 0)
    all_row = lambda r, sc: (r, 0, 0)
    return pl.pallas_call(
        functools.partial(attend_back_kernel, group, cap, tiles, heads),
        grid_spec=pltpu.PrefetchScalarGridSpec(
            num_scalar_prefetch=1,
            grid=(rows,),
            in_specs=[pl.BlockSpec((group, cap, cols), by_row)]
            + [pl.BlockSpec((group, cap, wide), by_row)] * 2
            + [pl.BlockSpec((1,) + q_docs.shape[1:], all_row)] * 2
            + [pl.BlockSpec((1, tiles, heads, TILE), lambda r, sc: (r, 0, 0, 0))],
            out_specs=pl.BlockSpec((group, cap, cols), by_row),
            scratch_shapes=[
                pltpu.VMEM((length, wide), BF16),
                pltpu.VMEM((length, deep), BF16),
                pltpu.VMEM((length, wide), BF16),
                pltpu.VMEM((wide, length), BF16),
            ]
            + [pltpu.VMEM((length, wide), BF16)] * 3
            + [pltpu.VMEM((length, wide), F32)] * 2,
        ),
        out_shape=jax.ShapeDtypeStruct((group, rows * cap, cols), BF16),
        compiler_params=params(),
        cost_estimate=pl.CostEstimate(
            flops=10 * 256 * pair, bytes_accessed=20 * rows * length * wide, transcendentals=pair
        ),
        name="attend_back",
    )(scalars, parts, ctx, grads, q_docs, k_docs, lse)


def norm_back(upper, n, rs, gain):
    e = upper * gain
    return rs * (
        e - jnp.mean(e, axis=-1, keepdims=True) - n * jnp.mean(e * n, axis=-1, keepdims=True)
    )


GELU_A = 0.7978845608028654
GELU_B = 0.044715


VECTORS = 10


def early_cols(cols, late):
    early = cols * 3 // 4
    return cols - early if late else early


def mid_kernel(wide, *refs):
    grid = Grid()
    group, ys, xs, zs = grid.seq, grid.y, grid.x, grid.z
    refs = list(refs)

    def take(n):
        out = refs[:n]
        del refs[:n]
        return out

    ctx_hbm, x_ref, g_ref, ow_hbm, uw_hbm, dw_hbm, ob, gain, shift, ub, db = take(11)
    grads, result_ref, mg_ref, early = take(4)
    down_out, up_out, out_out = take(2 * ys), take(xs + ys), take(zs)
    gots = take(3)
    landed, ctx, ow, uw, dw, hid, rise, mid_s, n2_s, normed, attn, chunk = take(12)
    rings, loaded, lefts = take(3), take(3), take(6)
    send_sem, recv_sem, load_sem, ring_sem, got_sem = take(5)

    me, dp = lax.axis_index("seq"), lax.axis_index("dp")
    core, row = dp % 2, dp // 2
    links = Links(send_sem, recv_sem)
    tokens, width = x_ref.shape
    hidden = hid.shape[1]
    block = min(512, hidden)
    partner_core = {"dp": flip(dp, 1)}
    loads = [
        pltpu.make_async_copy(src, dst, load_sem.at[k])
        for k, (src, dst) in enumerate(
            ((dw_hbm, dw), (ow_hbm, ow), (uw_hbm, uw), (ctx_hbm.at[0], landed.at[0]))
        )
    ]
    for copy in loads:
        copy.start()
    greet(range(1, group), [1])
    first = links.reserve(group)
    for m in range(group - 1, 0, -1):
        links.start(ctx_hbm.at[m], landed.at[m], first + m, first + m, {"seq": flip(me, m)})

    early[...] = jnp.zeros_like(early)
    early[5:6, :] = jnp.sum(g_ref[...].astype(F32), axis=0, keepdims=True)
    loads[0].wait()

    def lanes(f, size):
        return pl.ds(pl.multiple_of(f * size, size), size)

    def before(f, _):
        here = lanes(f, block)
        rise[:, here] = dot(g_ref[...], dw[here, :], NT).astype(BF16)
        return 0

    lax.fori_loop(0, hidden // block, before, 0)
    for copy in loads[1:]:
        copy.wait()
    for m in range(1, group):
        links.arrived(landed.at[m], first + m, {"seq": flip(me, m)})
    for s in range(group):
        chunk[s] = landed[flip(me, s)]
    for s in range(group):
        ctx[:, s * wide : (s + 1) * wide] = chunk[s]
    mid = x_ref[...].astype(F32) + dot(ctx[...], ow[...]) + ob[...]
    mid_s[...] = mid
    n, _ = centre_rows(mid)
    normed[...] = (n * gain[...] + shift[...]).astype(BF16)
    n2_s[...] = jnp.zeros_like(n2_s)

    def through(f, _):
        here = lanes(f, block)
        u = dot(normed[...], uw[:, here]) + ub[:, here]
        square = u * u
        t = jnp.tanh(GELU_A * u * (1.0 + GELU_B * square))
        half = 0.5 * (1.0 + t)
        hid[:, here] = (u * half).astype(BF16)
        slope = half + 0.5 * GELU_A * u * (1.0 - t * t) * (1.0 + 3.0 * GELU_B * square)
        up = (rise[:, here].astype(F32) * slope).astype(BF16)
        rise[:, here] = up
        n2_s[...] += dot(up, uw[:, here], NT)
        return 0

    def ordered(ring, spot, total, parts, share, got):
        for s in range(parts):
            rel = flip(me % parts, s)
            piece = total[s * share : (s + 1) * share]
            if got is not None:
                piece = piece + got[rel % xs, rel // xs].astype(F32)
            ring[spot, rel % xs, rel // xs] = piece.astype(BF16)

    def outputs(item, o, z, cols, ring):
        if item == 0:
            first = down_out[0].shape[-1]
            for h, here in enumerate((slice(0, first), slice(first, width))):
                yield ring.at[:, :, :, here], down_out[2 * o + h].at[:, z]
        elif item == 1:
            first = up_out[0].shape[-1]
            if cols.start >= first:
                here = slice(cols.start - first, cols.stop - first)
                yield ring, up_out[xs + o].at[:, :, :, here]
            else:
                for x in range(xs):
                    yield ring.at[x], up_out[x].at[o, :, :, cols]
        else:
            for z in range(zs):
                yield ring.at[:, z], out_out[z].at[o]

    def weight_grad(item, a, b):
        share = a.shape[1] // (2 * ys * group)
        parts = min(group, max(256 // share, xs))
        sub = group // parts
        depth = parts // xs
        cols = b.shape[1]
        piece = min(1024, cols)
        pieces = cols // piece
        count = ys * sub * pieces
        ring, got, left_s = rings[item], loaded[item], lefts[2 * item : 2 * item + 2]
        spots = ring.shape[0] // 2
        slot = links.reserve(count)

        def unit(n):
            u = n // pieces
            return ys - 1 - u // sub, u % sub, n % pieces

        def start_of(c, n):
            o, k, _ = unit(n)
            at = (flip(row, o, ys) * 2 + flip(core, c, 2)) * group * share
            return at + flip(me // parts, k, sub) * parts * share

        def product(c, n):
            o, k, p = unit(n)
            left = left_s[c]

            @pl.when(p == 0)
            def _():
                at = pl.multiple_of(start_of(c, n), 128)
                left[...] = transposed(a[:, pl.ds(at, parts * share)])

            return dot(left[...], b[:, pl.ds(pl.multiple_of(p * piece, piece), piece)])

        def place(n):
            o, k, p = unit(n)
            columns = pl.ds(pl.multiple_of(p * piece, piece), piece)
            return (o, slice(None), pl.ds(k * depth, depth), slice(None), columns)

        def away(n):
            links.left(ring.at[n % spots], slot + n, partner_core)

        def send(n):
            @pl.when(n >= spots)
            def _():
                away(n - spots)

            ordered(ring, n % spots, product(1, n), parts, share, None)
            there = gots[item].at[place(n)]
            links.start(ring.at[n % spots], there, slot + n, slot + n, partner_core, later=False)

        def fetch(n):
            src = gots[item].at[place(n)]
            return pltpu.make_async_copy(src, got.at[n % 2], got_sem.at[2 * item + n % 2])

        def fetch_start(n):
            links.arrived(gots[item].at[place(n)], slot + n, partner_core)
            fetch(n).start()

        def written(n, act):
            for fixed in range(ys):
                for p in range(pieces):
                    o, k, q = unit(n)

                    @pl.when((o == fixed) & (q == p))
                    def _(fixed=fixed, p=p):
                        spot = spots + n % spots
                        z = pl.ds(k * depth, depth)
                        here = slice(p * piece, (p + 1) * piece)
                        copies = outputs(item, fixed, z, here, ring.at[spot])
                        for h, (src, dst) in enumerate(copies):
                            at = (item * spots + n % spots) * max(2, xs, zs) + h
                            act(pltpu.make_async_copy(src, dst, ring_sem.at[at]))

        def keep(n):
            @pl.when(n + 1 < count)
            def _():
                fetch_start(n + 1)

            @pl.when(n >= spots)
            def _():
                written(n - spots, lambda copy: copy.wait())

            total = product(0, n)
            fetch(n).wait()
            ordered(ring, spots + n % spots, total, parts, share, got.at[n % 2])
            written(n, lambda copy: copy.start())

        def rest(act):
            for n in range(max(0, count - spots), count):
                act(n)

        def finish():
            rest(lambda n: written(n, lambda copy: copy.wait()))

        return count, send, lambda: rest(away), fetch_start, keep, finish, start_of

    first_job = weight_grad(0, hid, g_ref)
    steps = hidden // block
    per = first_job[0] * 2 // steps

    def mine(i):
        c = 1 - 2 * i // steps
        f = first_job[6](c, (i % (steps // 2)) * per) // block
        through(f, 0)

        @pl.when(c == 1)
        def _():
            for k in range(per):
                first_job[1](i * per + k)

    loop(0, steps, mine)
    first_job[2]()
    n, rs = centre_rows(mid_s[...])
    n2 = n2_s[...]
    early[3:4, :] = jnp.sum(n2 * n, axis=0, keepdims=True)
    early[4:5, :] = jnp.sum(n2, axis=0, keepdims=True)
    mid_grad = g_ref[...].astype(F32) + norm_back(n2, n, rs, gain[...])
    mg_ref[...] = mid_grad
    attn[...] = mid_grad.astype(BF16)
    full = dot(attn[...], ow[...], NT).astype(BF16)
    for s in range(group):
        chunk[flip(me, s)] = full[:, s * wide : (s + 1) * wide]
    second = links.reserve(group)
    for m in range(group - 1, 0, -1):
        links.start(chunk.at[m], grads.at[m], second + m, second + m, {"seq": flip(me, m)})
    own = pltpu.make_async_copy(chunk.at[0], grads.at[0], load_sem.at[0])
    own.start()

    jobs = [first_job, weight_grad(1, normed, rise), weight_grad(2, ctx, attn)]
    for stage in range(1, len(jobs) + 1):
        new = jobs[stage] if stage < len(jobs) else None
        old = jobs[stage - 1]
        old[3](0)

        def turn(n, new=new, old=old):
            for job, act in ((new, 1), (old, 4)):
                if job:
                    if new and old and job[0] < max(new[0], old[0]):
                        pl.when(n < job[0])(lambda job=job, act=act: job[act](n))
                    else:
                        job[act](n)

        loop(0, max(job[0] for job in (new, old) if job), turn)
        if new:
            new[2]()
        old[5]()


    def finished(k):
        here = lanes(k, 256)
        result_ref[:, here] = (
            mid_s[:, here] + (dot(hid[...], dw[:, here]) + db[:, here])
        ).astype(BF16)

    loop(0, width // 256, finished)
    early[2:3, :] = jnp.sum(attn[...].astype(F32), axis=0, keepdims=True)
    for k in range(hidden // width):
        part = rise[:, k * width : (k + 1) * width].astype(F32)
        early[6 + k : 7 + k, :] = jnp.sum(part, axis=0, keepdims=True)
    for m in range(1, group):
        links.arrived(grads.at[m], second + m, {"seq": flip(me, m)})
    own.wait()
    links.drain()


def feed_forward(branch, ctx, x, g, ow, ob, gain, shift, uw, ub, dw, db):
    grid = Grid()
    group, ys, xs, zs = grid.seq, grid.y, grid.x, grid.z
    rows, width = x.shape
    wide = width // group
    hidden = uw.shape[1]
    here = any_spec()
    anywhere = pl.BlockSpec(memory_space=pl.ANY)
    shape = jax.ShapeDtypeStruct
    low, high = width // (grid.dp * group), hidden // (grid.dp * group)
    vectors = VECTORS + group
    vectors += -vectors % 8
    sums = [
        shape((ys, xs, zs, high, width), BF16),
        shape((ys, xs, zs, low, hidden), BF16),
        shape((ys, xs, zs, low, width), BF16),
    ]
    parts = lambda share: min(group, max(256 // share, xs))
    block = lambda share: (xs, parts(share) // xs, share, width)
    rings = [pltpu.VMEM((n,) + block(share), BF16) for n in (4, 2) for share in (high, low, low)]
    turned = [pltpu.VMEM((parts(s) * s, rows), BF16) for s in (high, low, low) for _ in range(2)]
    blocks = ys * (group // parts(high)) + ys * (hidden // width) + ys
    vmem = lambda dims, kind=BF16: pltpu.VMEM(dims, kind)
    return pl.pallas_call(
        functools.partial(mid_kernel, wide),
        in_specs=[anywhere, here, here, anywhere, anywhere, anywhere] + [here] * 5,
        out_specs=[anywhere, here, here, here] + [anywhere] * (3 * ys + xs + zs + 3),
        out_shape=[
            shape((group, rows, wide), BF16),
            shape((rows, width), BF16),
            shape((rows, width), F32),
            shape((vectors, width), F32),
        ]
        + [shape((xs, zs, high, early_cols(width, k)), BF16) for _ in range(ys) for k in range(2)]
        + [shape((ys, zs, low, early_cols(hidden, 0)), BF16)] * xs
        + [shape((xs, zs, low, early_cols(hidden, 1)), BF16)] * ys
        + [shape((ys, xs, low, width), BF16)] * zs
        + sums,
        scratch_shapes=[
            vmem((group, rows, wide)),
            vmem((rows, width)),
            vmem((width, width)),
            vmem((width, hidden)),
            vmem((hidden, width)),
            vmem((rows, hidden)),
            vmem((rows, hidden)),
            vmem((rows, width), F32),
            vmem((rows, width), F32),
            vmem((rows, width)),
            vmem((rows, width)),
            vmem((group, rows, wide)),
        ]
        + rings
        + turned
        + [
            pltpu.SemaphoreType.DMA((2 * group + blocks,)),
            pltpu.SemaphoreType.DMA((2 * group + blocks,)),
            pltpu.SemaphoreType.DMA((4,)),
            pltpu.SemaphoreType.DMA((6 * max(2, xs, zs),)),
            pltpu.SemaphoreType.DMA((6,)),
        ],
        compiler_params=params(collective_id=3 * branch + 2, has_side_effects=True),
        cost_estimate=pl.CostEstimate(
            flops=8 * rows * width * width + 12 * rows * width * hidden,
            bytes_accessed=4 * width * width + 8 * width * hidden,
            transcendentals=rows * hidden,
        ),
        name="feed_forward",
    )(ctx, x, g, ow, uw, dw, ob[None], gain[None], shift[None], ub[None], db[None])


def partner(axis, mask):
    return [(i, i ^ mask) for i in range(lax.axis_size(axis))]


def exchange(axis, blocks):
    grid = Grid()
    out = [blocks[0]]
    for r in range(1, grid.size[axis]):
        name, mask = ("dp", 2 * r) if axis == "y" else ("seq", grid.mask(axis, r))
        out.append(lax.ppermute(blocks[r], name, partner(name, mask)))
    return out


def item_counts(ys, xs, zs):
    return (ys - 1) + 5, (xs - 1) + 5, 7, 7, (zs - 1) + 4


def tail_kernel(wide, *refs):
    grid = Grid()
    group, ys, xs, zs = grid.seq, grid.y, grid.x, grid.z
    refs = list(refs)

    def take(n):
        out = refs[:n]
        del refs[:n]
        return out

    back, weight, normed_ref, x_hbm, mg_hbm, gain_ref, early_ref = take(7)
    down_in, down_rest = take(ys), take(ys)
    up_in, up_rest = take(xs), take(ys)
    out_in = take(zs)
    tg_ref, project_ref, down_ref, up_ref, out_ref, vec_ref = take(6)
    landed, w_s, x_s, mg_s, acc, turned, order = take(7)
    send_a, send_b, keep_a, keep_b, pair_a, pair_b = take(6)
    got_a1, got_b1, mid_a, mid_b, got_a2, got_b2, z_a, z_b, got_za, got_zb = take(10)
    items = [take(count) for count in item_counts(ys, xs, zs)]
    vec_s, vec_g = take(2)
    send_sem, recv_sem, load_sem = take(3)

    me, dp = lax.axis_index("seq"), lax.axis_index("dp")
    core, row = dp % 2, dp // 2
    links = Links(send_sem, recv_sem)
    tokens, width = normed_ref.shape
    share = project_ref.shape[1]
    partner_core = {"dp": flip(dp, 1)}
    loads = []

    def load(src, dst):
        copy = pltpu.make_async_copy(src, dst, load_sem.at[len(loads)])
        copy.start()
        loads.append(copy)
        return copy

    greet(range(1, group), [1] + [2 * r for r in range(1, ys)])

    first = links.reserve(group)
    for m in range(1, group):
        links.start(back.at[m], landed.at[m], first + m, first + m, {"seq": flip(me, m)})
    own = load(back.at[0], landed.at[0])
    down_a, up_a, down_b, up_b, out_a = items
    loaded = [
        [load(src, dst) for src, dst in zip(up_in, [up_a[xs - 1]] + up_a[: xs - 1])],
        [load(src, dst) for src, dst in zip(down_in, [down_a[ys - 1]] + down_a[: ys - 1])],
        [load(src, dst) for src, dst in zip(out_in, [out_a[zs - 1]] + out_a[: zs - 1])],
        [load(src, down_b[0].at[o]) for o, src in enumerate(down_rest)],
        [load(src, up_b[0].at[o]) for o, src in enumerate(up_rest)],
    ]

    own_x = load(x_hbm, x_s)
    own_mg = load(mg_hbm, mg_s)
    ahead = w_s.shape[0]
    weight_first = len(loads)

    def weight_copies(m):
        source = flip(me, m, group)
        return [
            pltpu.make_async_copy(
                weight_view(weight, part, source, width, wide),
                w_s.at[m % ahead, part],
                load_sem.at[weight_first + 3 * m + part],
            )
            for part in range(3)
        ]

    for m in range(ahead):
        for copy in weight_copies(m):
            copy.start()

    def summed(axis, block, got):
        return Summed(links, grid, axis, block, got)

    up_a1 = summed("y", up_a[xs - 1], up_a[xs])
    up_a2 = LineSum(links, grid, *up_a[xs + 1 :])
    down_a1 = summed("x", down_a[ys - 1], down_a[ys])
    down_a2 = LineSum(links, grid, *down_a[ys + 1 :])
    down_b1, down_b2 = summed("y", down_b[0], down_b[1]), summed("x", down_b[2], down_b[3])
    down_b3 = LineSum(links, grid, *down_b[4:])
    up_b1, up_b2 = summed("y", up_b[0], up_b[1]), summed("x", up_b[2], up_b[3])
    up_b3 = LineSum(links, grid, *up_b[4:])
    out_1 = summed("y", out_a[zs - 1], out_a[zs])
    out_2 = summed("x", out_a[zs + 1], out_a[zs + 2])
    lines = (up_a2, down_a2, up_b3, down_b3)
    for copies in loaded[3:]:
        for copy in copies:
            copy.wait()
    down_b1.send()
    up_b1.send()
    for copies, item, count, stage in (
        (loaded[0], up_a, xs, up_a1),
        (loaded[1], down_a, ys, down_a1),
        (loaded[2], out_a, zs, out_1),
    ):
        for copy in copies:
            copy.wait()
        add_into(item[count - 1], item[: count - 1])
        stage.send()

    for k in range(0, width, 256):
        turned[k : k + 256, :] = normed_ref[:, k : k + 256].astype(F32).T
    for c in range(2):
        for o in range(ys):

            def place(s, c=c, o=o):
                there = (flip(row, o) * 2 + flip(core, c)) * group + flip(me, s, group)
                rows = turned[pl.ds(pl.multiple_of(there * share, share), share), :]
                order[c, o, s % xs, s // xs] = rows.astype(BF16)

            loop(0, group, place)
    half = ys * group * share
    acc[...] = jnp.zeros_like(acc)
    vec_s[0] = early_ref[...]
    own.wait()

    pair_first = links.reserve(2 * group)
    a1 = SlotSum(links, grid, "y", group, keep_a, got_a1)
    a2 = SlotSum(links, grid, "x", group, mid_a, got_a2)
    b1 = SlotSum(links, grid, "x", group, keep_b, got_b1, inner=True)
    b2 = SlotSum(links, grid, "y", group, mid_b, got_b2)
    cut = 2 * wide

    def multiply(m):
        source = flip(me, m, group)

        @pl.when(m > 0)
        def _():
            links.arrived(landed.at[m], first + m, {"seq": source})

        for k, (send, keep, pair, cols) in enumerate(
            (
                (send_a, keep_a, pair_a, slice(0, cut)),
                (send_b, keep_b, pair_b, slice(cut, 3 * wide)),
            )
        ):
            grad = landed[m, :, cols]
            left = order[1].reshape(half, tokens)
            send[m] = dot(left, grad).reshape(send.shape[1:]).astype(BF16)
            slot = pair_first + 2 * m + k
            links.start(send.at[m], pair.at[m], slot, slot, partner_core, later=False)
            left = order[0].reshape(half, tokens)
            keep[m] = dot(left, grad).reshape(keep.shape[1:]).astype(BF16)
        block = landed[m]
        for copy in weight_copies(m):
            copy.wait()
        pieces = [w_s[m % ahead, part] for part in range(3)]
        acc[...] += dot(block, jnp.concatenate(pieces, axis=1), NT)

        @pl.when(m + ahead < group)
        def _():
            for copy in weight_copies(m + ahead):
                copy.start()

        sums = jnp.sum(block.astype(F32), axis=0, keepdims=True)
        vec_s[0, pl.ds(VECTORS + source, 1), : 3 * wide] = sums

    def paired(m):
        for k, (keep, pair, nxt) in enumerate(((keep_a, pair_a, a1), (keep_b, pair_b, b1))):
            links.arrived(pair.at[m], pair_first + 2 * m + k, partner_core)
            keep[m] = total_of(keep[m], [pair[m]], BF16)
            nxt.send(m)

    def second(m):
        mid_a[m] = a1.receive(m).astype(BF16)
        a2.send(m)
        mid_b[m] = b1.receive(m).astype(BF16)
        b2.send(m)

    def third(m):
        for block, stage in ((z_a, a2), (z_b, b2)):
            total = stage.receive(m).astype(BF16)
            for z in range(zs):
                block[z, m] = total[z]

    def input_grads():
        own_x.wait()
        own_mg.wait()
        n, rs = centre_rows(x_s[...].astype(F32))
        n1 = acc[...]
        tg_ref[...] = (mg_s[...] + norm_back(n1, n, rs, gain_ref[...])).astype(BF16)
        vec_s[0, 0:1, :] = jnp.sum(n1 * n, axis=0, keepdims=True)
        vec_s[0, 1:2, :] = jnp.sum(n1, axis=0, keepdims=True)

    vec_first = links.reserve(1 + (ys - 1) + (xs - 1) + (zs - 1))
    hops = [[partner_core]]
    for axis in ("y", "x", "z"):
        hops.append([grid.device(axis, r) for r in range(1, grid.size[axis])])

    def vec_send(k):
        at = vec_first + sum(len(h) for h in hops[:k])
        for r, device in enumerate(hops[k]):
            links.start(vec_s.at[k], vec_g.at[at + r - vec_first], at + r, at + r, device)

    def vec_receive(k):
        at = vec_first + sum(len(h) for h in hops[:k])
        got = []
        for r, device in enumerate(hops[k]):
            links.arrived(vec_g.at[at + r - vec_first], at + r, device)
            got.append(vec_g[at + r - vec_first])
        total = total_of(vec_s[k], got, F32)
        if k + 1 < len(hops):
            vec_s[k + 1] = total
            vec_send(k + 1)
        else:
            vec_ref[...] = total

    def multiply_next(m):
        multiply(m)

        @pl.when(m > 0)
        def _():
            paired(m - 1)

    loop(0, group // 2 + 1, multiply_next)
    down_b1.receive(down_b[2])
    down_b2.send()
    loop(group // 2 + 1, group, multiply_next)
    paired(group - 1)
    down_a1.receive(down_a[ys + 1])
    down_a2.hop(0)
    up_b1.receive(up_b[2])
    up_b2.send()
    up_a1.receive(up_a[xs + 1])
    up_a2.hop(0)
    input_grads()
    vec_send(0)
    out_1.receive(out_a[zs + 1])
    out_2.send()
    down_b2.receive(down_b[4])
    down_b3.hop(0)
    for k in range(1, zs - 1):
        down_a2.hop(k)
        up_a2.hop(k)
    vec_receive(0)
    loop(0, group // 2, second)
    for k in range(1, zs - 1):
        down_b3.hop(k)
    loop(group // 2, group, second)
    vec_receive(1)
    up_b2.receive(up_b[4])
    up_b3.hop(0)
    loop(0, group // 2, third)
    for k in range(1, zs - 1):
        up_b3.hop(k)
    loop(group // 2, group, third)

    z_first = links.reserve(2 * (zs - 1))
    for r in range(1, zs):
        for k, (block, got) in enumerate(((z_a, got_za), (z_b, got_zb))):
            slot = z_first + 2 * (r - 1) + k
            links.start(block.at[r], got.at[r - 1], slot, slot, grid.device("z", r))
    vec_receive(2)
    cut_down, cut_up = early_cols(down_ref.shape[1], 0), early_cols(up_ref.shape[1], 0)
    out_2.receive_last(out_ref)
    up_a2.finish(up_ref, slice(0, cut_up))
    down_a2.finish(down_ref, slice(0, cut_down))
    up_b3.finish(up_ref, slice(cut_up, up_ref.shape[1]))
    down_b3.finish(down_ref, slice(cut_down, down_ref.shape[1]))
    vec_receive(3)
    for r in range(1, zs):
        for k, got in enumerate((got_za, got_zb)):
            links.arrived(got.at[r - 1], z_first + 2 * (r - 1) + k, grid.device("z", r))

    def share_of(m):
        source = flip(me, m, group)
        for block, got, cols in (
            (z_a, got_za, slice(0, cut)),
            (z_b, got_zb, slice(cut, 3 * wide)),
        ):
            others = [got[r - 1, flip(m, grid.mask("z", r), group)] for r in range(1, zs)]
            project_ref[source, :, cols] = total_of(block[0, m], others, F32)

    loop(0, group, share_of)

    def drain(m):
        for k, send in enumerate((send_a, send_b)):
            links.left(send.at[m], pair_first + 2 * m + k, partner_core)
        for stage in (a1, a2, b1, b2):
            stage.drain(m)

    loop(0, group, drain)
    links.drain()


def tail(branch, back, normed, weight, x, mid_grad, gain, early, down, up, out):
    grid = Grid()
    group, ys, xs, zs = grid.seq, grid.y, grid.x, grid.z
    rows, width = x.shape
    wide = width // group
    shape = jax.ShapeDtypeStruct
    any_place = pl.BlockSpec(memory_space=pl.ANY)
    here = any_spec()
    share = width // (grid.dp * grid.seq)
    (down, down_rest), (up, up_rest) = down, up
    down_block, up_block, out_block = down[0].shape, up[0].shape, out[0].shape
    vmem = lambda dims, kind=BF16: pltpu.VMEM(tuple(dims), kind)
    a_full, b_full = (share, 2 * wide), (share, wide)
    copies = (
        group
        + 2 * group
        + 2 * group * (ys - 1)
        + 2 * group * (xs - 1)
        + 4 * (xs - 1)
        + 4 * (ys - 1)
        + 8 * zs
        + (1 + (ys - 1) + (xs - 1) + (zs - 1))
        + 2 * (zs - 1)
    )
    hops = 1 + (ys - 1) + (xs - 1) + (zs - 1)
    scratch = (
        [
            vmem((group, rows, 3 * wide)),
            vmem((min(4, group), 3, width, wide)),
            vmem((rows, width)),
            vmem((rows, width), F32),
            vmem((rows, width), F32),
            vmem((width, rows), F32),
            vmem((2, ys, xs, zs, share, rows)),
        ]
        + [vmem((group, ys, xs, zs) + a_full), vmem((group, ys, xs, zs) + b_full)] * 3
        + [
            vmem((group, ys - 1, xs, zs) + a_full),
            vmem((group, xs - 1, ys, zs) + b_full),
            vmem((group, xs, zs) + a_full),
            vmem((group, ys, zs) + b_full),
            vmem((group, xs - 1, zs) + a_full),
            vmem((group, ys - 1, zs) + b_full),
            vmem((zs, group) + a_full),
            vmem((zs, group) + b_full),
            vmem((zs - 1, group) + a_full),
            vmem((zs - 1, group) + b_full),
        ]
        + [vmem(down_block)] * ys
        + [vmem((xs - 1,) + down_block[1:])]
        + [vmem(down_block[1:])] * 3
        + [vmem(up_block)] * xs
        + [vmem((ys - 1,) + up_block[1:])]
        + [vmem(up_block[1:])] * 3
        + [
            vmem((ys,) + down_rest[0].shape),
            vmem((ys - 1,) + down_rest[0].shape),
            vmem(down_rest[0].shape),
            vmem((xs - 1,) + down_rest[0].shape[1:]),
        ]
        + [vmem(down_rest[0].shape[1:])] * 3
        + [
            vmem((ys,) + up_rest[0].shape),
            vmem((ys - 1,) + up_rest[0].shape),
            vmem(up_rest[0].shape),
            vmem((xs - 1,) + up_rest[0].shape[1:]),
        ]
        + [vmem(up_rest[0].shape[1:])] * 3
        + [vmem(out_block)] * zs
        + [
            vmem((ys - 1,) + out_block[1:]),
            vmem(out_block[1:]),
            vmem((xs - 1,) + out_block[2:]),
        ]
        + [
            vmem((4,) + early.shape, F32),
            vmem((hops,) + early.shape, F32),
            pltpu.SemaphoreType.DMA((copies,)),
            pltpu.SemaphoreType.DMA((copies,)),
            pltpu.SemaphoreType.DMA((3 + 3 * ys + xs + zs + 3 * group,)),
        ]
    )
    return pl.pallas_call(
        functools.partial(tail_kernel, wide),
        in_specs=[any_place, any_place, here, any_place, any_place, here, here]
        + [any_place] * (3 * ys + xs + zs),
        out_specs=[here] * 6,
        out_shape=[
            shape((rows, width), BF16),
            shape((group, share, 3 * wide), F32),
            shape((down_block[2], width), F32),
            shape((up_block[2], up_block[3] + up_rest[0].shape[3]), F32),
            shape(out_block[2:], F32),
            shape(early.shape, F32),
        ],
        scratch_shapes=scratch,
        compiler_params=params(collective_id=3 * branch + 3, has_side_effects=True),
        cost_estimate=pl.CostEstimate(
            flops=12 * rows * width * width, bytes_accessed=2**25, transcendentals=0
        ),
        name="tail",
    )(back, weight, normed, x, mid_grad, gain[None], early, *down, *down_rest, *up, *up_rest, *out)


def agree_kernel(count_ref, most_ref, got, send_sem, recv_sem):
    links = Links(send_sem, recv_sem)
    others = lax.axis_size("dp") - 1
    greet([], range(1, others + 1))
    dp = lax.axis_index("dp")
    for m in range(1, others + 1):
        links.start(count_ref, got.at[m - 1], m - 1, m - 1, {"dp": flip(dp, m)})
    most = count_ref[...]
    for m in range(1, others + 1):
        links.arrived(got.at[m - 1], m - 1, {"dp": flip(dp, m)})
        most = jnp.maximum(most, got[m - 1])
    most_ref[...] = most
    links.drain()


def agree(count):
    others = lax.axis_size("dp") - 1
    block = jnp.broadcast_to(count.astype(F32), (8, 128))
    most = pl.pallas_call(
        agree_kernel,
        in_specs=[any_spec()],
        out_specs=any_spec(),
        out_shape=jax.ShapeDtypeStruct((8, 128), F32),
        scratch_shapes=[
            pltpu.VMEM((others, 8, 128), F32),
            pltpu.SemaphoreType.DMA((others,)),
            pltpu.SemaphoreType.DMA((others,)),
        ],
        compiler_params=pltpu.CompilerParams(collective_id=0, has_side_effects=True),
        name="agree",
    )(block)
    return most[0, 0]


def layer(
    branch,
    cap,
    docs,
    tokens,
    first_gain,
    first_shift,
    project_weight,
    query_bias,
    value_bias,
    output_weight,
    output_bias,
    second_gain,
    second_shift,
    up_weight,
    up_bias,
    down_weight,
    down_bias,
    live,
    rank,
    ids,
    upstream,
):
    group = lax.axis_size("seq")
    outer = lax.axis_size("dp") // 2
    rows, shard, width = tokens.shape
    wide = width // group
    heads = wide // HEAD_DIM
    me = lax.axis_index("seq").astype(jnp.int32)
    dp = lax.axis_index("dp").astype(jnp.int32)
    count = rows * cap

    slot = jnp.arange(cap, dtype=jnp.int32)[:, None]
    chosen = (rank[:, :, None, :] == slot) & live[:, :, None, :]
    ids = jnp.sum(
        jnp.where(chosen, ids.reshape(rows, group, 1, shard) + 1, 0), axis=3
    ).reshape(rows, group * cap)
    tiles = pl.cdiv(group * cap, TILE)
    ids = jnp.pad(ids, ((0, 0), (0, tiles * TILE - group * cap)))
    padded = -docs % 128
    unit = ids[:, :, None] == 1 + jnp.arange(docs + padded, dtype=jnp.int32)
    q_docs = unit.astype(BF16)
    k_docs = jnp.where(unit | (jnp.arange(docs + padded) >= docs), 0.0, NEG).astype(BF16)
    last = jnp.max(ids.reshape(rows, tiles, TILE), axis=2)
    first = jnp.min(jnp.where(ids == 0, docs + 1, ids).reshape(rows, tiles, TILE), axis=2)
    number = jnp.arange(tiles, dtype=jnp.int32)
    needed = (last[:, None, :] >= first[:, :, None]) & (number < number[:, None])
    low = jnp.min(jnp.where(needed, number, number[:, None]), axis=2) // 2
    scalars = jnp.concatenate([me[None], low.reshape(-1)])
    pick = lax.dynamic_index_in_dim(chosen, me, 1, keepdims=False).astype(BF16)
    live_here = lax.dynamic_index_in_dim(live, me, 1, keepdims=False)[:, :, None]

    def pack(values):
        return (
            jnp.einsum("rct,rtd->rcd", pick, values, preferred_element_type=F32)
            .astype(BF16)
            .reshape(count, width)
        )

    def unpack(packed, values):
        spread = jnp.einsum(
            "rct,rcd->rtd", pick, packed.reshape(rows, cap, width), preferred_element_type=F32
        ).astype(BF16)
        return jnp.where(live_here, spread, values)

    x = pack(tokens)
    g = pack(upstream)

    biases = jnp.stack([query_bias, jnp.zeros_like(query_bias), value_bias])
    bias_parts = biases.reshape(3, group, wide).transpose(1, 0, 2).reshape(group, 1, 3 * wide)

    weight = split_weight(project_weight, group)
    normed, head_parts = project(branch, x, first_gain, first_shift, weight, bias_parts)
    ctx_chunks, lse = attend(scalars, head_parts, q_docs, k_docs, cap, heads)
    grad_parts, result, middle_grad, early, *halves = feed_forward(
        branch,
        ctx_chunks,
        x,
        g,
        output_weight,
        output_bias,
        second_gain,
        second_shift,
        up_weight,
        up_bias,
        down_weight,
        down_bias,
    )
    ys, xs = Grid().y, Grid().x
    down, up, out = halves[: 2 * ys], halves[2 * ys : 3 * ys + xs], halves[3 * ys + xs : -3]
    down_parts = exchange("y", down[0::2]), down[1::2]
    up_parts = exchange("x", up[:xs]), up[xs:]
    out_parts = exchange("z", out)
    back = attend_back(
        scalars, head_parts, ctx_chunks, grad_parts, q_docs, k_docs, lse, cap, heads
    )
    token_grad, project_share, down_share, up_share, out_share, sums = tail(
        branch, back, normed, weight, x, middle_grad, first_gain, early, down_parts, up_parts, out_parts
    )
    project_share = project_share.reshape(group, -1, 3, wide).transpose(1, 2, 0, 3)
    devices = 2 * outer * group
    index = dp * group + me
    mine = lambda v: lax.dynamic_index_in_dim(v, index, 1, keepdims=False)
    singles = mine(sums[:6].reshape(6, devices, -1))
    up_bias_share = mine(sums[6:VECTORS].reshape(1, devices, -1))[0]
    by_part = sums[VECTORS : VECTORS + group, : 3 * wide].reshape(group, 3, wide).transpose(1, 0, 2)
    by_part = mine(by_part.reshape(3, devices, -1))
    return (
        unpack(result, tokens),
        unpack(token_grad, upstream),
        singles[0],
        singles[1],
        project_share.reshape(-1, 3 * width),
        by_part[0],
        by_part[2],
        out_share,
        singles[2],
        singles[3],
        singles[4],
        up_share,
        up_bias_share,
        down_share,
        singles[5],
    )


CAPS = (12, 14, 16, 10)


def per_device(*args):
    *most, doc_offsets, exit_layers, layer_index, upstream = args
    rows, shard, _ = most[0].shape
    group = lax.axis_size("seq")
    active = exit_layers > layer_index[0]
    place = jnp.arange(active.shape[1], dtype=jnp.int32)
    ids = jnp.sum((doc_offsets[:, 1:, None] <= place).astype(jnp.int32), axis=1)
    live = active.reshape(rows, group, shard)
    rank = jnp.cumsum(live.astype(jnp.int32), axis=2) - 1
    caps = [shard * k // 16 for k in CAPS]
    count = agree(jnp.max(jnp.sum(live.astype(jnp.int32), axis=2)))
    branch = sum(
        jnp.where((count <= cap) & (count > max([0] + [c for c in caps if c < cap])), k, 0)
        for k, cap in enumerate(caps)
    )
    branch = jnp.where(count <= 0, caps.index(min(caps)), branch)
    steps = [
        functools.partial(layer, k, cap, doc_offsets.shape[1]) for k, cap in enumerate(caps)
    ]
    return lax.switch(branch, steps, *most, live, rank, ids, upstream)


def solution(mesh):
    rows = P("dp", "seq", None)
    shares = P(("dp", "seq"))
    wide_shares = P(("dp", "seq"), None)
    in_specs = (rows,) + (P(),) * 13 + (P("dp", None), P("dp", None), P(), rows)
    out_specs = (
        rows,
        rows,
        shares,
        shares,
        wide_shares,
        shares,
        shares,
        wide_shares,
        shares,
        shares,
        shares,
        wide_shares,
        shares,
        wide_shares,
        shares,
    )
    return jax.shard_map(
        per_device, mesh=mesh, in_specs=in_specs, out_specs=out_specs, check_vma=False
    )
```

```python
import functools
import math

import jax
import jax.numpy as jnp
from jax import lax
from jax.experimental import pallas as pl
from jax.experimental.pallas import tpu as pltpu
from jax.sharding import PartitionSpec as P

HEAD_DIM = 64
SCALE = HEAD_DIM**-0.5
TILE = 256
PAIR = 2 * TILE
NEG = -1e30
EPS = 1e-05
VMEM_LIMIT = 60 * 2**20
F32 = jnp.float32
BF16 = jnp.bfloat16

NT = (((1,), (1,)), ((), ()))
NN = (((1,), (0,)), ((), ()))
TN = (((0,), (0,)), ((), ()))


def dot(a, b, dims=NN):
    return lax.dot_general(a, b, dims, preferred_element_type=F32)


def any_spec():
    return pl.BlockSpec(memory_space=pltpu.VMEM)


def params(**kw):
    return pltpu.CompilerParams(vmem_limit_bytes=VMEM_LIMIT, **kw)


def centre_rows(x):
    centred = x - jnp.mean(x, axis=-1, keepdims=True)
    spread = jnp.mean(centred * centred, axis=-1, keepdims=True)
    rs = lax.rsqrt(spread + EPS)
    return centred * rs, rs


def smem():
    return pl.BlockSpec(memory_space=pltpu.SMEM)


def flip(index, mask, size=64):
    bit = 1
    out = index
    while bit < size:
        if not isinstance(mask, int):
            ours, theirs = (index // bit) % 2, (mask // bit) % 2
            out = out + bit * (theirs - 2 * ours * theirs)
        elif mask & bit:
            out = out + bit * (1 - 2 * ((index // bit) % 2))
        bit *= 2
    return out


def loop(first, last, body):
    def turn(i, _):
        body(i)
        return 0

    lax.fori_loop(first, last, turn, 0)


class Links:
    def __init__(self, send_sem, recv_sem):
        self.send_sem, self.recv_sem, self.used, self.sent = send_sem, recv_sem, 0, []

    def reserve(self, count):
        first, self.used = self.used, self.used + count
        return first

    def start(self, src, dst, slot, there, device, later=True):
        copy = pltpu.make_async_remote_copy(
            src_ref=src,
            dst_ref=dst,
            send_sem=self.send_sem.at[slot],
            recv_sem=self.recv_sem.at[there],
            device_id=device,
            device_id_type=pl.DeviceIdType.MESH,
        )
        copy.start()
        if later:
            self.sent.append(copy)

    def left(self, src, slot, device):
        pltpu.make_async_remote_copy(
            src_ref=src,
            dst_ref=src,
            send_sem=self.send_sem.at[slot],
            recv_sem=self.recv_sem.at[slot],
            device_id=device,
            device_id_type=pl.DeviceIdType.MESH,
        ).wait_send()

    def arrived(self, ref, slot, device):
        pltpu.make_async_remote_copy(
            src_ref=ref,
            dst_ref=ref,
            send_sem=self.send_sem.at[slot],
            recv_sem=self.recv_sem.at[slot],
            device_id=device,
            device_id_type=pl.DeviceIdType.MESH,
        ).wait_recv()

    def drain(self):
        for copy in self.sent:
            copy.wait_send()


def greet(seq_masks, dp_masks):
    me, dp = lax.axis_index("seq"), lax.axis_index("dp")
    barrier = pltpu.get_barrier_semaphore()
    others = [{"seq": flip(me, m)} for m in seq_masks] + [{"dp": flip(dp, m)} for m in dp_masks]
    for device in others:
        pl.semaphore_signal(barrier, inc=1, device_id=device, device_id_type=pl.DeviceIdType.MESH)
    pl.semaphore_wait(barrier, len(others))


class Grid:
    def __init__(self):
        self.dp, self.seq = lax.axis_size("dp"), lax.axis_size("seq")
        self.y = self.dp // 2
        self.x = min(self.y, self.seq)
        self.z = self.seq // self.x
        self.size = {"y": self.y, "x": self.x, "z": self.z}

    def device(self, axis, r):
        me, dp = lax.axis_index("seq"), lax.axis_index("dp")
        if axis == "y":
            return {"dp": flip(dp, 2 * r)}
        return {"seq": flip(me, self.mask(axis, r))}

    def mask(self, axis, r):
        return {"y": 0, "x": r, "z": r * self.x}[axis]


def row_copies(slots, packed, sem, first):
    rows = slots.shape[0]
    cap = packed.shape[0] // rows
    return [
        pltpu.make_async_copy(
            slots.at[r, pl.ds(0, cap)], packed.at[pl.ds(r * cap, cap)], sem.at[first + r]
        )
        for r in range(rows)
    ]


def put_rows(slots, r, cap, values):
    slots[r, :cap] = values.astype(slots.dtype)
    if cap < slots.shape[1]:
        slots[r, cap:] = jnp.zeros((slots.shape[1] - cap, slots.shape[2]), slots.dtype)


def total_of(first, others, kind):
    total = first.astype(F32)
    for other in others:
        total = total + other.astype(F32)
    return total.astype(kind)


def add_into(total, others):
    inner = total.shape[1]

    def one(k):
        i, j = k // inner, k % inner
        total[i, j] = total_of(total[i, j], [other[i, j] for other in others], total.dtype)

    loop(0, total.shape[0] * inner, one)


class Summed:
    def __init__(self, links, grid, axis, block, got):
        self.links, self.grid, self.axis, self.block, self.got = links, grid, axis, block, got
        self.size = grid.size[axis]
        self.slot = links.reserve(self.size - 1)

    def send(self):
        for r in range(1, self.size):
            slot = self.slot + r - 1
            self.links.start(
                self.block.at[r], self.got.at[r - 1], slot, slot, self.grid.device(self.axis, r)
            )

    def receive(self, store, kind=BF16):
        for r in range(1, self.size):
            self.links.arrived(
                self.got.at[r - 1], self.slot + r - 1, self.grid.device(self.axis, r)
            )
        inner = store.shape[1]

        def one(k):
            i, j = k // inner, k % inner
            others = [self.got[r - 1, i, j] for r in range(1, self.size)]
            store[i, j] = total_of(self.block[0, i, j], others, kind)

        if len(store.shape) == 4:
            loop(0, store.shape[0] * inner, one)
        else:
            store[...] = total_of(self.block[0], [self.got[r - 1] for r in range(1, self.size)], kind)

    def receive_last(self, store):
        for r in range(1, self.size):
            self.links.arrived(
                self.got.at[r - 1], self.slot + r - 1, self.grid.device(self.axis, r)
            )
        store[...] = total_of(self.block[0], [self.got[r - 1] for r in range(1, self.size)], F32)


class LineSum:
    def __init__(self, links, grid, block, right, left):
        self.links, self.grid, self.block = links, grid, block
        self.got = {1: right, -1: left}
        self.size = grid.z
        self.place = lax.axis_index("seq") // grid.x
        self.slot = {1: links.reserve(self.size), -1: links.reserve(self.size)}

    def next(self, way):
        return {"seq": lax.axis_index("seq") + way * self.grid.x}

    def copy(self, way, goal, src):
        slot = self.slot[way] + goal
        return pltpu.make_async_remote_copy(
            src_ref=src,
            dst_ref=self.got[way].at[goal],
            send_sem=self.links.send_sem.at[slot],
            recv_sem=self.links.recv_sem.at[slot],
            device_id=self.next(way),
            device_id_type=pl.DeviceIdType.MESH,
        )

    def source(self, way, goal, first):
        if first:
            return self.block.at[flip(self.place, goal)]
        return self.got[way].at[goal]

    def hop(self, k):
        for way, at in ((1, k), (-1, self.size - 1 - k)):
            goals = range(self.size - 1, at, -1) if way == 1 else range(at)

            @pl.when(self.place == at)
            def _(way=way, goals=goals):
                for goal in goals:
                    if k:
                        self.arrived(way, goal)
                        got = self.got[way]
                        own = self.block.at[flip(self.place, goal)]
                        for i in range(got.shape[1]):
                            got[goal, i] = total_of(own[i], [got[goal, i]], BF16)
                    self.copy(way, goal, self.source(way, goal, k == 0)).start()

    def arrived(self, way, goal):
        self.copy(way, goal, self.got[way].at[goal]).wait_recv()

    def finish(self, store, cols):
        store[:, cols] = self.block[0].astype(F32)
        for way, limit in ((1, self.place > 0), (-1, self.place < self.size - 1)):

            @pl.when(limit)
            def _(way=way):
                self.arrived(way, self.place)
                store[:, cols] = store[:, cols] + self.got[way][self.place].astype(F32)

        for way in (1, -1):
            for goal in range(self.size):

                @pl.when(self.place < goal if way == 1 else self.place > goal)
                def _(way=way, goal=goal):
                    self.copy(way, goal, self.got[way].at[goal]).wait_send()


class SlotSum:
    def __init__(self, links, grid, axis, slots, block, got, inner=False):
        self.links, self.grid, self.axis, self.got = links, grid, axis, got
        self.block = (lambda m, r: block.at[m, :, r]) if inner else (lambda m, r: block.at[m, r])
        self.size, self.slots = grid.size[axis], slots
        self.first = links.reserve(slots * (self.size - 1))

    def id(self, m, r):
        return self.first + m * (self.size - 1) + r - 1

    def send(self, m):
        for r in range(1, self.size):
            there = flip(m, self.grid.mask(self.axis, r), self.slots)
            self.links.start(
                self.block(m, r),
                self.got.at[there, r - 1],
                self.id(m, r),
                self.id(there, r),
                self.grid.device(self.axis, r),
                later=False,
            )

    def receive(self, m):
        for r in range(1, self.size):
            self.links.arrived(
                self.got.at[m, r - 1], self.id(m, r), self.grid.device(self.axis, r)
            )
        return total_of(
            self.block(m, 0)[...], [self.got[m, r - 1] for r in range(1, self.size)], F32
        )

    def drain(self, m):
        for r in range(1, self.size):
            self.links.left(self.block(m, r), self.id(m, r), self.grid.device(self.axis, r))


def split_weight(weight, group):
    width = weight.shape[0]
    wide = width // group
    if wide % 128 == 0:
        return weight
    return weight.reshape(width, 3, group, wide).transpose(1, 2, 0, 3)


def weight_view(weight, part, source, width, wide):
    if wide % 128 == 0:
        return weight.at[:, pl.ds(pl.multiple_of(part * width + source * wide, 128), wide)]
    return weight.at[part, source]


def only_head(block, head, heads):
    if heads == 1:
        return block
    lane = lax.broadcasted_iota(jnp.int32, block.shape, 1)
    return jnp.where(lane // HEAD_DIM == head, block, jnp.zeros_like(block))


def transposed(block):
    return block.astype(F32).T.astype(BF16)


def causal(size, offset):
    key = lax.broadcasted_iota(jnp.int32, (size, TILE), 0)
    query = lax.broadcasted_iota(jnp.int32, (size, TILE), 1)
    return key <= query + offset


def sweep(tiles, low_of, start, step, finish):
    def before(i, whole_blocks):
        low = low_of(i)
        return lax.fori_loop(
            low, whole_blocks, lambda b, c: step(i, b * PAIR, PAIR, None, c), start(i)
        )

    def even(i, half):
        finish(i, step(i, i * TILE, TILE, 0, before(i, half)))

    def odd(i, half):
        finish(i, step(i, half * PAIR, PAIR, TILE, before(i, half)))

    def both(half, _):
        even(2 * half, half)
        odd(2 * half + 1, half)
        return 0

    lax.fori_loop(0, tiles // 2, both, 0)
    if tiles % 2:
        even(tiles - 1, tiles // 2)


def span(at, size):
    return pl.ds(at if isinstance(at, int) else pl.multiple_of(at, TILE), size)


def blank_rest(used, *arrays):
    if used < arrays[0].shape[0]:
        for array in arrays:
            array[used:, :] = jnp.zeros((array.shape[0] - used, array.shape[1]), array.dtype)


def load_heads(me, cap, parts, q_s, k_s, v_s):
    wide = v_s.shape[1]
    blank_rest(parts.shape[0] * cap, q_s, k_s, v_s)
    for m in range(parts.shape[0]):
        here = pl.ds(pl.multiple_of((me ^ m) * cap, math.gcd(cap, 128)), cap)
        q_s[here, :] = parts[m, :, :wide] * SCALE
        k_s[here, :wide] = parts[m, :, wide : 2 * wide]
        v_s[here, :] = parts[m, :, 2 * wide :]


def documents(ids, docs):
    row = lax.broadcasted_iota(jnp.int32, (128, TILE), 0).astype(F32)
    unit = row + 1.0 == ids
    query = jnp.where(unit, 1.0, 0.0).astype(BF16)
    return query, jnp.where(unit | (row >= docs), 0.0, NEG)


def by_head(turned, heads):
    if heads == 1:
        return [turned]
    row = lax.broadcasted_iota(jnp.int32, turned.shape, 0) // HEAD_DIM
    return [jnp.where(row == h, turned, jnp.zeros_like(turned)) for h in range(heads)]


def query_rows(queries, ids, docs, heads):
    unit, _ = documents(ids, docs)
    turned = queries.astype(F32).T
    return tuple(
        jnp.concatenate([part.astype(BF16), unit], axis=0) for part in by_head(turned, heads)
    )


def key_documents(ids_ref, k_s, wide, docs):
    for t in range(ids_ref.shape[0]):
        _, keys = documents(ids_ref[t], docs)
        k_s[t * TILE : (t + 1) * TILE, wide:] = keys.T.astype(BF16)


def attend_row(heads, docs, tiles, ids, lse, q_s, k_s, v_s, vt_s, o_s):
    for t in range(tiles):
        vt_s[:, t * TILE : (t + 1) * TILE] = transposed(v_s[t * TILE : (t + 1) * TILE, :])

    def start(i):
        blank = (
            jnp.full((1, TILE), NEG, F32),
            jnp.zeros((1, TILE), F32),
            jnp.zeros((HEAD_DIM, TILE), F32),
        )
        return query_rows(q_s[span(i * TILE, TILE), :], ids[i], docs, heads), (blank,) * heads

    def step(i, at, size, diagonal, carry):
        queries, states = carry
        there = span(at, size)
        keys = k_s[there, :]
        new = []
        for h in range(heads):
            top, total, acc = states[h]
            s = dot(keys, queries[h])
            if diagonal is not None:
                s = jnp.where(causal(size, diagonal), s, NEG)
            top2 = jnp.maximum(top, jnp.max(s, axis=0, keepdims=True))
            p = jnp.exp(s - top2)
            fade = jnp.exp(top - top2)
            total = total * fade + jnp.sum(p, axis=0, keepdims=True)
            vt = vt_s[h * HEAD_DIM : (h + 1) * HEAD_DIM, there]
            acc = acc * fade + dot(vt, p.astype(BF16))
            new.append((top2, total, acc))
        return queries, tuple(new)

    def finish(i, carry):
        pieces = []
        for h in range(heads):
            top, total, acc = carry[1][h]
            pieces.append(acc * (1.0 / total))
            lse[i, h : h + 1, :] = top + jnp.log(total)
        o_s[span(i * TILE, TILE), :] = jnp.concatenate(pieces, axis=0).T.astype(BF16)

    sweep(tiles, lambda i: 0, start, step, finish)


def first_kernel(wide, docs, *refs):
    x_hbm, g_hbm, gain_ref, shift_ref, weight, bias_ref, dw_hbm, ids_ref = refs[:8]
    normed_ref, heads_hbm, context_hbm, ctx_hbm, lse_ref, slope_hbm = refs[8:14]
    w_s, stage, landed, x_ref, g_ref, dw, slope, q_s, k_s, v_s, vt_s, o_s = refs[14:26]
    send_sem, recv_sem, load_sem = refs[26:]
    group = lax.axis_size("seq")
    me = lax.axis_index("seq")
    width = x_ref.shape[1]
    rows, tiles = ids_ref.shape[0], ids_ref.shape[1]
    cap = x_ref.shape[0] // rows
    heads = wide // HEAD_DIM
    hidden = dw.shape[0]
    links = Links(send_sem, recv_sem)
    first, second = links.reserve(rows * group), links.reserve(rows * group)
    order = list(range(group - 1, 0, -1)) + [0]
    used = [0]

    def local(src, dst):
        copy = pltpu.make_async_copy(src, dst, load_sem.at[used[0]])
        used[0] += 1
        copy.start()
        return copy

    held_x = [local(x_hbm.at[r, pl.ds(0, cap)], x_ref.at[pl.ds(r * cap, cap)]) for r in range(rows)]
    held_w = {}
    for m in order:
        source = flip(me, m)
        held_w[m] = [
            local(weight_view(weight, part, source, width, wide), w_s.at[m, part])
            for part in range(3)
        ]
    held_g = [local(g_hbm.at[r, pl.ds(0, cap)], g_ref.at[pl.ds(r * cap, cap)]) for r in range(rows)]
    held_g.append(local(dw_hbm, dw))
    for copy in held_x:
        copy.wait()
    n, _ = centre_rows(x_ref[...].astype(F32))
    normed_ref[...] = (n * gain_ref[...] + shift_ref[...]).astype(BF16)
    greet(range(1, group), [])

    for r in range(rows):
        here = slice(r * cap, (r + 1) * cap)
        for m in order:
            if r == 0:
                for copy in held_w[m]:
                    copy.wait()
            joined = jnp.concatenate([w_s[m, part] for part in range(3)], axis=1)
            value = (dot(normed_ref[here, :], joined) + bias_ref[flip(me, m)]).astype(BF16)
            if m:
                stage[m, here, :] = value
                links.start(
                    stage.at[m, here],
                    landed.at[m, here],
                    first + r * group + m,
                    first + r * group + m,
                    {"seq": flip(me, m)},
                )
            else:
                landed[0, here, :] = value

    for copy in held_g:
        copy.wait()
    block = min(512, hidden)

    def before(f):
        at = pl.ds(pl.multiple_of(f * block, block), block)
        slope[:, at] = dot(g_ref[...], dw[at, :], NT).astype(BF16)

    loop(0, hidden // block, before)
    leaving = [local(slope, slope_hbm)]
    blank_rest(group * cap, q_s, k_s, v_s)
    for r in range(rows):
        here = slice(r * cap, (r + 1) * cap)
        for m in range(1, group):
            links.arrived(landed.at[m, here], first + r * group + m, {"seq": flip(me, m)})
        for m in range(group):
            there = pl.ds(pl.multiple_of(flip(me, m) * cap, math.gcd(cap, 128)), cap)
            q_s[there, :] = landed[m, here, :wide] * SCALE
            k_s[there, :wide] = landed[m, here, wide : 2 * wide]
            v_s[there, :] = landed[m, here, 2 * wide :]
        key_documents(ids_ref.at[r], k_s, wide, docs)
        attend_row(heads, docs, tiles, ids_ref.at[r], lse_ref.at[r], q_s, k_s, v_s, vt_s, o_s.at[r])
        for m in order:
            src = o_s.at[r, pl.ds(pl.multiple_of(flip(me, m) * cap, math.gcd(cap, 128)), cap)]
            if m:
                links.start(
                    src,
                    ctx_hbm.at[m, here],
                    second + r * group + m,
                    second + r * group + m,
                    {"seq": flip(me, m)},
                )
            else:
                leaving.append(local(src, ctx_hbm.at[0, here]))
        leaving.append(local(o_s.at[r], context_hbm.at[r]))
    leaving.append(local(landed, heads_hbm))
    for r in range(rows):
        here = slice(r * cap, (r + 1) * cap)
        for m in range(1, group):
            links.arrived(ctx_hbm.at[m, here], second + r * group + m, {"seq": flip(me, m)})
    links.drain()
    for copy in leaving:
        copy.wait()


def project_attend(branch, cap, docs, x, g, gain, shift, weight, bias_parts, dw, ids):
    slots, width = x.shape[0], x.shape[2]
    rows = slots * cap
    group = bias_parts.shape[0]
    wide = width // group
    cols = 3 * wide
    tiles = ids.shape[1]
    length = tiles * TILE
    heads = wide // HEAD_DIM
    hidden = dw.shape[0]
    here = any_spec()
    anywhere = pl.BlockSpec(memory_space=pl.ANY)
    shape = jax.ShapeDtypeStruct
    vmem = lambda dims, kind=BF16: pltpu.VMEM(dims, kind)
    pair = slots * heads * length * length // 2
    return pl.pallas_call(
        functools.partial(first_kernel, wide, docs),
        in_specs=[anywhere, anywhere, here, here, anywhere, here, anywhere, here],
        out_specs=[here, anywhere, anywhere, anywhere, here, anywhere],
        out_shape=[
            shape((rows, width), BF16),
            shape((group, rows, cols), BF16),
            shape((slots, length, wide), BF16),
            shape((group, rows, wide), BF16),
            shape((slots, tiles, heads, TILE), F32),
            shape((rows, hidden), BF16),
        ],
        scratch_shapes=[
            vmem((group, 3, width, wide)),
            vmem((group, rows, cols)),
            vmem((group, rows, cols)),
            vmem((rows, width)),
            vmem((rows, width)),
            vmem((hidden, width)),
            vmem((rows, hidden)),
            vmem((length, wide)),
            vmem((length, wide + 128)),
            vmem((length, wide)),
            vmem((wide, length)),
            vmem((slots, length, wide)),
            pltpu.SemaphoreType.DMA((2 * slots * group,)),
            pltpu.SemaphoreType.DMA((2 * slots * group,)),
            pltpu.SemaphoreType.DMA((4 * slots + 3 * group + 3,)),
        ],
        compiler_params=params(collective_id=3 * branch + 1, has_side_effects=True),
        cost_estimate=pl.CostEstimate(
            flops=2 * rows * width * (cols * group + hidden) + 4 * 256 * pair,
            bytes_accessed=2 * group * cols * (width + rows) + 2 * hidden * width,
            transcendentals=pair,
        ),
        name="project_attend",
    )(x, g, gain[None], shift[None], weight, bias_parts, dw, ids)


def attend_back_kernel(group, cap, tiles, heads, docs, sc_ref, *refs):
    parts, ctx, grads, ids_ref, lse_ref, out_ref = refs[:6]
    refs = refs[6:]
    q_s, k_s, v_s, kt_s, g_s, dq_s, dk_s, dv_s = refs
    wide = heads * HEAD_DIM
    me = sc_ref[0]
    row = pl.program_id(0)
    load_heads(me, cap, parts, q_s, k_s, v_s)
    key_documents(ids_ref.at[0], k_s, wide, docs)
    blank_rest(group * cap, g_s)
    for m in range(group):
        here = pl.ds(pl.multiple_of((me ^ m) * cap, math.gcd(cap, 128)), cap)
        g_s[here, :] = grads[m]
    for t in range(tiles):
        kt_s[:, t * TILE : (t + 1) * TILE] = transposed(k_s[t * TILE : (t + 1) * TILE, :wide])
    dk_s[...] = jnp.zeros_like(dk_s)
    dv_s[...] = jnp.zeros_like(dv_s)

    def start(i):
        at = span(i * TILE, TILE)
        queries = q_s[at, :]
        grad = g_s[at, :]
        product = (grad.astype(F32) * ctx[0, at, :].astype(F32)).T
        delta = tuple(
            jnp.sum(product[h * HEAD_DIM : (h + 1) * HEAD_DIM], axis=0, keepdims=True)
            for h in range(heads)
        )
        split_q = tuple(only_head(queries, h, heads) for h in range(heads))
        split_g = tuple(only_head(grad, h, heads) for h in range(heads))
        turned_q = query_rows(queries, ids_ref[0, i], docs, heads)
        turned_g = tuple(part.astype(BF16) for part in by_head(grad.astype(F32).T, heads))
        fixed = (split_q, split_g, turned_q, turned_g, delta)
        return fixed, tuple(jnp.zeros((HEAD_DIM, TILE), F32) for _ in range(heads))

    def step(i, at, size, diagonal, carry):
        fixed, sums = carry
        split_q, split_g, turned_q, turned_g, delta = fixed
        there = span(at, size)
        keys = k_s[there, :]
        values = v_s[there, :]
        new, ps, dss = [], [], []
        for h in range(heads):
            s = dot(keys, turned_q[h]) - lse_ref[0, i, h : h + 1, :]
            if diagonal is not None:
                s = jnp.where(causal(size, diagonal), s, NEG)
            p = jnp.exp(s)
            dp = dot(values, turned_g[h])
            ds = (p * (dp - delta[h])).astype(BF16)
            ps.append(p.astype(BF16))
            dss.append(ds)
            kt = kt_s[h * HEAD_DIM : (h + 1) * HEAD_DIM, there]
            new.append(sums[h] + dot(kt, ds))
        dv = dot(ps[0], split_g[0])
        dk = dot(dss[0], split_q[0])
        for h in range(1, heads):
            dv = dv + dot(ps[h], split_g[h])
            dk = dk + dot(dss[h], split_q[h])
        dv_s[there, :] += dv
        dk_s[there, :] += dk
        return fixed, tuple(new)

    def finish(i, carry):
        dq_s[span(i * TILE, TILE), :] = (jnp.concatenate(carry[1], axis=0).T * SCALE).astype(BF16)

    sweep(tiles, lambda i: sc_ref[1 + row * tiles + i], start, step, finish)
    for m in range(group):
        here = pl.ds(pl.multiple_of((me ^ m) * cap, math.gcd(cap, 128)), cap)
        out_ref[m, :, :wide] = dq_s[here, :]
        out_ref[m, :, wide : 2 * wide] = dk_s[here, :].astype(BF16)
        out_ref[m, :, 2 * wide :] = dv_s[here, :].astype(BF16)


def attend_back(scalars, parts, ctx, grads, ids, lse, docs, cap, heads):
    group, tokens, cols = parts.shape
    rows = tokens // cap
    tiles = pl.cdiv(group * cap, TILE)
    length = tiles * TILE
    wide = heads * HEAD_DIM
    deep = wide + 128
    pair = rows * heads * length * length // 2
    by_row = lambda r, sc: (0, r, 0)
    all_row = lambda r, sc: (r, 0, 0, 0)
    return pl.pallas_call(
        functools.partial(attend_back_kernel, group, cap, tiles, heads, docs),
        grid_spec=pltpu.PrefetchScalarGridSpec(
            num_scalar_prefetch=1,
            grid=(rows,),
            in_specs=[pl.BlockSpec((group, cap, cols), by_row)]
            + [pl.BlockSpec((1, length, wide), lambda r, sc: (r, 0, 0))]
            + [pl.BlockSpec((group, cap, wide), by_row)]
            + [pl.BlockSpec((1, tiles, 1, TILE), all_row)]
            + [pl.BlockSpec((1, tiles, heads, TILE), lambda r, sc: (r, 0, 0, 0))],
            out_specs=pl.BlockSpec((group, cap, cols), by_row),
            scratch_shapes=[
                pltpu.VMEM((length, wide), BF16),
                pltpu.VMEM((length, deep), BF16),
                pltpu.VMEM((length, wide), BF16),
                pltpu.VMEM((wide, length), BF16),
            ]
            + [pltpu.VMEM((length, wide), BF16)] * 2
            + [pltpu.VMEM((length, wide), F32)] * 2,
        ),
        out_shape=jax.ShapeDtypeStruct((group, rows * cap, cols), BF16),
        compiler_params=params(),
        cost_estimate=pl.CostEstimate(
            flops=10 * 256 * pair, bytes_accessed=20 * rows * length * wide, transcendentals=pair
        ),
        name="attend_back",
    )(scalars, parts, ctx, grads, ids, lse)


def norm_back(upper, n, rs, gain):
    e = upper * gain
    return rs * (
        e - jnp.mean(e, axis=-1, keepdims=True) - n * jnp.mean(e * n, axis=-1, keepdims=True)
    )


GELU_A = 0.7978845608028654
GELU_B = 0.044715


VECTORS = 10


def early_cols(cols, late):
    early = cols * 3 // 4
    return cols - early if late else early


def mid_kernel(wide, *refs):
    grid = Grid()
    group, ys, xs, zs = grid.seq, grid.y, grid.x, grid.z
    refs = list(refs)

    def take(n):
        out = refs[:n]
        del refs[:n]
        return out

    ctx_hbm, x_hbm, g_hbm, slope_hbm, ow_hbm, uw_hbm, dw_hbm, ob, gain, shift, ub, db = take(12)
    grads, result_ref, mg_ref, early = take(4)
    down_out, up_out, out_out = take(2 * ys), take(xs + ys), take(zs)
    gots = take(3)
    x_ref, g_ref, landed, ctx, ow, uw, dw, hid, rise, mid_s, n2_s, normed, attn, chunk = take(14)
    rings, loaded, lefts = take(3), take(3), take(6)
    send_sem, recv_sem, load_sem, ring_sem, got_sem = take(5)

    me, dp = lax.axis_index("seq"), lax.axis_index("dp")
    core, row = dp % 2, dp // 2
    links = Links(send_sem, recv_sem)
    tokens, width = x_ref.shape
    hidden = hid.shape[1]
    block = min(512, hidden)
    partner_core = {"dp": flip(dp, 1)}
    loads = [
        pltpu.make_async_copy(src, dst, load_sem.at[k])
        for k, (src, dst) in enumerate(
            ((ow_hbm, ow), (ctx_hbm, landed), (uw_hbm, uw), (slope_hbm, rise), (dw_hbm, dw))
        )
    ]
    held = row_copies(g_hbm, g_ref, load_sem, 5) + row_copies(x_hbm, x_ref, load_sem, 5 + x_hbm.shape[0])
    for copy in loads[:2] + held + loads[2:]:
        copy.start()
    greet(range(1, group), [1])
    for copy in held + loads[:2]:
        copy.wait()
    early[...] = jnp.zeros_like(early)
    early[5:6, :] = jnp.sum(g_ref[...].astype(F32), axis=0, keepdims=True)

    def lanes(f, size):
        return pl.ds(pl.multiple_of(f * size, size), size)

    for s in range(group):
        chunk[s] = landed[flip(me, s)]
    for s in range(group):
        ctx[:, s * wide : (s + 1) * wide] = chunk[s]
    mid = x_ref[...].astype(F32) + dot(ctx[...], ow[...]) + ob[...]
    mid_s[...] = mid
    n, _ = centre_rows(mid)
    normed[...] = (n * gain[...] + shift[...]).astype(BF16)
    n2_s[...] = jnp.zeros_like(n2_s)
    for copy in loads[2:4]:
        copy.wait()

    def through(f, _):
        here = lanes(f, block)
        u = dot(normed[...], uw[:, here]) + ub[:, here]
        square = u * u
        t = jnp.tanh(GELU_A * u * (1.0 + GELU_B * square))
        half = 0.5 * (1.0 + t)
        hid[:, here] = (u * half).astype(BF16)
        slope = half + 0.5 * GELU_A * u * (1.0 - t * t) * (1.0 + 3.0 * GELU_B * square)
        up = (rise[:, here].astype(F32) * slope).astype(BF16)
        rise[:, here] = up
        n2_s[...] += dot(up, uw[:, here], NT)
        return 0

    def ordered(ring, spot, total, parts, share, got):
        for s in range(parts):
            rel = flip(me % parts, s)
            piece = total[s * share : (s + 1) * share]
            if got is not None:
                piece = piece + got[rel % xs, rel // xs].astype(F32)
            ring[spot, rel % xs, rel // xs] = piece.astype(BF16)

    def outputs(item, o, z, cols, ring):
        if item == 0:
            first = down_out[0].shape[-1]
            for h, here in enumerate((slice(0, first), slice(first, width))):
                yield ring.at[:, :, :, here], down_out[2 * o + h].at[:, z]
        elif item == 1:
            first = up_out[0].shape[-1]
            if cols.start >= first:
                here = slice(cols.start - first, cols.stop - first)
                yield ring, up_out[xs + o].at[:, :, :, here]
            else:
                for x in range(xs):
                    yield ring.at[x], up_out[x].at[o, :, :, cols]
        else:
            for z in range(zs):
                yield ring.at[:, z], out_out[z].at[o]

    def weight_grad(item, a, b):
        share = a.shape[1] // (2 * ys * group)
        parts = min(group, max(256 // share, xs))
        sub = group // parts
        depth = parts // xs
        cols = b.shape[1]
        piece = min(1024, cols)
        pieces = cols // piece
        count = ys * sub * pieces
        ring, got, left_s = rings[item], loaded[item], lefts[2 * item : 2 * item + 2]
        spots = ring.shape[0] // 2
        slot = links.reserve(count)

        def unit(n):
            u = n // pieces
            return ys - 1 - u // sub, u % sub, n % pieces

        def start_of(c, n):
            o, k, _ = unit(n)
            at = (flip(row, o, ys) * 2 + flip(core, c, 2)) * group * share
            return at + flip(me // parts, k, sub) * parts * share

        def product(c, n):
            o, k, p = unit(n)
            left = left_s[c]

            @pl.when(p == 0)
            def _():
                at = pl.multiple_of(start_of(c, n), 128)
                left[...] = transposed(a[:, pl.ds(at, parts * share)])

            return dot(left[...], b[:, pl.ds(pl.multiple_of(p * piece, piece), piece)])

        def place(n):
            o, k, p = unit(n)
            columns = pl.ds(pl.multiple_of(p * piece, piece), piece)
            return (o, slice(None), pl.ds(k * depth, depth), slice(None), columns)

        def away(n):
            links.left(ring.at[n % spots], slot + n, partner_core)

        def send(n):
            @pl.when(n >= spots)
            def _():
                away(n - spots)

            ordered(ring, n % spots, product(1, n), parts, share, None)
            there = gots[item].at[place(n)]
            links.start(ring.at[n % spots], there, slot + n, slot + n, partner_core, later=False)

        def fetch(n):
            src = gots[item].at[place(n)]
            return pltpu.make_async_copy(src, got.at[n % 2], got_sem.at[2 * item + n % 2])

        def fetch_start(n):
            links.arrived(gots[item].at[place(n)], slot + n, partner_core)
            fetch(n).start()

        def written(n, act):
            for fixed in range(ys):
                for p in range(pieces):
                    o, k, q = unit(n)

                    @pl.when((o == fixed) & (q == p))
                    def _(fixed=fixed, p=p):
                        spot = spots + n % spots
                        z = pl.ds(k * depth, depth)
                        here = slice(p * piece, (p + 1) * piece)
                        copies = outputs(item, fixed, z, here, ring.at[spot])
                        for h, (src, dst) in enumerate(copies):
                            at = (item * spots + n % spots) * max(2, xs, zs) + h
                            act(pltpu.make_async_copy(src, dst, ring_sem.at[at]))

        def keep(n):
            @pl.when(n + 1 < count)
            def _():
                fetch_start(n + 1)

            @pl.when(n >= spots)
            def _():
                written(n - spots, lambda copy: copy.wait())

            total = product(0, n)
            fetch(n).wait()
            ordered(ring, spots + n % spots, total, parts, share, got.at[n % 2])
            written(n, lambda copy: copy.start())

        def rest(act):
            for n in range(max(0, count - spots), count):
                act(n)

        def finish():
            rest(lambda n: written(n, lambda copy: copy.wait()))

        return count, send, lambda: rest(away), fetch_start, keep, finish, start_of

    first_job = weight_grad(0, hid, g_ref)
    steps = hidden // block
    per = first_job[0] * 2 // steps

    def mine(i):
        c = 1 - 2 * i // steps
        f = first_job[6](c, (i % (steps // 2)) * per) // block
        through(f, 0)

        @pl.when(c == 1)
        def _():
            for k in range(per):
                first_job[1](i * per + k)

    loop(0, steps, mine)
    first_job[2]()
    n, rs = centre_rows(mid_s[...])
    n2 = n2_s[...]
    early[3:4, :] = jnp.sum(n2 * n, axis=0, keepdims=True)
    early[4:5, :] = jnp.sum(n2, axis=0, keepdims=True)
    mid_grad = g_ref[...].astype(F32) + norm_back(n2, n, rs, gain[...])
    mg_ref[...] = mid_grad
    attn[...] = mid_grad.astype(BF16)
    full = dot(attn[...], ow[...], NT).astype(BF16)
    for s in range(group):
        chunk[flip(me, s)] = full[:, s * wide : (s + 1) * wide]
    second = links.reserve(group)
    for m in range(group - 1, 0, -1):
        links.start(chunk.at[m], grads.at[m], second + m, second + m, {"seq": flip(me, m)})
    own = pltpu.make_async_copy(chunk.at[0], grads.at[0], load_sem.at[0])
    own.start()

    jobs = [first_job, weight_grad(1, normed, rise), weight_grad(2, ctx, attn)]
    for stage in range(1, len(jobs) + 1):
        new = jobs[stage] if stage < len(jobs) else None
        old = jobs[stage - 1]
        old[3](0)

        def turn(n, new=new, old=old):
            for job, act in ((new, 1), (old, 4)):
                if job:
                    if new and old and job[0] < max(new[0], old[0]):
                        pl.when(n < job[0])(lambda job=job, act=act: job[act](n))
                    else:
                        job[act](n)

        loop(0, max(job[0] for job in (new, old) if job), turn)
        if new:
            new[2]()
        old[5]()


    loads[4].wait()

    def finished(k):
        here = lanes(k, 256)
        mid_s[:, here] = mid_s[:, here] + (dot(hid[...], dw[:, here]) + db[:, here])

    loop(0, width // 256, finished)
    cap = tokens // result_ref.shape[0]
    for r in range(result_ref.shape[0]):
        put_rows(result_ref, r, cap, mid_s[r * cap : (r + 1) * cap, :])
    early[2:3, :] = jnp.sum(attn[...].astype(F32), axis=0, keepdims=True)
    for k in range(hidden // width):
        part = rise[:, k * width : (k + 1) * width].astype(F32)
        early[6 + k : 7 + k, :] = jnp.sum(part, axis=0, keepdims=True)
    for m in range(1, group):
        links.arrived(grads.at[m], second + m, {"seq": flip(me, m)})
    own.wait()
    links.drain()


def feed_forward(branch, cap, ctx, x, g, slope, ow, ob, gain, shift, uw, ub, dw, db):
    grid = Grid()
    group, ys, xs, zs = grid.seq, grid.y, grid.x, grid.z
    rows, width = x.shape[0] * cap, x.shape[2]
    wide = width // group
    hidden = uw.shape[1]
    here = any_spec()
    anywhere = pl.BlockSpec(memory_space=pl.ANY)
    shape = jax.ShapeDtypeStruct
    low, high = width // (grid.dp * group), hidden // (grid.dp * group)
    vectors = VECTORS + group
    vectors += -vectors % 8
    sums = [
        shape((ys, xs, zs, high, width), BF16),
        shape((ys, xs, zs, low, hidden), BF16),
        shape((ys, xs, zs, low, width), BF16),
    ]
    parts = lambda share: min(group, max(256 // share, xs))
    block = lambda share: (xs, parts(share) // xs, share, width)
    rings = [pltpu.VMEM((n,) + block(share), BF16) for n in (4, 2) for share in (high, low, low)]
    turned = [pltpu.VMEM((parts(s) * s, rows), BF16) for s in (high, low, low) for _ in range(2)]
    blocks = ys * (group // parts(high)) + ys * (hidden // width) + ys
    vmem = lambda dims, kind=BF16: pltpu.VMEM(dims, kind)
    return pl.pallas_call(
        functools.partial(mid_kernel, wide),
        in_specs=[anywhere] * 7 + [here] * 5,
        out_specs=[anywhere, here, here, here] + [anywhere] * (3 * ys + xs + zs + 3),
        out_shape=[
            shape((group, rows, wide), BF16),
            shape(x.shape, BF16),
            shape((rows, width), F32),
            shape((vectors, width), F32),
        ]
        + [shape((xs, zs, high, early_cols(width, k)), BF16) for _ in range(ys) for k in range(2)]
        + [shape((ys, zs, low, early_cols(hidden, 0)), BF16)] * xs
        + [shape((xs, zs, low, early_cols(hidden, 1)), BF16)] * ys
        + [shape((ys, xs, low, width), BF16)] * zs
        + sums,
        scratch_shapes=[
            vmem((rows, width)),
            vmem((rows, width)),
            vmem((group, rows, wide)),
            vmem((rows, width)),
            vmem((width, width)),
            vmem((width, hidden)),
            vmem((hidden, width)),
            vmem((rows, hidden)),
            vmem((rows, hidden)),
            vmem((rows, width), F32),
            vmem((rows, width), F32),
            vmem((rows, width)),
            vmem((rows, width)),
            vmem((group, rows, wide)),
        ]
        + rings
        + turned
        + [
            pltpu.SemaphoreType.DMA((2 * group + blocks,)),
            pltpu.SemaphoreType.DMA((2 * group + blocks,)),
            pltpu.SemaphoreType.DMA((5 + 2 * x.shape[0],)),
            pltpu.SemaphoreType.DMA((6 * max(2, xs, zs),)),
            pltpu.SemaphoreType.DMA((6,)),
        ],
        compiler_params=params(collective_id=3 * branch + 2, has_side_effects=True),
        cost_estimate=pl.CostEstimate(
            flops=8 * rows * width * width + 12 * rows * width * hidden,
            bytes_accessed=4 * width * width + 8 * width * hidden,
            transcendentals=rows * hidden,
        ),
        name="feed_forward",
    )(ctx, x, g, slope, ow, uw, dw, ob[None], gain[None], shift[None], ub[None], db[None])


def partner(axis, mask):
    return [(i, i ^ mask) for i in range(lax.axis_size(axis))]


def exchange(axis, blocks):
    grid = Grid()
    out = [blocks[0]]
    for r in range(1, grid.size[axis]):
        name, mask = ("dp", 2 * r) if axis == "y" else ("seq", grid.mask(axis, r))
        out.append(lax.ppermute(blocks[r], name, partner(name, mask)))
    return out


def item_counts(ys, xs, zs):
    return (ys - 1) + 5, (xs - 1) + 5, 7, 7, (zs - 1) + 4


def tail_kernel(wide, *refs):
    grid = Grid()
    group, ys, xs, zs = grid.seq, grid.y, grid.x, grid.z
    refs = list(refs)

    def take(n):
        out = refs[:n]
        del refs[:n]
        return out

    back, weight, normed_ref, x_hbm, mg_hbm, gain_ref, early_ref = take(7)
    down_in, down_rest = take(ys), take(ys)
    up_in, up_rest = take(xs), take(ys)
    out_in = take(zs)
    tg_ref, project_ref, down_ref, up_ref, out_ref, vec_ref = take(6)
    landed, w_s, x_s, mg_s, acc, turned, order = take(7)
    send_a, send_b, keep_a, keep_b, pair_a, pair_b = take(6)
    got_a1, got_b1, mid_a, mid_b, got_a2, got_b2, z_a, z_b, got_za, got_zb = take(10)
    items = [take(count) for count in item_counts(ys, xs, zs)]
    vec_s, vec_g = take(2)
    send_sem, recv_sem, load_sem = take(3)

    me, dp = lax.axis_index("seq"), lax.axis_index("dp")
    core, row = dp % 2, dp // 2
    links = Links(send_sem, recv_sem)
    tokens, width = normed_ref.shape
    share = project_ref.shape[1]
    partner_core = {"dp": flip(dp, 1)}
    loads = []

    def load(src, dst):
        copy = pltpu.make_async_copy(src, dst, load_sem.at[len(loads)])
        copy.start()
        loads.append(copy)
        return copy

    greet(range(1, group), [1] + [2 * r for r in range(1, ys)])

    first = links.reserve(group)
    for m in range(1, group):
        links.start(back.at[m], landed.at[m], first + m, first + m, {"seq": flip(me, m)})
    own = load(back.at[0], landed.at[0])
    down_a, up_a, down_b, up_b, out_a = items
    loaded = [
        [load(src, dst) for src, dst in zip(up_in, [up_a[xs - 1]] + up_a[: xs - 1])],
        [load(src, dst) for src, dst in zip(down_in, [down_a[ys - 1]] + down_a[: ys - 1])],
        [load(src, dst) for src, dst in zip(out_in, [out_a[zs - 1]] + out_a[: zs - 1])],
        [load(src, down_b[0].at[o]) for o, src in enumerate(down_rest)],
        [load(src, up_b[0].at[o]) for o, src in enumerate(up_rest)],
    ]

    cap = tokens // x_hbm.shape[0]
    own_x = [load(x_hbm.at[r, pl.ds(0, cap)], x_s.at[pl.ds(r * cap, cap)]) for r in range(x_hbm.shape[0])]
    own_mg = load(mg_hbm, mg_s)
    ahead = w_s.shape[0]
    weight_first = len(loads)

    def weight_copies(m):
        source = flip(me, m, group)
        return [
            pltpu.make_async_copy(
                weight_view(weight, part, source, width, wide),
                w_s.at[m % ahead, part],
                load_sem.at[weight_first + 3 * m + part],
            )
            for part in range(3)
        ]

    for m in range(ahead):
        for copy in weight_copies(m):
            copy.start()

    def summed(axis, block, got):
        return Summed(links, grid, axis, block, got)

    up_a1 = summed("y", up_a[xs - 1], up_a[xs])
    up_a2 = LineSum(links, grid, *up_a[xs + 1 :])
    down_a1 = summed("x", down_a[ys - 1], down_a[ys])
    down_a2 = LineSum(links, grid, *down_a[ys + 1 :])
    down_b1, down_b2 = summed("y", down_b[0], down_b[1]), summed("x", down_b[2], down_b[3])
    down_b3 = LineSum(links, grid, *down_b[4:])
    up_b1, up_b2 = summed("y", up_b[0], up_b[1]), summed("x", up_b[2], up_b[3])
    up_b3 = LineSum(links, grid, *up_b[4:])
    out_1 = summed("y", out_a[zs - 1], out_a[zs])
    out_2 = summed("x", out_a[zs + 1], out_a[zs + 2])
    lines = (up_a2, down_a2, up_b3, down_b3)
    for copies in loaded[3:]:
        for copy in copies:
            copy.wait()
    down_b1.send()
    up_b1.send()
    for copies, item, count, stage in (
        (loaded[0], up_a, xs, up_a1),
        (loaded[1], down_a, ys, down_a1),
        (loaded[2], out_a, zs, out_1),
    ):
        for copy in copies:
            copy.wait()
        add_into(item[count - 1], item[: count - 1])
        stage.send()

    for k in range(0, width, 256):
        turned[k : k + 256, :] = normed_ref[:, k : k + 256].astype(F32).T
    for c in range(2):
        for o in range(ys):

            def place(s, c=c, o=o):
                there = (flip(row, o) * 2 + flip(core, c)) * group + flip(me, s, group)
                rows = turned[pl.ds(pl.multiple_of(there * share, share), share), :]
                order[c, o, s % xs, s // xs] = rows.astype(BF16)

            loop(0, group, place)
    half = ys * group * share
    acc[...] = jnp.zeros_like(acc)
    vec_s[0] = early_ref[...]
    own.wait()

    pair_first = links.reserve(2 * group)
    a1 = SlotSum(links, grid, "y", group, keep_a, got_a1)
    a2 = SlotSum(links, grid, "x", group, mid_a, got_a2)
    b1 = SlotSum(links, grid, "x", group, keep_b, got_b1, inner=True)
    b2 = SlotSum(links, grid, "y", group, mid_b, got_b2)
    cut = 2 * wide

    def multiply(m):
        source = flip(me, m, group)

        @pl.when(m > 0)
        def _():
            links.arrived(landed.at[m], first + m, {"seq": source})

        for k, (send, keep, pair, cols) in enumerate(
            (
                (send_a, keep_a, pair_a, slice(0, cut)),
                (send_b, keep_b, pair_b, slice(cut, 3 * wide)),
            )
        ):
            grad = landed[m, :, cols]
            left = order[1].reshape(half, tokens)
            send[m] = dot(left, grad).reshape(send.shape[1:]).astype(BF16)
            slot = pair_first + 2 * m + k
            links.start(send.at[m], pair.at[m], slot, slot, partner_core, later=False)
            left = order[0].reshape(half, tokens)
            keep[m] = dot(left, grad).reshape(keep.shape[1:]).astype(BF16)
        block = landed[m]
        for copy in weight_copies(m):
            copy.wait()
        pieces = [w_s[m % ahead, part] for part in range(3)]
        acc[...] += dot(block, jnp.concatenate(pieces, axis=1), NT)

        @pl.when(m + ahead < group)
        def _():
            for copy in weight_copies(m + ahead):
                copy.start()

        sums = jnp.sum(block.astype(F32), axis=0, keepdims=True)
        vec_s[0, pl.ds(VECTORS + source, 1), : 3 * wide] = sums

    def paired(m):
        for k, (keep, pair, nxt) in enumerate(((keep_a, pair_a, a1), (keep_b, pair_b, b1))):
            links.arrived(pair.at[m], pair_first + 2 * m + k, partner_core)
            keep[m] = total_of(keep[m], [pair[m]], BF16)
            nxt.send(m)

    def second(m):
        mid_a[m] = a1.receive(m).astype(BF16)
        a2.send(m)
        mid_b[m] = b1.receive(m).astype(BF16)
        b2.send(m)

    def third(m):
        for block, stage in ((z_a, a2), (z_b, b2)):
            total = stage.receive(m).astype(BF16)
            for z in range(zs):
                block[z, m] = total[z]

    def input_grads():
        for copy in own_x:
            copy.wait()
        own_mg.wait()
        n, rs = centre_rows(x_s[...].astype(F32))
        n1 = acc[...]
        grad = mg_s[...] + norm_back(n1, n, rs, gain_ref[...])
        for r in range(tg_ref.shape[0]):
            put_rows(tg_ref, r, cap, grad[r * cap : (r + 1) * cap])
        vec_s[0, 0:1, :] = jnp.sum(n1 * n, axis=0, keepdims=True)
        vec_s[0, 1:2, :] = jnp.sum(n1, axis=0, keepdims=True)

    vec_first = links.reserve(1 + (ys - 1) + (xs - 1) + (zs - 1))
    hops = [[partner_core]]
    for axis in ("y", "x", "z"):
        hops.append([grid.device(axis, r) for r in range(1, grid.size[axis])])

    def vec_send(k):
        at = vec_first + sum(len(h) for h in hops[:k])
        for r, device in enumerate(hops[k]):
            links.start(vec_s.at[k], vec_g.at[at + r - vec_first], at + r, at + r, device)

    def vec_receive(k):
        at = vec_first + sum(len(h) for h in hops[:k])
        got = []
        for r, device in enumerate(hops[k]):
            links.arrived(vec_g.at[at + r - vec_first], at + r, device)
            got.append(vec_g[at + r - vec_first])
        total = total_of(vec_s[k], got, F32)
        if k + 1 < len(hops):
            vec_s[k + 1] = total
            vec_send(k + 1)
        else:
            vec_ref[...] = total

    def multiply_next(m):
        multiply(m)

        @pl.when(m > 0)
        def _():
            paired(m - 1)

    loop(0, group // 2 + 1, multiply_next)
    down_b1.receive(down_b[2])
    down_b2.send()
    loop(group // 2 + 1, group, multiply_next)
    paired(group - 1)
    down_a1.receive(down_a[ys + 1])
    down_a2.hop(0)
    up_b1.receive(up_b[2])
    up_b2.send()
    up_a1.receive(up_a[xs + 1])
    up_a2.hop(0)
    input_grads()
    vec_send(0)
    out_1.receive(out_a[zs + 1])
    out_2.send()
    down_b2.receive(down_b[4])
    down_b3.hop(0)
    for k in range(1, zs - 1):
        down_a2.hop(k)
        up_a2.hop(k)
    vec_receive(0)
    loop(0, group // 2, second)
    for k in range(1, zs - 1):
        down_b3.hop(k)
    loop(group // 2, group, second)
    vec_receive(1)
    up_b2.receive(up_b[4])
    up_b3.hop(0)
    loop(0, group // 2, third)
    for k in range(1, zs - 1):
        up_b3.hop(k)
    loop(group // 2, group, third)

    z_first = links.reserve(2 * (zs - 1))
    for r in range(1, zs):
        for k, (block, got) in enumerate(((z_a, got_za), (z_b, got_zb))):
            slot = z_first + 2 * (r - 1) + k
            links.start(block.at[r], got.at[r - 1], slot, slot, grid.device("z", r))
    vec_receive(2)
    cut_down, cut_up = early_cols(down_ref.shape[1], 0), early_cols(up_ref.shape[1], 0)
    out_2.receive_last(out_ref)
    up_a2.finish(up_ref, slice(0, cut_up))
    down_a2.finish(down_ref, slice(0, cut_down))
    up_b3.finish(up_ref, slice(cut_up, up_ref.shape[1]))
    down_b3.finish(down_ref, slice(cut_down, down_ref.shape[1]))
    vec_receive(3)
    for r in range(1, zs):
        for k, got in enumerate((got_za, got_zb)):
            links.arrived(got.at[r - 1], z_first + 2 * (r - 1) + k, grid.device("z", r))

    def share_of(m):
        source = flip(me, m, group)
        for block, got, cols in (
            (z_a, got_za, slice(0, cut)),
            (z_b, got_zb, slice(cut, 3 * wide)),
        ):
            others = [got[r - 1, flip(m, grid.mask("z", r), group)] for r in range(1, zs)]
            project_ref[source, :, cols] = total_of(block[0, m], others, F32)

    loop(0, group, share_of)

    def drain(m):
        for k, send in enumerate((send_a, send_b)):
            links.left(send.at[m], pair_first + 2 * m + k, partner_core)
        for stage in (a1, a2, b1, b2):
            stage.drain(m)

    loop(0, group, drain)
    links.drain()


def tail(branch, back, normed, weight, x, mid_grad, gain, early, down, up, out):
    grid = Grid()
    group, ys, xs, zs = grid.seq, grid.y, grid.x, grid.z
    rows, width = normed.shape
    wide = width // group
    shape = jax.ShapeDtypeStruct
    any_place = pl.BlockSpec(memory_space=pl.ANY)
    here = any_spec()
    share = width // (grid.dp * grid.seq)
    (down, down_rest), (up, up_rest) = down, up
    down_block, up_block, out_block = down[0].shape, up[0].shape, out[0].shape
    vmem = lambda dims, kind=BF16: pltpu.VMEM(tuple(dims), kind)
    a_full, b_full = (share, 2 * wide), (share, wide)
    copies = (
        group
        + 2 * group
        + 2 * group * (ys - 1)
        + 2 * group * (xs - 1)
        + 4 * (xs - 1)
        + 4 * (ys - 1)
        + 8 * zs
        + (1 + (ys - 1) + (xs - 1) + (zs - 1))
        + 2 * (zs - 1)
    )
    hops = 1 + (ys - 1) + (xs - 1) + (zs - 1)
    scratch = (
        [
            vmem((group, rows, 3 * wide)),
            vmem((min(4, group), 3, width, wide)),
            vmem((rows, width)),
            vmem((rows, width), F32),
            vmem((rows, width), F32),
            vmem((width, rows), F32),
            vmem((2, ys, xs, zs, share, rows)),
        ]
        + [vmem((group, ys, xs, zs) + a_full), vmem((group, ys, xs, zs) + b_full)] * 3
        + [
            vmem((group, ys - 1, xs, zs) + a_full),
            vmem((group, xs - 1, ys, zs) + b_full),
            vmem((group, xs, zs) + a_full),
            vmem((group, ys, zs) + b_full),
            vmem((group, xs - 1, zs) + a_full),
            vmem((group, ys - 1, zs) + b_full),
            vmem((zs, group) + a_full),
            vmem((zs, group) + b_full),
            vmem((zs - 1, group) + a_full),
            vmem((zs - 1, group) + b_full),
        ]
        + [vmem(down_block)] * ys
        + [vmem((xs - 1,) + down_block[1:])]
        + [vmem(down_block[1:])] * 3
        + [vmem(up_block)] * xs
        + [vmem((ys - 1,) + up_block[1:])]
        + [vmem(up_block[1:])] * 3
        + [
            vmem((ys,) + down_rest[0].shape),
            vmem((ys - 1,) + down_rest[0].shape),
            vmem(down_rest[0].shape),
            vmem((xs - 1,) + down_rest[0].shape[1:]),
        ]
        + [vmem(down_rest[0].shape[1:])] * 3
        + [
            vmem((ys,) + up_rest[0].shape),
            vmem((ys - 1,) + up_rest[0].shape),
            vmem(up_rest[0].shape),
            vmem((xs - 1,) + up_rest[0].shape[1:]),
        ]
        + [vmem(up_rest[0].shape[1:])] * 3
        + [vmem(out_block)] * zs
        + [
            vmem((ys - 1,) + out_block[1:]),
            vmem(out_block[1:]),
            vmem((xs - 1,) + out_block[2:]),
        ]
        + [
            vmem((4,) + early.shape, F32),
            vmem((hops,) + early.shape, F32),
            pltpu.SemaphoreType.DMA((copies,)),
            pltpu.SemaphoreType.DMA((copies,)),
            pltpu.SemaphoreType.DMA((2 + x.shape[0] + 3 * ys + xs + zs + 3 * group,)),
        ]
    )
    return pl.pallas_call(
        functools.partial(tail_kernel, wide),
        in_specs=[any_place, any_place, here, any_place, any_place, here, here]
        + [any_place] * (3 * ys + xs + zs),
        out_specs=[here] * 6,
        out_shape=[
            shape(x.shape, BF16),
            shape((group, share, 3 * wide), F32),
            shape((down_block[2], width), F32),
            shape((up_block[2], up_block[3] + up_rest[0].shape[3]), F32),
            shape(out_block[2:], F32),
            shape(early.shape, F32),
        ],
        scratch_shapes=scratch,
        compiler_params=params(collective_id=3 * branch + 3, has_side_effects=True),
        cost_estimate=pl.CostEstimate(
            flops=12 * rows * width * width, bytes_accessed=2**25, transcendentals=0
        ),
        name="tail",
    )(back, weight, normed, x, mid_grad, gain[None], early, *down, *down_rest, *up, *up_rest, *out)


def prepare_kernel(exit_ref, offsets, limit, tokens, upstream, x_ref, g_ref, pick_ref, ids_ref, most_ref, *scratch):
    rank_s, live_s, mine_s, got, send_sem, recv_sem = scratch
    rows, shard, _ = tokens.shape
    group = ids_ref.shape[1]
    docs = offsets.shape[1]
    dp, me = lax.axis_index("dp"), lax.axis_index("seq")
    others = lax.axis_size("dp") - 1
    links = Links(send_sem, recv_sem)
    for r in range(rows):
        for s in range(group):
            live = exit_ref[r : r + 1, s * shard : (s + 1) * shard] > limit[0]
            live_s[r * group + s : r * group + s + 1, :] = jnp.where(live, 1.0, 0.0)
    before = lax.broadcasted_iota(jnp.int32, (shard, shard), 0)
    after = lax.broadcasted_iota(jnp.int32, (shard, shard), 1)
    ones = jnp.where(before <= after, 1.0, 0.0).astype(BF16)
    rank = dot(live_s[...].astype(BF16), ones)
    rank_s[...] = jnp.where(live_s[...] > 0.0, rank - 1.0, -1.0)
    mine_s[...] = jnp.broadcast_to(jnp.max(rank), mine_s.shape)
    greet([], range(1, others + 1))
    for m in range(1, others + 1):
        links.start(mine_s, got.at[m - 1], m - 1, m - 1, {"dp": flip(dp, m)})
    slot = before.astype(F32)
    for r in range(rows):
        here = rank_s[pl.ds(r * group + me, 1), :]
        pick = jnp.where(slot == here, 1.0, 0.0).astype(BF16)
        pick_ref[r] = pick
        x_ref[r] = dot(pick, tokens[r]).astype(BF16)
        g_ref[r] = dot(pick, upstream[r]).astype(BF16)
    place = lax.broadcasted_iota(jnp.int32, (8, shard), 1)
    for r in range(rows):

        def document(s, r=r):
            at = place + s * shard
            ids = jnp.ones((8, shard), F32)
            for j in range(1, docs):
                ids = ids + jnp.where(at >= offsets[r, j], 1.0, 0.0)
            here = rank_s[pl.ds(r * group + s, 1), :]
            pick = jnp.where(slot == here, 1.0, 0.0).astype(BF16)
            ids_ref[r, s] = dot(ids.astype(BF16), pick, NT)[:1]

        loop(0, group, document)
    most = mine_s[...]
    for m in range(1, others + 1):
        links.arrived(got.at[m - 1], m - 1, {"dp": flip(dp, m)})
        most = jnp.maximum(most, got[m - 1])
    most_ref[...] = most
    links.drain()


def prepare(exit_layers, doc_offsets, layer_index, tokens, upstream):
    others = lax.axis_size("dp") - 1
    group = lax.axis_size("seq")
    rows, shard, width = tokens.shape
    shape = jax.ShapeDtypeStruct
    here, scalar = any_spec(), smem()
    return pl.pallas_call(
        prepare_kernel,
        in_specs=[here, scalar, scalar, here, here],
        out_specs=[here] * 5,
        out_shape=[
            shape(tokens.shape, BF16),
            shape(tokens.shape, BF16),
            shape((rows, shard, shard), BF16),
            shape((rows, group, 1, shard), F32),
            shape((8, 128), F32),
        ],
        scratch_shapes=[
            pltpu.VMEM((rows * group, shard), F32),
            pltpu.VMEM((rows * group, shard), F32),
            pltpu.VMEM((8, 128), F32),
            pltpu.VMEM((others, 8, 128), F32),
            pltpu.SemaphoreType.DMA((others,)),
            pltpu.SemaphoreType.DMA((others,)),
        ],
        compiler_params=params(collective_id=0, has_side_effects=True),
        name="prepare",
    )(exit_layers, doc_offsets, layer_index, tokens, upstream)


def layer(
    branch,
    cap,
    docs,
    x,
    g,
    ids,
    first_gain,
    first_shift,
    project_weight,
    query_bias,
    value_bias,
    output_weight,
    output_bias,
    second_gain,
    second_shift,
    up_weight,
    up_bias,
    down_weight,
    down_bias,
):
    group = lax.axis_size("seq")
    rows, shard, width = x.shape
    wide = width // group
    heads = wide // HEAD_DIM
    me = lax.axis_index("seq").astype(jnp.int32)
    tiles = pl.cdiv(group * cap, TILE)
    ids = ids[:, :, 0, :cap].reshape(rows, group * cap)
    ids = jnp.pad(ids, ((0, 0), (0, tiles * TILE - group * cap))).reshape(rows, tiles, 1, TILE)
    last = jnp.max(ids[:, :, 0], axis=2)
    first = jnp.min(jnp.where(ids == 0, docs + 1, ids)[:, :, 0], axis=2)
    number = jnp.arange(tiles, dtype=jnp.int32)
    needed = (last[:, None, :] >= first[:, :, None]) & (number < number[:, None])
    low = jnp.min(jnp.where(needed, number, number[:, None]), axis=2) // 2
    scalars = jnp.concatenate([me[None], low.reshape(-1)])
    biases = jnp.stack([query_bias, jnp.zeros_like(query_bias), value_bias])
    bias_parts = biases.reshape(3, group, wide).transpose(1, 0, 2).reshape(group, 1, 3 * wide)

    weight = split_weight(project_weight, group)
    normed, head_parts, context, ctx_parts, lse, slope = project_attend(
        branch, cap, docs, x, g, first_gain, first_shift, weight, bias_parts, down_weight, ids
    )
    grad_parts, result, middle_grad, early, *halves = feed_forward(
        branch,
        cap,
        ctx_parts,
        x,
        g,
        slope,
        output_weight,
        output_bias,
        second_gain,
        second_shift,
        up_weight,
        up_bias,
        down_weight,
        down_bias,
    )
    ys, xs = Grid().y, Grid().x
    down, up, out = halves[: 2 * ys], halves[2 * ys : 3 * ys + xs], halves[3 * ys + xs : -3]
    down_parts = exchange("y", down[0::2]), down[1::2]
    up_parts = exchange("x", up[:xs]), up[xs:]
    out_parts = exchange("z", out)
    back = attend_back(
        scalars, head_parts, context, grad_parts, ids, lse, docs, cap, heads
    )
    token_grad, project_share, down_share, up_share, out_share, sums = tail(
        branch, back, normed, weight, x, middle_grad, first_gain, early, down_parts, up_parts, out_parts
    )
    return (result, token_grad, project_share, out_share, up_share, down_share, sums)


CAPS = (12, 14, 16, 10)


def per_device(tokens, *args):
    *weights, doc_offsets, exit_layers, layer_index, upstream = args
    rows, shard, width = tokens.shape
    group = lax.axis_size("seq")
    wide = width // group
    docs = doc_offsets.shape[1]
    x, g, pick, ids, most = prepare(exit_layers, doc_offsets, layer_index, tokens, upstream)
    caps = [shard * k // 16 for k in CAPS]
    count = jnp.maximum(most[0, 0], 1.0)
    branch = sum(
        jnp.where((count <= cap) & (count > max([0] + [c for c in caps if c < cap])), k, 0)
        for k, cap in enumerate(caps)
    )
    steps = [functools.partial(layer, k, cap, docs) for k, cap in enumerate(caps)]
    result, token_grad, project_share, out_share, up_share, down_share, sums = lax.switch(
        branch, steps, x, g, ids, *weights
    )
    me = lax.axis_index("seq").astype(jnp.int32)
    live = lax.dynamic_slice_in_dim(exit_layers, me * shard, shard, 1) > layer_index[0]

    def unpack(packed, values):
        spread = jnp.einsum("rct,rcd->rtd", pick, packed, preferred_element_type=F32)
        return jnp.where(live[:, :, None], spread.astype(BF16), values)

    project_share = project_share.reshape(group, -1, 3, wide).transpose(1, 2, 0, 3)
    devices = lax.axis_size("dp") * group
    index = lax.axis_index("dp").astype(jnp.int32) * group + me
    part = width // devices
    singles = lax.dynamic_slice(sums, (0, index * part), (6, part))
    high = up_share.shape[1] // devices
    at = index * high
    up_bias_share = lax.dynamic_slice(sums, (6 + at // width, at % width), (1, high))[0]
    at = index * part
    by_part = [
        lax.dynamic_slice(sums, (VECTORS + at // wide, k * wide + at % wide), (1, part))[0]
        for k in range(3)
    ]
    return (
        unpack(result, tokens),
        unpack(token_grad, upstream),
        singles[0],
        singles[1],
        project_share.reshape(-1, 3 * width),
        by_part[0],
        by_part[2],
        out_share,
        singles[2],
        singles[3],
        singles[4],
        up_share,
        up_bias_share,
        down_share,
        singles[5],
    )


def solution(mesh):
    rows = P("dp", "seq", None)
    shares = P(("dp", "seq"))
    wide_shares = P(("dp", "seq"), None)
    in_specs = (rows,) + (P(),) * 13 + (P("dp", None), P("dp", None), P(), rows)
    out_specs = (
        rows,
        rows,
        shares,
        shares,
        wide_shares,
        shares,
        shares,
        wide_shares,
        shares,
        shares,
        shares,
        wide_shares,
        shares,
        wide_shares,
        shares,
    )
    return jax.shard_map(
        per_device, mesh=mesh, in_specs=in_specs, out_specs=out_specs, check_vma=False
    )
```

```python
import functools
import math

import jax
import jax.numpy as jnp
from jax import lax
from jax.experimental import pallas as pl
from jax.experimental.pallas import tpu as pltpu
from jax.sharding import PartitionSpec as P

HEAD_DIM = 64
SCALE = HEAD_DIM**-0.5
TILE = 256
PAIR = 2 * TILE
NEG = -1e30
EPS = 1e-05
VMEM_LIMIT = 60 * 2**20
F32 = jnp.float32
BF16 = jnp.bfloat16

NT = (((1,), (1,)), ((), ()))
NN = (((1,), (0,)), ((), ()))
TN = (((0,), (0,)), ((), ()))


def dot(a, b, dims=NN):
    return lax.dot_general(a, b, dims, preferred_element_type=F32)


def any_spec():
    return pl.BlockSpec(memory_space=pltpu.VMEM)


def params(**kw):
    return pltpu.CompilerParams(vmem_limit_bytes=VMEM_LIMIT, **kw)


def centre_rows(x):
    centred = x - jnp.mean(x, axis=-1, keepdims=True)
    spread = jnp.mean(centred * centred, axis=-1, keepdims=True)
    rs = lax.rsqrt(spread + EPS)
    return centred * rs, rs


def smem():
    return pl.BlockSpec(memory_space=pltpu.SMEM)


def flip(index, mask, size=64):
    bit = 1
    out = index
    while bit < size:
        if not isinstance(mask, int):
            ours, theirs = (index // bit) % 2, (mask // bit) % 2
            out = out + bit * (theirs - 2 * ours * theirs)
        elif mask & bit:
            out = out + bit * (1 - 2 * ((index // bit) % 2))
        bit *= 2
    return out


def loop(first, last, body):
    def turn(i, _):
        body(i)
        return 0

    lax.fori_loop(first, last, turn, 0)


class Links:
    def __init__(self, send_sem, recv_sem):
        self.send_sem, self.recv_sem, self.used, self.sent = send_sem, recv_sem, 0, []

    def reserve(self, count):
        first, self.used = self.used, self.used + count
        return first

    def start(self, src, dst, slot, there, device, later=True):
        copy = pltpu.make_async_remote_copy(
            src_ref=src,
            dst_ref=dst,
            send_sem=self.send_sem.at[slot],
            recv_sem=self.recv_sem.at[there],
            device_id=device,
            device_id_type=pl.DeviceIdType.MESH,
        )
        copy.start()
        if later:
            self.sent.append(copy)

    def left(self, src, slot, device):
        pltpu.make_async_remote_copy(
            src_ref=src,
            dst_ref=src,
            send_sem=self.send_sem.at[slot],
            recv_sem=self.recv_sem.at[slot],
            device_id=device,
            device_id_type=pl.DeviceIdType.MESH,
        ).wait_send()

    def arrived(self, ref, slot, device):
        pltpu.make_async_remote_copy(
            src_ref=ref,
            dst_ref=ref,
            send_sem=self.send_sem.at[slot],
            recv_sem=self.recv_sem.at[slot],
            device_id=device,
            device_id_type=pl.DeviceIdType.MESH,
        ).wait_recv()

    def drain(self):
        for copy in self.sent:
            copy.wait_send()


def greet(seq_masks, dp_masks):
    me, dp = lax.axis_index("seq"), lax.axis_index("dp")
    barrier = pltpu.get_barrier_semaphore()
    others = [{"seq": flip(me, m)} for m in seq_masks] + [{"dp": flip(dp, m)} for m in dp_masks]
    for device in others:
        pl.semaphore_signal(barrier, inc=1, device_id=device, device_id_type=pl.DeviceIdType.MESH)
    pl.semaphore_wait(barrier, len(others))


class Grid:
    def __init__(self):
        self.dp, self.seq = lax.axis_size("dp"), lax.axis_size("seq")
        self.y = self.dp // 2
        self.x = min(self.y, self.seq)
        self.z = self.seq // self.x
        self.size = {"y": self.y, "x": self.x, "z": self.z}

    def device(self, axis, r):
        me, dp = lax.axis_index("seq"), lax.axis_index("dp")
        if axis == "y":
            return {"dp": flip(dp, 2 * r)}
        return {"seq": flip(me, self.mask(axis, r))}

    def mask(self, axis, r):
        return {"y": 0, "x": r, "z": r * self.x}[axis]


def row_copies(slots, packed, sem, first):
    rows = slots.shape[0]
    cap = packed.shape[0] // rows
    return [
        pltpu.make_async_copy(
            slots.at[r, pl.ds(0, cap)], packed.at[pl.ds(r * cap, cap)], sem.at[first + r]
        )
        for r in range(rows)
    ]


def put_rows(slots, r, cap, values):
    slots[r, :cap] = values.astype(slots.dtype)
    if cap < slots.shape[1]:
        slots[r, cap:] = jnp.zeros((slots.shape[1] - cap, slots.shape[2]), slots.dtype)


def total_of(first, others, kind):
    total = first.astype(F32)
    for other in others:
        total = total + other.astype(F32)
    return total.astype(kind)


def add_into(total, others):
    inner = total.shape[1]

    def one(k):
        i, j = k // inner, k % inner
        total[i, j] = total_of(total[i, j], [other[i, j] for other in others], total.dtype)

    loop(0, total.shape[0] * inner, one)


class Summed:
    def __init__(self, links, grid, axis, block, got):
        self.links, self.grid, self.axis, self.block, self.got = links, grid, axis, block, got
        self.size = grid.size[axis]
        self.slot = links.reserve(self.size - 1)

    def send(self):
        for r in range(1, self.size):
            slot = self.slot + r - 1
            self.links.start(
                self.block.at[r], self.got.at[r - 1], slot, slot, self.grid.device(self.axis, r)
            )

    def receive(self, store, kind=BF16):
        for r in range(1, self.size):
            self.links.arrived(
                self.got.at[r - 1], self.slot + r - 1, self.grid.device(self.axis, r)
            )
        inner = store.shape[1]

        def one(k):
            i, j = k // inner, k % inner
            others = [self.got[r - 1, i, j] for r in range(1, self.size)]
            store[i, j] = total_of(self.block[0, i, j], others, kind)

        if len(store.shape) == 4:
            loop(0, store.shape[0] * inner, one)
        else:
            store[...] = total_of(self.block[0], [self.got[r - 1] for r in range(1, self.size)], kind)

    def receive_last(self, store):
        for r in range(1, self.size):
            self.links.arrived(
                self.got.at[r - 1], self.slot + r - 1, self.grid.device(self.axis, r)
            )
        store[...] = total_of(self.block[0], [self.got[r - 1] for r in range(1, self.size)], F32)


class LineSum:
    def __init__(self, links, grid, block, right, left):
        self.links, self.grid, self.block = links, grid, block
        self.got = {1: right, -1: left}
        self.size = grid.z
        self.place = lax.axis_index("seq") // grid.x
        self.slot = {1: links.reserve(self.size), -1: links.reserve(self.size)}

    def next(self, way):
        return {"seq": lax.axis_index("seq") + way * self.grid.x}

    def copy(self, way, goal, src):
        slot = self.slot[way] + goal
        return pltpu.make_async_remote_copy(
            src_ref=src,
            dst_ref=self.got[way].at[goal],
            send_sem=self.links.send_sem.at[slot],
            recv_sem=self.links.recv_sem.at[slot],
            device_id=self.next(way),
            device_id_type=pl.DeviceIdType.MESH,
        )

    def source(self, way, goal, first):
        if first:
            return self.block.at[flip(self.place, goal)]
        return self.got[way].at[goal]

    def hop(self, k):
        for way, at in ((1, k), (-1, self.size - 1 - k)):
            goals = range(self.size - 1, at, -1) if way == 1 else range(at)

            @pl.when(self.place == at)
            def _(way=way, goals=goals):
                for goal in goals:
                    if k:
                        self.arrived(way, goal)
                        got = self.got[way]
                        own = self.block.at[flip(self.place, goal)]
                        for i in range(got.shape[1]):
                            got[goal, i] = total_of(own[i], [got[goal, i]], BF16)
                    self.copy(way, goal, self.source(way, goal, k == 0)).start()

    def arrived(self, way, goal):
        self.copy(way, goal, self.got[way].at[goal]).wait_recv()

    def finish(self, store, cols):
        store[:, cols] = self.block[0].astype(F32)
        for way, limit in ((1, self.place > 0), (-1, self.place < self.size - 1)):

            @pl.when(limit)
            def _(way=way):
                self.arrived(way, self.place)
                store[:, cols] = store[:, cols] + self.got[way][self.place].astype(F32)

        for way in (1, -1):
            for goal in range(self.size):

                @pl.when(self.place < goal if way == 1 else self.place > goal)
                def _(way=way, goal=goal):
                    self.copy(way, goal, self.got[way].at[goal]).wait_send()


class SlotSum:
    def __init__(self, links, grid, axis, slots, block, got, inner=False):
        self.links, self.grid, self.axis, self.got = links, grid, axis, got
        self.block = (lambda m, r: block.at[m, :, r]) if inner else (lambda m, r: block.at[m, r])
        self.size, self.slots = grid.size[axis], slots
        self.first = links.reserve(slots * (self.size - 1))

    def id(self, m, r):
        return self.first + m * (self.size - 1) + r - 1

    def send(self, m):
        for r in range(1, self.size):
            there = flip(m, self.grid.mask(self.axis, r), self.slots)
            self.links.start(
                self.block(m, r),
                self.got.at[there, r - 1],
                self.id(m, r),
                self.id(there, r),
                self.grid.device(self.axis, r),
                later=False,
            )

    def receive(self, m):
        for r in range(1, self.size):
            self.links.arrived(
                self.got.at[m, r - 1], self.id(m, r), self.grid.device(self.axis, r)
            )
        return total_of(
            self.block(m, 0)[...], [self.got[m, r - 1] for r in range(1, self.size)], F32
        )

    def drain(self, m):
        for r in range(1, self.size):
            self.links.left(self.block(m, r), self.id(m, r), self.grid.device(self.axis, r))


def split_weight(weight, group):
    width = weight.shape[0]
    wide = width // group
    if wide % 128 == 0:
        return weight
    return weight.reshape(width, 3, group, wide).transpose(1, 2, 0, 3)


def weight_view(weight, part, source, width, wide):
    if wide % 128 == 0:
        return weight.at[:, pl.ds(pl.multiple_of(part * width + source * wide, 128), wide)]
    return weight.at[part, source]


def only_head(block, head, heads):
    if heads == 1:
        return block
    lane = lax.broadcasted_iota(jnp.int32, block.shape, 1)
    return jnp.where(lane // HEAD_DIM == head, block, jnp.zeros_like(block))


def transposed(block):
    return block.astype(F32).T.astype(BF16)


def causal(size, offset):
    key = lax.broadcasted_iota(jnp.int32, (size, TILE), 0)
    query = lax.broadcasted_iota(jnp.int32, (size, TILE), 1)
    return key <= query + offset


def sweep(tiles, low_of, start, step, finish):
    def before(i, whole_blocks):
        low = low_of(i)
        return lax.fori_loop(
            low, whole_blocks, lambda b, c: step(i, b * PAIR, PAIR, None, c), start(i)
        )

    def even(i, half):
        finish(i, step(i, i * TILE, TILE, 0, before(i, half)))

    def odd(i, half):
        finish(i, step(i, half * PAIR, PAIR, TILE, before(i, half)))

    def both(half, _):
        even(2 * half, half)
        odd(2 * half + 1, half)
        return 0

    lax.fori_loop(0, tiles // 2, both, 0)
    if tiles % 2:
        even(tiles - 1, tiles // 2)


def span(at, size):
    return pl.ds(at if isinstance(at, int) else pl.multiple_of(at, TILE), size)


def blank_rest(used, *arrays):
    if used < arrays[0].shape[0]:
        for array in arrays:
            array[used:, :] = jnp.zeros((array.shape[0] - used, array.shape[1]), array.dtype)


def load_heads(me, cap, parts, q_s, k_s, v_s):
    wide = v_s.shape[1]
    blank_rest(parts.shape[0] * cap, q_s, k_s, v_s)
    for m in range(parts.shape[0]):
        here = pl.ds(pl.multiple_of((me ^ m) * cap, math.gcd(cap, 128)), cap)
        q_s[here, :] = parts[m, :, :wide] * SCALE
        k_s[here, :wide] = parts[m, :, wide : 2 * wide]
        v_s[here, :] = parts[m, :, 2 * wide :]


def documents(ids, docs):
    row = lax.broadcasted_iota(jnp.int32, (128, TILE), 0).astype(F32)
    unit = row + 1.0 == ids
    query = jnp.where(unit, 1.0, 0.0).astype(BF16)
    return query, jnp.where(unit | (row >= docs), 0.0, NEG)


def by_head(turned, heads):
    if heads == 1:
        return [turned]
    row = lax.broadcasted_iota(jnp.int32, turned.shape, 0) // HEAD_DIM
    return [jnp.where(row == h, turned, jnp.zeros_like(turned)) for h in range(heads)]


def query_rows(queries, ids, docs, heads):
    unit, _ = documents(ids, docs)
    turned = queries.astype(F32).T
    return tuple(
        jnp.concatenate([part.astype(BF16), unit], axis=0) for part in by_head(turned, heads)
    )


def key_documents(ids_ref, k_s, wide, docs):
    for t in range(ids_ref.shape[0]):
        _, keys = documents(ids_ref[t], docs)
        k_s[t * TILE : (t + 1) * TILE, wide:] = keys.T.astype(BF16)


def attend_row(heads, docs, tiles, ids, lse, q_s, k_s, v_s, vt_s, o_s):
    for t in range(tiles):
        vt_s[:, t * TILE : (t + 1) * TILE] = transposed(v_s[t * TILE : (t + 1) * TILE, :])

    def start(i):
        blank = (
            jnp.full((1, TILE), NEG, F32),
            jnp.zeros((1, TILE), F32),
            jnp.zeros((HEAD_DIM, TILE), F32),
        )
        return query_rows(q_s[span(i * TILE, TILE), :], ids[i], docs, heads), (blank,) * heads

    def step(i, at, size, diagonal, carry):
        queries, states = carry
        there = span(at, size)
        keys = k_s[there, :]
        new = []
        for h in range(heads):
            top, total, acc = states[h]
            s = dot(keys, queries[h])
            if diagonal is not None:
                s = jnp.where(causal(size, diagonal), s, NEG)
            top2 = jnp.maximum(top, jnp.max(s, axis=0, keepdims=True))
            p = jnp.exp(s - top2)
            fade = jnp.exp(top - top2)
            total = total * fade + jnp.sum(p, axis=0, keepdims=True)
            vt = vt_s[h * HEAD_DIM : (h + 1) * HEAD_DIM, there]
            acc = acc * fade + dot(vt, p.astype(BF16))
            new.append((top2, total, acc))
        return queries, tuple(new)

    def finish(i, carry):
        pieces = []
        for h in range(heads):
            top, total, acc = carry[1][h]
            pieces.append(acc * (1.0 / total))
            lse[i, h : h + 1, :] = top + jnp.log(total)
        o_s[span(i * TILE, TILE), :] = jnp.concatenate(pieces, axis=0).T.astype(BF16)

    sweep(tiles, lambda i: 0, start, step, finish)


def first_kernel(wide, docs, *refs):
    x_hbm, g_hbm, gain_ref, shift_ref, weight, bias_ref, dw_hbm, ids_ref = refs[:8]
    normed_ref, heads_hbm, context_hbm, ctx_hbm, lse_ref, slope_hbm = refs[8:14]
    w_s, stage, landed, x_ref, g_ref, dw, slope, q_s, k_s, v_s, vt_s, o_s = refs[14:26]
    send_sem, recv_sem, load_sem = refs[26:]
    group = lax.axis_size("seq")
    me = lax.axis_index("seq")
    width = x_ref.shape[1]
    rows, tiles = ids_ref.shape[0], ids_ref.shape[1]
    cap = x_ref.shape[0] // rows
    heads = wide // HEAD_DIM
    hidden = dw.shape[0]
    links = Links(send_sem, recv_sem)
    first, second = links.reserve(rows * group), links.reserve(rows * group)
    order = list(range(group - 1, 0, -1)) + [0]
    used = [0]

    def local(src, dst):
        copy = pltpu.make_async_copy(src, dst, load_sem.at[used[0]])
        used[0] += 1
        copy.start()
        return copy

    held_x = [local(x_hbm.at[r, pl.ds(0, cap)], x_ref.at[pl.ds(r * cap, cap)]) for r in range(rows)]
    held_w = {}
    for m in order:
        source = flip(me, m)
        held_w[m] = [
            local(weight_view(weight, part, source, width, wide), w_s.at[m, part])
            for part in range(3)
        ]
    held_g = [local(g_hbm.at[r, pl.ds(0, cap)], g_ref.at[pl.ds(r * cap, cap)]) for r in range(rows)]
    held_g.append(local(dw_hbm, dw))
    for copy in held_x:
        copy.wait()
    n, _ = centre_rows(x_ref[...].astype(F32))
    normed_ref[...] = (n * gain_ref[...] + shift_ref[...]).astype(BF16)
    greet(range(1, group), [])

    for r in range(rows):
        here = slice(r * cap, (r + 1) * cap)
        for m in order:
            if r == 0:
                for copy in held_w[m]:
                    copy.wait()
            joined = jnp.concatenate([w_s[m, part] for part in range(3)], axis=1)
            value = (dot(normed_ref[here, :], joined) + bias_ref[flip(me, m)]).astype(BF16)
            if m:
                stage[m, here, :] = value
                links.start(
                    stage.at[m, here],
                    landed.at[m, here],
                    first + r * group + m,
                    first + r * group + m,
                    {"seq": flip(me, m)},
                )
            else:
                landed[0, here, :] = value

    for copy in held_g:
        copy.wait()
    block = min(512, hidden)

    def before(f):
        at = pl.ds(pl.multiple_of(f * block, block), block)
        slope[:, at] = dot(g_ref[...], dw[at, :], NT).astype(BF16)

    loop(0, hidden // block, before)
    leaving = [local(slope, slope_hbm)]
    blank_rest(group * cap, q_s, k_s, v_s)
    for r in range(rows):
        here = slice(r * cap, (r + 1) * cap)
        for m in range(1, group):
            links.arrived(landed.at[m, here], first + r * group + m, {"seq": flip(me, m)})
        for m in range(group):
            there = pl.ds(pl.multiple_of(flip(me, m) * cap, math.gcd(cap, 128)), cap)
            q_s[there, :] = landed[m, here, :wide] * SCALE
            k_s[there, :wide] = landed[m, here, wide : 2 * wide]
            v_s[there, :] = landed[m, here, 2 * wide :]
        key_documents(ids_ref.at[r], k_s, wide, docs)
        attend_row(heads, docs, tiles, ids_ref.at[r], lse_ref.at[r], q_s, k_s, v_s, vt_s, o_s.at[r])
        for m in order:
            src = o_s.at[r, pl.ds(pl.multiple_of(flip(me, m) * cap, math.gcd(cap, 128)), cap)]
            if m:
                links.start(
                    src,
                    ctx_hbm.at[m, here],
                    second + r * group + m,
                    second + r * group + m,
                    {"seq": flip(me, m)},
                )
            else:
                leaving.append(local(src, ctx_hbm.at[0, here]))
        leaving.append(local(o_s.at[r], context_hbm.at[r]))
    leaving.append(local(landed, heads_hbm))
    for r in range(rows):
        here = slice(r * cap, (r + 1) * cap)
        for m in range(1, group):
            links.arrived(ctx_hbm.at[m, here], second + r * group + m, {"seq": flip(me, m)})
    links.drain()
    for copy in leaving:
        copy.wait()


def project_attend(branch, cap, docs, x, g, gain, shift, weight, bias_parts, dw, ids):
    slots, width = x.shape[0], x.shape[2]
    rows = slots * cap
    group = bias_parts.shape[0]
    wide = width // group
    cols = 3 * wide
    tiles = ids.shape[1]
    length = tiles * TILE
    heads = wide // HEAD_DIM
    hidden = dw.shape[0]
    here = any_spec()
    anywhere = pl.BlockSpec(memory_space=pl.ANY)
    shape = jax.ShapeDtypeStruct
    vmem = lambda dims, kind=BF16: pltpu.VMEM(dims, kind)
    pair = slots * heads * length * length // 2
    return pl.pallas_call(
        functools.partial(first_kernel, wide, docs),
        in_specs=[anywhere, anywhere, here, here, anywhere, here, anywhere, here],
        out_specs=[here, anywhere, anywhere, anywhere, here, anywhere],
        out_shape=[
            shape((rows, width), BF16),
            shape((group, rows, cols), BF16),
            shape((slots, length, wide), BF16),
            shape((group, rows, wide), BF16),
            shape((slots, tiles, heads, TILE), F32),
            shape((rows, hidden), BF16),
        ],
        scratch_shapes=[
            vmem((group, 3, width, wide)),
            vmem((group, rows, cols)),
            vmem((group, rows, cols)),
            vmem((rows, width)),
            vmem((rows, width)),
            vmem((hidden, width)),
            vmem((rows, hidden)),
            vmem((length, wide)),
            vmem((length, wide + 128)),
            vmem((length, wide)),
            vmem((wide, length)),
            vmem((slots, length, wide)),
            pltpu.SemaphoreType.DMA((2 * slots * group,)),
            pltpu.SemaphoreType.DMA((2 * slots * group,)),
            pltpu.SemaphoreType.DMA((4 * slots + 3 * group + 3,)),
        ],
        compiler_params=params(collective_id=3 * branch + 1, has_side_effects=True),
        cost_estimate=pl.CostEstimate(
            flops=2 * rows * width * (cols * group + hidden) + 4 * 256 * pair,
            bytes_accessed=2 * group * cols * (width + rows) + 2 * hidden * width,
            transcendentals=pair,
        ),
        name="project_attend",
    )(x, g, gain[None], shift[None], weight, bias_parts, dw, ids)


def attend_back_kernel(group, cap, tiles, heads, docs, sc_ref, *refs):
    parts, ctx, grads, ids_ref, lse_ref, out_ref = refs[:6]
    refs = refs[6:]
    q_s, k_s, v_s, kt_s, g_s, dq_s, dk_s, dv_s = refs
    wide = heads * HEAD_DIM
    me = sc_ref[0]
    row = pl.program_id(0)
    load_heads(me, cap, parts, q_s, k_s, v_s)
    key_documents(ids_ref.at[0], k_s, wide, docs)
    blank_rest(group * cap, g_s)
    for m in range(group):
        here = pl.ds(pl.multiple_of((me ^ m) * cap, math.gcd(cap, 128)), cap)
        g_s[here, :] = grads[m]
    for t in range(tiles):
        kt_s[:, t * TILE : (t + 1) * TILE] = transposed(k_s[t * TILE : (t + 1) * TILE, :wide])
    dk_s[...] = jnp.zeros_like(dk_s)
    dv_s[...] = jnp.zeros_like(dv_s)

    def start(i):
        at = span(i * TILE, TILE)
        queries = q_s[at, :]
        grad = g_s[at, :]
        product = (grad.astype(F32) * ctx[0, at, :].astype(F32)).T
        delta = tuple(
            jnp.sum(product[h * HEAD_DIM : (h + 1) * HEAD_DIM], axis=0, keepdims=True)
            for h in range(heads)
        )
        split_q = tuple(only_head(queries, h, heads) for h in range(heads))
        split_g = tuple(only_head(grad, h, heads) for h in range(heads))
        turned_q = query_rows(queries, ids_ref[0, i], docs, heads)
        turned_g = tuple(part.astype(BF16) for part in by_head(grad.astype(F32).T, heads))
        fixed = (split_q, split_g, turned_q, turned_g, delta)
        return fixed, tuple(jnp.zeros((HEAD_DIM, TILE), F32) for _ in range(heads))

    def step(i, at, size, diagonal, carry):
        fixed, sums = carry
        split_q, split_g, turned_q, turned_g, delta = fixed
        there = span(at, size)
        keys = k_s[there, :]
        values = v_s[there, :]
        new, ps, dss = [], [], []
        for h in range(heads):
            s = dot(keys, turned_q[h]) - lse_ref[0, i, h : h + 1, :]
            if diagonal is not None:
                s = jnp.where(causal(size, diagonal), s, NEG)
            p = jnp.exp(s)
            dp = dot(values, turned_g[h])
            ds = (p * (dp - delta[h])).astype(BF16)
            ps.append(p.astype(BF16))
            dss.append(ds)
            kt = kt_s[h * HEAD_DIM : (h + 1) * HEAD_DIM, there]
            new.append(sums[h] + dot(kt, ds))
        dv = dot(ps[0], split_g[0])
        dk = dot(dss[0], split_q[0])
        for h in range(1, heads):
            dv = dv + dot(ps[h], split_g[h])
            dk = dk + dot(dss[h], split_q[h])
        dv_s[there, :] += dv
        dk_s[there, :] += dk
        return fixed, tuple(new)

    def finish(i, carry):
        dq_s[span(i * TILE, TILE), :] = (jnp.concatenate(carry[1], axis=0).T * SCALE).astype(BF16)

    sweep(tiles, lambda i: sc_ref[1 + row * tiles + i], start, step, finish)
    for m in range(group):
        here = pl.ds(pl.multiple_of((me ^ m) * cap, math.gcd(cap, 128)), cap)
        out_ref[m, :, :wide] = dq_s[here, :]
        out_ref[m, :, wide : 2 * wide] = dk_s[here, :].astype(BF16)
        out_ref[m, :, 2 * wide :] = dv_s[here, :].astype(BF16)


def attend_back(scalars, parts, ctx, grads, ids, lse, docs, cap, heads):
    group, tokens, cols = parts.shape
    rows = tokens // cap
    tiles = pl.cdiv(group * cap, TILE)
    length = tiles * TILE
    wide = heads * HEAD_DIM
    deep = wide + 128
    pair = rows * heads * length * length // 2
    by_row = lambda r, sc: (0, r, 0)
    all_row = lambda r, sc: (r, 0, 0, 0)
    return pl.pallas_call(
        functools.partial(attend_back_kernel, group, cap, tiles, heads, docs),
        grid_spec=pltpu.PrefetchScalarGridSpec(
            num_scalar_prefetch=1,
            grid=(rows,),
            in_specs=[pl.BlockSpec((group, cap, cols), by_row)]
            + [pl.BlockSpec((1, length, wide), lambda r, sc: (r, 0, 0))]
            + [pl.BlockSpec((group, cap, wide), by_row)]
            + [pl.BlockSpec((1, tiles, 1, TILE), all_row)]
            + [pl.BlockSpec((1, tiles, heads, TILE), lambda r, sc: (r, 0, 0, 0))],
            out_specs=pl.BlockSpec((group, cap, cols), by_row),
            scratch_shapes=[
                pltpu.VMEM((length, wide), BF16),
                pltpu.VMEM((length, deep), BF16),
                pltpu.VMEM((length, wide), BF16),
                pltpu.VMEM((wide, length), BF16),
            ]
            + [pltpu.VMEM((length, wide), BF16)] * 2
            + [pltpu.VMEM((length, wide), F32)] * 2,
        ),
        out_shape=jax.ShapeDtypeStruct((group, rows * cap, cols), BF16),
        compiler_params=params(),
        cost_estimate=pl.CostEstimate(
            flops=10 * 256 * pair, bytes_accessed=20 * rows * length * wide, transcendentals=pair
        ),
        name="attend_back",
    )(scalars, parts, ctx, grads, ids, lse)


def norm_back(upper, n, rs, gain):
    e = upper * gain
    return rs * (
        e - jnp.mean(e, axis=-1, keepdims=True) - n * jnp.mean(e * n, axis=-1, keepdims=True)
    )


GELU_A = 0.7978845608028654
GELU_B = 0.044715


VECTORS = 10


def early_cols(cols, late):
    early = cols * 3 // 4
    return cols - early if late else early


def mid_kernel(wide, *refs):
    grid = Grid()
    group, ys, xs, zs = grid.seq, grid.y, grid.x, grid.z
    refs = list(refs)

    def take(n):
        out = refs[:n]
        del refs[:n]
        return out

    ctx_hbm, x_hbm, g_hbm, slope_hbm, ow_hbm, uw_hbm, dw_hbm, ob, gain, shift, ub, db = take(12)
    grads, result_ref, mg_ref, early = take(4)
    down_out, up_out, out_out = take(2 * ys), take(xs + ys), take(zs)
    gots = take(3)
    x_ref, g_ref, landed, ctx, ow, uw, dw, hid, rise, mid_s, n2_s, normed, attn, chunk = take(14)
    rings, loaded, lefts = take(3), take(3), take(6)
    send_sem, recv_sem, load_sem, ring_sem, got_sem = take(5)

    me, dp = lax.axis_index("seq"), lax.axis_index("dp")
    core, row = dp % 2, dp // 2
    links = Links(send_sem, recv_sem)
    tokens, width = x_ref.shape
    hidden = hid.shape[1]
    block = min(512, hidden)
    partner_core = {"dp": flip(dp, 1)}
    loads = [
        pltpu.make_async_copy(src, dst, load_sem.at[k])
        for k, (src, dst) in enumerate(
            ((ow_hbm, ow), (ctx_hbm, landed), (uw_hbm, uw), (slope_hbm, rise), (dw_hbm, dw))
        )
    ]
    held = row_copies(g_hbm, g_ref, load_sem, 5) + row_copies(x_hbm, x_ref, load_sem, 5 + x_hbm.shape[0])
    for copy in loads[:2] + held + loads[2:]:
        copy.start()
    greet(range(1, group), [1])
    for copy in held + loads[:2]:
        copy.wait()
    early[...] = jnp.zeros_like(early)
    early[5:6, :] = jnp.sum(g_ref[...].astype(F32), axis=0, keepdims=True)

    def lanes(f, size):
        return pl.ds(pl.multiple_of(f * size, size), size)

    for s in range(group):
        chunk[s] = landed[flip(me, s)]
    for s in range(group):
        ctx[:, s * wide : (s + 1) * wide] = chunk[s]
    mid = x_ref[...].astype(F32) + dot(ctx[...], ow[...]) + ob[...]
    mid_s[...] = mid
    n, _ = centre_rows(mid)
    normed[...] = (n * gain[...] + shift[...]).astype(BF16)
    n2_s[...] = jnp.zeros_like(n2_s)
    for copy in loads[2:4]:
        copy.wait()

    def through(f, _):
        here = lanes(f, block)
        u = dot(normed[...], uw[:, here]) + ub[:, here]
        square = u * u
        t = jnp.tanh(GELU_A * u * (1.0 + GELU_B * square))
        half = 0.5 * (1.0 + t)
        hid[:, here] = (u * half).astype(BF16)
        slope = half + 0.5 * GELU_A * u * (1.0 - t * t) * (1.0 + 3.0 * GELU_B * square)
        up = (rise[:, here].astype(F32) * slope).astype(BF16)
        rise[:, here] = up
        n2_s[...] += dot(up, uw[:, here], NT)
        return 0

    def ordered(ring, spot, total, parts, share, got):
        for s in range(parts):
            rel = flip(me % parts, s)
            piece = total[s * share : (s + 1) * share]
            if got is not None:
                piece = piece + got[rel % xs, rel // xs].astype(F32)
            ring[spot, rel % xs, rel // xs] = piece.astype(BF16)

    def outputs(item, o, z, cols, ring):
        if item == 0:
            first = down_out[0].shape[-1]
            for h, here in enumerate((slice(0, first), slice(first, width))):
                yield ring.at[:, :, :, here], down_out[2 * o + h].at[:, z]
        elif item == 1:
            first = up_out[0].shape[-1]
            if cols.start >= first:
                here = slice(cols.start - first, cols.stop - first)
                yield ring, up_out[xs + o].at[:, :, :, here]
            else:
                for x in range(xs):
                    yield ring.at[x], up_out[x].at[o, :, :, cols]
        else:
            for z in range(zs):
                yield ring.at[:, z], out_out[z].at[o]

    def weight_grad(item, a, b):
        share = a.shape[1] // (2 * ys * group)
        parts = min(group, max(256 // share, xs))
        sub = group // parts
        depth = parts // xs
        cols = b.shape[1]
        piece = min(1024, cols)
        pieces = cols // piece
        count = ys * sub * pieces
        ring, got, left_s = rings[item], loaded[item], lefts[2 * item : 2 * item + 2]
        spots = ring.shape[0] // 2
        slot = links.reserve(count)

        def unit(n):
            u = n // pieces
            return ys - 1 - u // sub, u % sub, n % pieces

        def start_of(c, n):
            o, k, _ = unit(n)
            at = (flip(row, o, ys) * 2 + flip(core, c, 2)) * group * share
            return at + flip(me // parts, k, sub) * parts * share

        def product(c, n):
            o, k, p = unit(n)
            left = left_s[c]

            @pl.when(p == 0)
            def _():
                at = pl.multiple_of(start_of(c, n), 128)
                left[...] = transposed(a[:, pl.ds(at, parts * share)])

            return dot(left[...], b[:, pl.ds(pl.multiple_of(p * piece, piece), piece)])

        def place(n):
            o, k, p = unit(n)
            columns = pl.ds(pl.multiple_of(p * piece, piece), piece)
            return (o, slice(None), pl.ds(k * depth, depth), slice(None), columns)

        def away(n):
            links.left(ring.at[n % spots], slot + n, partner_core)

        def send(n):
            @pl.when(n >= spots)
            def _():
                away(n - spots)

            ordered(ring, n % spots, product(1, n), parts, share, None)
            there = gots[item].at[place(n)]
            links.start(ring.at[n % spots], there, slot + n, slot + n, partner_core, later=False)

        def fetch(n):
            src = gots[item].at[place(n)]
            return pltpu.make_async_copy(src, got.at[n % 2], got_sem.at[2 * item + n % 2])

        def fetch_start(n):
            links.arrived(gots[item].at[place(n)], slot + n, partner_core)
            fetch(n).start()

        def written(n, act):
            for fixed in range(ys):
                for p in range(pieces):
                    o, k, q = unit(n)

                    @pl.when((o == fixed) & (q == p))
                    def _(fixed=fixed, p=p):
                        spot = spots + n % spots
                        z = pl.ds(k * depth, depth)
                        here = slice(p * piece, (p + 1) * piece)
                        copies = outputs(item, fixed, z, here, ring.at[spot])
                        for h, (src, dst) in enumerate(copies):
                            at = (item * spots + n % spots) * max(2, xs, zs) + h
                            act(pltpu.make_async_copy(src, dst, ring_sem.at[at]))

        def keep(n):
            @pl.when(n + 1 < count)
            def _():
                fetch_start(n + 1)

            @pl.when(n >= spots)
            def _():
                written(n - spots, lambda copy: copy.wait())

            total = product(0, n)
            fetch(n).wait()
            ordered(ring, spots + n % spots, total, parts, share, got.at[n % 2])
            written(n, lambda copy: copy.start())

        def rest(act):
            for n in range(max(0, count - spots), count):
                act(n)

        def finish():
            rest(lambda n: written(n, lambda copy: copy.wait()))

        return count, send, lambda: rest(away), fetch_start, keep, finish, start_of

    first_job = weight_grad(0, hid, g_ref)
    steps = hidden // block
    per = first_job[0] * 2 // steps

    def mine(i):
        c = 1 - 2 * i // steps
        f = first_job[6](c, (i % (steps // 2)) * per) // block
        through(f, 0)

        @pl.when(c == 1)
        def _():
            for k in range(per):
                first_job[1](i * per + k)

    loop(0, steps, mine)
    first_job[2]()
    n, rs = centre_rows(mid_s[...])
    n2 = n2_s[...]
    early[3:4, :] = jnp.sum(n2 * n, axis=0, keepdims=True)
    early[4:5, :] = jnp.sum(n2, axis=0, keepdims=True)
    mid_grad = g_ref[...].astype(F32) + norm_back(n2, n, rs, gain[...])
    mg_ref[...] = mid_grad
    attn[...] = mid_grad.astype(BF16)
    full = dot(attn[...], ow[...], NT).astype(BF16)
    for s in range(group):
        chunk[flip(me, s)] = full[:, s * wide : (s + 1) * wide]
    second = links.reserve(group)
    for m in range(group - 1, 0, -1):
        links.start(chunk.at[m], grads.at[m], second + m, second + m, {"seq": flip(me, m)})
    own = pltpu.make_async_copy(chunk.at[0], grads.at[0], load_sem.at[0])
    own.start()

    jobs = [first_job, weight_grad(1, normed, rise), weight_grad(2, ctx, attn)]
    for stage in range(1, len(jobs) + 1):
        new = jobs[stage] if stage < len(jobs) else None
        old = jobs[stage - 1]
        old[3](0)

        def turn(n, new=new, old=old):
            for job, act in ((new, 1), (old, 4)):
                if job:
                    if new and old and job[0] < max(new[0], old[0]):
                        pl.when(n < job[0])(lambda job=job, act=act: job[act](n))
                    else:
                        job[act](n)

        loop(0, max(job[0] for job in (new, old) if job), turn)
        if new:
            new[2]()
        old[5]()


    loads[4].wait()

    def finished(k):
        here = lanes(k, 256)
        mid_s[:, here] = mid_s[:, here] + (dot(hid[...], dw[:, here]) + db[:, here])

    loop(0, width // 256, finished)
    cap = tokens // result_ref.shape[0]
    for r in range(result_ref.shape[0]):
        put_rows(result_ref, r, cap, mid_s[r * cap : (r + 1) * cap, :])
    early[2:3, :] = jnp.sum(attn[...].astype(F32), axis=0, keepdims=True)
    for k in range(hidden // width):
        part = rise[:, k * width : (k + 1) * width].astype(F32)
        early[6 + k : 7 + k, :] = jnp.sum(part, axis=0, keepdims=True)
    for m in range(1, group):
        links.arrived(grads.at[m], second + m, {"seq": flip(me, m)})
    own.wait()
    links.drain()


def feed_forward(branch, cap, ctx, x, g, slope, ow, ob, gain, shift, uw, ub, dw, db):
    grid = Grid()
    group, ys, xs, zs = grid.seq, grid.y, grid.x, grid.z
    rows, width = x.shape[0] * cap, x.shape[2]
    wide = width // group
    hidden = uw.shape[1]
    here = any_spec()
    anywhere = pl.BlockSpec(memory_space=pl.ANY)
    shape = jax.ShapeDtypeStruct
    low, high = width // (grid.dp * group), hidden // (grid.dp * group)
    vectors = VECTORS + group
    vectors += -vectors % 8
    sums = [
        shape((ys, xs, zs, high, width), BF16),
        shape((ys, xs, zs, low, hidden), BF16),
        shape((ys, xs, zs, low, width), BF16),
    ]
    parts = lambda share: min(group, max(256 // share, xs))
    block = lambda share: (xs, parts(share) // xs, share, width)
    rings = [pltpu.VMEM((n,) + block(share), BF16) for n in (4, 2) for share in (high, low, low)]
    turned = [pltpu.VMEM((parts(s) * s, rows), BF16) for s in (high, low, low) for _ in range(2)]
    blocks = ys * (group // parts(high)) + ys * (hidden // width) + ys
    vmem = lambda dims, kind=BF16: pltpu.VMEM(dims, kind)
    return pl.pallas_call(
        functools.partial(mid_kernel, wide),
        in_specs=[anywhere] * 7 + [here] * 5,
        out_specs=[anywhere, here, here, here] + [anywhere] * (3 * ys + xs + zs + 3),
        out_shape=[
            shape((group, rows, wide), BF16),
            shape(x.shape, BF16),
            shape((rows, width), F32),
            shape((vectors, width), F32),
        ]
        + [shape((xs, zs, high, early_cols(width, k)), BF16) for _ in range(ys) for k in range(2)]
        + [shape((ys, zs, low, early_cols(hidden, 0)), BF16)] * xs
        + [shape((xs, zs, low, early_cols(hidden, 1)), BF16)] * ys
        + [shape((ys, xs, low, width), BF16)] * zs
        + sums,
        scratch_shapes=[
            vmem((rows, width)),
            vmem((rows, width)),
            vmem((group, rows, wide)),
            vmem((rows, width)),
            vmem((width, width)),
            vmem((width, hidden)),
            vmem((hidden, width)),
            vmem((rows, hidden)),
            vmem((rows, hidden)),
            vmem((rows, width), F32),
            vmem((rows, width), F32),
            vmem((rows, width)),
            vmem((rows, width)),
            vmem((group, rows, wide)),
        ]
        + rings
        + turned
        + [
            pltpu.SemaphoreType.DMA((2 * group + blocks,)),
            pltpu.SemaphoreType.DMA((2 * group + blocks,)),
            pltpu.SemaphoreType.DMA((5 + 2 * x.shape[0],)),
            pltpu.SemaphoreType.DMA((6 * max(2, xs, zs),)),
            pltpu.SemaphoreType.DMA((6,)),
        ],
        compiler_params=params(collective_id=3 * branch + 2, has_side_effects=True),
        cost_estimate=pl.CostEstimate(
            flops=8 * rows * width * width + 12 * rows * width * hidden,
            bytes_accessed=4 * width * width + 8 * width * hidden,
            transcendentals=rows * hidden,
        ),
        name="feed_forward",
    )(ctx, x, g, slope, ow, uw, dw, ob[None], gain[None], shift[None], ub[None], db[None])


def partner(axis, mask):
    return [(i, i ^ mask) for i in range(lax.axis_size(axis))]


def exchange(axis, blocks):
    grid = Grid()
    out = [blocks[0]]
    for r in range(1, grid.size[axis]):
        name, mask = ("dp", 2 * r) if axis == "y" else ("seq", grid.mask(axis, r))
        out.append(lax.ppermute(blocks[r], name, partner(name, mask)))
    return out


def item_counts(ys, xs, zs):
    return (ys - 1) + 5, (xs - 1) + 5, 7, 7, (zs - 1) + 4


def tail_kernel(wide, *refs):
    grid = Grid()
    group, ys, xs, zs = grid.seq, grid.y, grid.x, grid.z
    refs = list(refs)

    def take(n):
        out = refs[:n]
        del refs[:n]
        return out

    back, weight, normed_ref, x_hbm, mg_hbm, gain_ref, early_ref = take(7)
    down_in, down_rest = take(ys), take(ys)
    up_in, up_rest = take(xs), take(ys)
    out_in = take(zs)
    tg_ref, project_ref, down_ref, up_ref, out_ref, vec_ref = take(6)
    landed, w_s, x_s, mg_s, acc, turned, order = take(7)
    send_a, send_b, keep_a, keep_b, pair_a, pair_b = take(6)
    got_a1, got_b1, mid_a, mid_b, got_a2, got_b2, z_a, z_b, got_za, got_zb = take(10)
    items = [take(count) for count in item_counts(ys, xs, zs)]
    vec_s, vec_g = take(2)
    send_sem, recv_sem, load_sem = take(3)

    me, dp = lax.axis_index("seq"), lax.axis_index("dp")
    core, row = dp % 2, dp // 2
    links = Links(send_sem, recv_sem)
    tokens, width = normed_ref.shape
    share = project_ref.shape[1]
    partner_core = {"dp": flip(dp, 1)}
    loads = []

    def load(src, dst):
        copy = pltpu.make_async_copy(src, dst, load_sem.at[len(loads)])
        copy.start()
        loads.append(copy)
        return copy

    greet(range(1, group), [1] + [2 * r for r in range(1, ys)])

    first = links.reserve(group)
    for m in range(1, group):
        links.start(back.at[m], landed.at[m], first + m, first + m, {"seq": flip(me, m)})
    own = load(back.at[0], landed.at[0])
    down_a, up_a, down_b, up_b, out_a = items
    loaded = [
        [load(src, dst) for src, dst in zip(up_in, [up_a[xs - 1]] + up_a[: xs - 1])],
        [load(src, dst) for src, dst in zip(down_in, [down_a[ys - 1]] + down_a[: ys - 1])],
        [load(src, dst) for src, dst in zip(out_in, [out_a[zs - 1]] + out_a[: zs - 1])],
        [load(src, down_b[0].at[o]) for o, src in enumerate(down_rest)],
        [load(src, up_b[0].at[o]) for o, src in enumerate(up_rest)],
    ]

    cap = tokens // x_hbm.shape[0]
    own_x = [load(x_hbm.at[r, pl.ds(0, cap)], x_s.at[pl.ds(r * cap, cap)]) for r in range(x_hbm.shape[0])]
    own_mg = load(mg_hbm, mg_s)
    ahead = w_s.shape[0]
    weight_first = len(loads)

    def weight_copies(m):
        source = flip(me, m, group)
        return [
            pltpu.make_async_copy(
                weight_view(weight, part, source, width, wide),
                w_s.at[m % ahead, part],
                load_sem.at[weight_first + 3 * m + part],
            )
            for part in range(3)
        ]

    for m in range(ahead):
        for copy in weight_copies(m):
            copy.start()

    def summed(axis, block, got):
        return Summed(links, grid, axis, block, got)

    up_a1 = summed("y", up_a[xs - 1], up_a[xs])
    up_a2 = LineSum(links, grid, *up_a[xs + 1 :])
    down_a1 = summed("x", down_a[ys - 1], down_a[ys])
    down_a2 = LineSum(links, grid, *down_a[ys + 1 :])
    down_b1, down_b2 = summed("y", down_b[0], down_b[1]), summed("x", down_b[2], down_b[3])
    down_b3 = LineSum(links, grid, *down_b[4:])
    up_b1, up_b2 = summed("y", up_b[0], up_b[1]), summed("x", up_b[2], up_b[3])
    up_b3 = LineSum(links, grid, *up_b[4:])
    out_1 = summed("y", out_a[zs - 1], out_a[zs])
    out_2 = summed("x", out_a[zs + 1], out_a[zs + 2])
    lines = (up_a2, down_a2, up_b3, down_b3)
    for copies in loaded[3:]:
        for copy in copies:
            copy.wait()
    down_b1.send()
    up_b1.send()
    for copies, item, count, stage in (
        (loaded[0], up_a, xs, up_a1),
        (loaded[1], down_a, ys, down_a1),
        (loaded[2], out_a, zs, out_1),
    ):
        for copy in copies:
            copy.wait()
        add_into(item[count - 1], item[: count - 1])
        stage.send()

    for k in range(0, width, 256):
        turned[k : k + 256, :] = normed_ref[:, k : k + 256].astype(F32).T
    for c in range(2):
        for o in range(ys):

            def place(s, c=c, o=o):
                there = (flip(row, o) * 2 + flip(core, c)) * group + flip(me, s, group)
                rows = turned[pl.ds(pl.multiple_of(there * share, share), share), :]
                order[c, o, s % xs, s // xs] = rows.astype(BF16)

            loop(0, group, place)
    half = ys * group * share
    acc[...] = jnp.zeros_like(acc)
    vec_s[0] = early_ref[...]
    own.wait()

    pair_first = links.reserve(2 * group)
    a1 = SlotSum(links, grid, "y", group, keep_a, got_a1)
    a2 = SlotSum(links, grid, "x", group, mid_a, got_a2)
    b1 = SlotSum(links, grid, "x", group, keep_b, got_b1, inner=True)
    b2 = SlotSum(links, grid, "y", group, mid_b, got_b2)
    cut = 2 * wide

    def multiply(m):
        source = flip(me, m, group)

        @pl.when(m > 0)
        def _():
            links.arrived(landed.at[m], first + m, {"seq": source})

        for k, (send, keep, pair, cols) in enumerate(
            (
                (send_a, keep_a, pair_a, slice(0, cut)),
                (send_b, keep_b, pair_b, slice(cut, 3 * wide)),
            )
        ):
            grad = landed[m, :, cols]
            left = order[1].reshape(half, tokens)
            send[m] = dot(left, grad).reshape(send.shape[1:]).astype(BF16)
            slot = pair_first + 2 * m + k
            links.start(send.at[m], pair.at[m], slot, slot, partner_core, later=False)
            left = order[0].reshape(half, tokens)
            keep[m] = dot(left, grad).reshape(keep.shape[1:]).astype(BF16)
        block = landed[m]
        for copy in weight_copies(m):
            copy.wait()
        pieces = [w_s[m % ahead, part] for part in range(3)]
        acc[...] += dot(block, jnp.concatenate(pieces, axis=1), NT)

        @pl.when(m + ahead < group)
        def _():
            for copy in weight_copies(m + ahead):
                copy.start()

        sums = jnp.sum(block.astype(F32), axis=0, keepdims=True)
        vec_s[0, pl.ds(VECTORS + source, 1), : 3 * wide] = sums

    def paired(m):
        for k, (keep, pair, nxt) in enumerate(((keep_a, pair_a, a1), (keep_b, pair_b, b1))):
            links.arrived(pair.at[m], pair_first + 2 * m + k, partner_core)
            keep[m] = total_of(keep[m], [pair[m]], BF16)
            nxt.send(m)

    def second(m):
        mid_a[m] = a1.receive(m).astype(BF16)
        a2.send(m)
        mid_b[m] = b1.receive(m).astype(BF16)
        b2.send(m)

    def third(m):
        for block, stage in ((z_a, a2), (z_b, b2)):
            total = stage.receive(m).astype(BF16)
            for z in range(zs):
                block[z, m] = total[z]

    def input_grads():
        for copy in own_x:
            copy.wait()
        own_mg.wait()
        n, rs = centre_rows(x_s[...].astype(F32))
        n1 = acc[...]
        grad = mg_s[...] + norm_back(n1, n, rs, gain_ref[...])
        for r in range(tg_ref.shape[0]):
            put_rows(tg_ref, r, cap, grad[r * cap : (r + 1) * cap])
        vec_s[0, 0:1, :] = jnp.sum(n1 * n, axis=0, keepdims=True)
        vec_s[0, 1:2, :] = jnp.sum(n1, axis=0, keepdims=True)

    vec_first = links.reserve(1 + (ys - 1) + (xs - 1) + (zs - 1))
    hops = [[partner_core]]
    for axis in ("y", "x", "z"):
        hops.append([grid.device(axis, r) for r in range(1, grid.size[axis])])

    def vec_send(k):
        at = vec_first + sum(len(h) for h in hops[:k])
        for r, device in enumerate(hops[k]):
            links.start(vec_s.at[k], vec_g.at[at + r - vec_first], at + r, at + r, device)

    def vec_receive(k):
        at = vec_first + sum(len(h) for h in hops[:k])
        got = []
        for r, device in enumerate(hops[k]):
            links.arrived(vec_g.at[at + r - vec_first], at + r, device)
            got.append(vec_g[at + r - vec_first])
        total = total_of(vec_s[k], got, F32)
        if k + 1 < len(hops):
            vec_s[k + 1] = total
            vec_send(k + 1)
        else:
            vec_ref[...] = total

    def multiply_next(m):
        multiply(m)

        @pl.when(m > 0)
        def _():
            paired(m - 1)

    loop(0, group // 2 + 1, multiply_next)
    down_b1.receive(down_b[2])
    down_b2.send()
    loop(group // 2 + 1, group, multiply_next)
    paired(group - 1)
    down_a1.receive(down_a[ys + 1])
    down_a2.hop(0)
    up_b1.receive(up_b[2])
    up_b2.send()
    up_a1.receive(up_a[xs + 1])
    up_a2.hop(0)
    input_grads()
    vec_send(0)
    out_1.receive(out_a[zs + 1])
    out_2.send()
    down_b2.receive(down_b[4])
    down_b3.hop(0)
    for k in range(1, zs - 1):
        down_a2.hop(k)
        up_a2.hop(k)
    vec_receive(0)
    loop(0, group // 2, second)
    for k in range(1, zs - 1):
        down_b3.hop(k)
    loop(group // 2, group, second)
    vec_receive(1)
    up_b2.receive(up_b[4])
    up_b3.hop(0)
    loop(0, group // 2, third)
    for k in range(1, zs - 1):
        up_b3.hop(k)
    loop(group // 2, group, third)

    z_first = links.reserve(2 * (zs - 1))
    for r in range(1, zs):
        for k, (block, got) in enumerate(((z_a, got_za), (z_b, got_zb))):
            slot = z_first + 2 * (r - 1) + k
            links.start(block.at[r], got.at[r - 1], slot, slot, grid.device("z", r))
    vec_receive(2)
    cut_down, cut_up = early_cols(down_ref.shape[1], 0), early_cols(up_ref.shape[1], 0)
    out_2.receive_last(out_ref)
    up_a2.finish(up_ref, slice(0, cut_up))
    down_a2.finish(down_ref, slice(0, cut_down))
    up_b3.finish(up_ref, slice(cut_up, up_ref.shape[1]))
    down_b3.finish(down_ref, slice(cut_down, down_ref.shape[1]))
    vec_receive(3)
    for r in range(1, zs):
        for k, got in enumerate((got_za, got_zb)):
            links.arrived(got.at[r - 1], z_first + 2 * (r - 1) + k, grid.device("z", r))

    def share_of(m):
        source = flip(me, m, group)
        for block, got, cols in (
            (z_a, got_za, slice(0, cut)),
            (z_b, got_zb, slice(cut, 3 * wide)),
        ):
            others = [got[r - 1, flip(m, grid.mask("z", r), group)] for r in range(1, zs)]
            project_ref[source, :, cols] = total_of(block[0, m], others, F32)

    loop(0, group, share_of)

    def drain(m):
        for k, send in enumerate((send_a, send_b)):
            links.left(send.at[m], pair_first + 2 * m + k, partner_core)
        for stage in (a1, a2, b1, b2):
            stage.drain(m)

    loop(0, group, drain)
    links.drain()


def tail(branch, back, normed, weight, x, mid_grad, gain, early, down, up, out):
    grid = Grid()
    group, ys, xs, zs = grid.seq, grid.y, grid.x, grid.z
    rows, width = normed.shape
    wide = width // group
    shape = jax.ShapeDtypeStruct
    any_place = pl.BlockSpec(memory_space=pl.ANY)
    here = any_spec()
    share = width // (grid.dp * grid.seq)
    (down, down_rest), (up, up_rest) = down, up
    down_block, up_block, out_block = down[0].shape, up[0].shape, out[0].shape
    vmem = lambda dims, kind=BF16: pltpu.VMEM(tuple(dims), kind)
    a_full, b_full = (share, 2 * wide), (share, wide)
    copies = (
        group
        + 2 * group
        + 2 * group * (ys - 1)
        + 2 * group * (xs - 1)
        + 4 * (xs - 1)
        + 4 * (ys - 1)
        + 8 * zs
        + (1 + (ys - 1) + (xs - 1) + (zs - 1))
        + 2 * (zs - 1)
    )
    hops = 1 + (ys - 1) + (xs - 1) + (zs - 1)
    scratch = (
        [
            vmem((group, rows, 3 * wide)),
            vmem((min(4, group), 3, width, wide)),
            vmem((rows, width)),
            vmem((rows, width), F32),
            vmem((rows, width), F32),
            vmem((width, rows), F32),
            vmem((2, ys, xs, zs, share, rows)),
        ]
        + [vmem((group, ys, xs, zs) + a_full), vmem((group, ys, xs, zs) + b_full)] * 3
        + [
            vmem((group, ys - 1, xs, zs) + a_full),
            vmem((group, xs - 1, ys, zs) + b_full),
            vmem((group, xs, zs) + a_full),
            vmem((group, ys, zs) + b_full),
            vmem((group, xs - 1, zs) + a_full),
            vmem((group, ys - 1, zs) + b_full),
            vmem((zs, group) + a_full),
            vmem((zs, group) + b_full),
            vmem((zs - 1, group) + a_full),
            vmem((zs - 1, group) + b_full),
        ]
        + [vmem(down_block)] * ys
        + [vmem((xs - 1,) + down_block[1:])]
        + [vmem(down_block[1:])] * 3
        + [vmem(up_block)] * xs
        + [vmem((ys - 1,) + up_block[1:])]
        + [vmem(up_block[1:])] * 3
        + [
            vmem((ys,) + down_rest[0].shape),
            vmem((ys - 1,) + down_rest[0].shape),
            vmem(down_rest[0].shape),
            vmem((xs - 1,) + down_rest[0].shape[1:]),
        ]
        + [vmem(down_rest[0].shape[1:])] * 3
        + [
            vmem((ys,) + up_rest[0].shape),
            vmem((ys - 1,) + up_rest[0].shape),
            vmem(up_rest[0].shape),
            vmem((xs - 1,) + up_rest[0].shape[1:]),
        ]
        + [vmem(up_rest[0].shape[1:])] * 3
        + [vmem(out_block)] * zs
        + [
            vmem((ys - 1,) + out_block[1:]),
            vmem(out_block[1:]),
            vmem((xs - 1,) + out_block[2:]),
        ]
        + [
            vmem((4,) + early.shape, F32),
            vmem((hops,) + early.shape, F32),
            pltpu.SemaphoreType.DMA((copies,)),
            pltpu.SemaphoreType.DMA((copies,)),
            pltpu.SemaphoreType.DMA((2 + x.shape[0] + 3 * ys + xs + zs + 3 * group,)),
        ]
    )
    return pl.pallas_call(
        functools.partial(tail_kernel, wide),
        in_specs=[any_place, any_place, here, any_place, any_place, here, here]
        + [any_place] * (3 * ys + xs + zs),
        out_specs=[here] * 6,
        out_shape=[
            shape(x.shape, BF16),
            shape((group, share, 3 * wide), F32),
            shape((down_block[2], width), F32),
            shape((up_block[2], up_block[3] + up_rest[0].shape[3]), F32),
            shape(out_block[2:], F32),
            shape(early.shape, F32),
        ],
        scratch_shapes=scratch,
        compiler_params=params(collective_id=3 * branch + 3, has_side_effects=True),
        cost_estimate=pl.CostEstimate(
            flops=12 * rows * width * width, bytes_accessed=2**25, transcendentals=0
        ),
        name="tail",
    )(back, weight, normed, x, mid_grad, gain[None], early, *down, *down_rest, *up, *up_rest, *out)


def prepare_kernel(exit_ref, offsets, limit, tokens, upstream, x_ref, g_ref, pick_ref, ids_ref, most_ref, *scratch):
    rank_s, live_s, mine_s, got, send_sem, recv_sem = scratch
    rows, shard, _ = tokens.shape
    group = ids_ref.shape[1]
    docs = offsets.shape[1]
    dp, me = lax.axis_index("dp"), lax.axis_index("seq")
    others = lax.axis_size("dp") - 1
    links = Links(send_sem, recv_sem)
    for r in range(rows):
        for s in range(group):
            live = exit_ref[r : r + 1, s * shard : (s + 1) * shard] > limit[0]
            live_s[r * group + s : r * group + s + 1, :] = jnp.where(live, 1.0, 0.0)
    before = lax.broadcasted_iota(jnp.int32, (shard, shard), 0)
    after = lax.broadcasted_iota(jnp.int32, (shard, shard), 1)
    ones = jnp.where(before <= after, 1.0, 0.0).astype(BF16)
    rank = dot(live_s[...].astype(BF16), ones)
    rank_s[...] = jnp.where(live_s[...] > 0.0, rank - 1.0, -1.0)
    mine_s[...] = jnp.broadcast_to(jnp.max(rank), mine_s.shape)
    greet([], range(1, others + 1))
    for m in range(1, others + 1):
        links.start(mine_s, got.at[m - 1], m - 1, m - 1, {"dp": flip(dp, m)})
    slot = before.astype(F32)
    for r in range(rows):
        here = rank_s[pl.ds(r * group + me, 1), :]
        pick = jnp.where(slot == here, 1.0, 0.0).astype(BF16)
        pick_ref[r] = pick
        x_ref[r] = dot(pick, tokens[r]).astype(BF16)
        g_ref[r] = dot(pick, upstream[r]).astype(BF16)
    seat = lax.broadcasted_iota(jnp.int32, (group, shard), 1)
    place = seat + shard * lax.broadcasted_iota(jnp.int32, (group, shard), 0)
    for r in range(rows):
        live = live_s[r * group : (r + 1) * group, :]
        ids = jnp.ones((group, shard), F32)
        for j in range(1, docs):
            ahead = jnp.where(place < offsets[r, j], live, 0.0)
            ahead = jnp.sum(ahead, axis=1, keepdims=True)
            ids = ids + jnp.where(seat.astype(F32) >= ahead, 1.0, 0.0)
        used = jnp.sum(live, axis=1, keepdims=True)
        ids = jnp.where(seat.astype(F32) < used, ids, 0.0)
        for s in range(group):
            ids_ref[r, s] = ids[s : s + 1]
    most = mine_s[...]
    for m in range(1, others + 1):
        links.arrived(got.at[m - 1], m - 1, {"dp": flip(dp, m)})
        most = jnp.maximum(most, got[m - 1])
    most_ref[...] = most
    links.drain()


def prepare(exit_layers, doc_offsets, layer_index, tokens, upstream):
    others = lax.axis_size("dp") - 1
    group = lax.axis_size("seq")
    rows, shard, width = tokens.shape
    shape = jax.ShapeDtypeStruct
    here, scalar = any_spec(), smem()
    return pl.pallas_call(
        prepare_kernel,
        in_specs=[here, scalar, scalar, here, here],
        out_specs=[here] * 5,
        out_shape=[
            shape(tokens.shape, BF16),
            shape(tokens.shape, BF16),
            shape((rows, shard, shard), BF16),
            shape((rows, group, 1, shard), F32),
            shape((8, 128), F32),
        ],
        scratch_shapes=[
            pltpu.VMEM((rows * group, shard), F32),
            pltpu.VMEM((rows * group, shard), F32),
            pltpu.VMEM((8, 128), F32),
            pltpu.VMEM((others, 8, 128), F32),
            pltpu.SemaphoreType.DMA((others,)),
            pltpu.SemaphoreType.DMA((others,)),
        ],
        compiler_params=params(collective_id=0, has_side_effects=True),
        name="prepare",
    )(exit_layers, doc_offsets, layer_index, tokens, upstream)


def layer(
    branch,
    cap,
    docs,
    x,
    g,
    ids,
    first_gain,
    first_shift,
    project_weight,
    query_bias,
    value_bias,
    output_weight,
    output_bias,
    second_gain,
    second_shift,
    up_weight,
    up_bias,
    down_weight,
    down_bias,
):
    group = lax.axis_size("seq")
    rows, shard, width = x.shape
    wide = width // group
    heads = wide // HEAD_DIM
    me = lax.axis_index("seq").astype(jnp.int32)
    tiles = pl.cdiv(group * cap, TILE)
    ids = ids[:, :, 0, :cap].reshape(rows, group * cap)
    ids = jnp.pad(ids, ((0, 0), (0, tiles * TILE - group * cap))).reshape(rows, tiles, 1, TILE)
    last = jnp.max(ids[:, :, 0], axis=2)
    first = jnp.min(jnp.where(ids == 0, docs + 1, ids)[:, :, 0], axis=2)
    number = jnp.arange(tiles, dtype=jnp.int32)
    needed = (last[:, None, :] >= first[:, :, None]) & (number < number[:, None])
    low = jnp.min(jnp.where(needed, number, number[:, None]), axis=2) // 2
    scalars = jnp.concatenate([me[None], low.reshape(-1)])
    biases = jnp.stack([query_bias, jnp.zeros_like(query_bias), value_bias])
    bias_parts = biases.reshape(3, group, wide).transpose(1, 0, 2).reshape(group, 1, 3 * wide)

    weight = split_weight(project_weight, group)
    normed, head_parts, context, ctx_parts, lse, slope = project_attend(
        branch, cap, docs, x, g, first_gain, first_shift, weight, bias_parts, down_weight, ids
    )
    grad_parts, result, middle_grad, early, *halves = feed_forward(
        branch,
        cap,
        ctx_parts,
        x,
        g,
        slope,
        output_weight,
        output_bias,
        second_gain,
        second_shift,
        up_weight,
        up_bias,
        down_weight,
        down_bias,
    )
    ys, xs = Grid().y, Grid().x
    down, up, out = halves[: 2 * ys], halves[2 * ys : 3 * ys + xs], halves[3 * ys + xs : -3]
    down_parts = exchange("y", down[0::2]), down[1::2]
    up_parts = exchange("x", up[:xs]), up[xs:]
    out_parts = exchange("z", out)
    back = attend_back(
        scalars, head_parts, context, grad_parts, ids, lse, docs, cap, heads
    )
    token_grad, project_share, down_share, up_share, out_share, sums = tail(
        branch, back, normed, weight, x, middle_grad, first_gain, early, down_parts, up_parts, out_parts
    )
    return (result, token_grad, project_share, out_share, up_share, down_share, sums)


CAPS = (12, 11, 13, 10, 16)


def per_device(tokens, *args):
    *weights, doc_offsets, exit_layers, layer_index, upstream = args
    rows, shard, width = tokens.shape
    group = lax.axis_size("seq")
    wide = width // group
    docs = doc_offsets.shape[1]
    x, g, pick, ids, most = prepare(exit_layers, doc_offsets, layer_index, tokens, upstream)
    caps = list(dict.fromkeys(pl.cdiv(shard * k, 256) * 16 for k in CAPS))
    count = jnp.maximum(most[0, 0], 1.0)
    branch = sum(
        jnp.where((count <= cap) & (count > max([0] + [c for c in caps if c < cap])), k, 0)
        for k, cap in enumerate(caps)
    )
    steps = [functools.partial(layer, k, cap, docs) for k, cap in enumerate(caps)]
    result, token_grad, project_share, out_share, up_share, down_share, sums = lax.switch(
        branch, steps, x, g, ids, *weights
    )
    me = lax.axis_index("seq").astype(jnp.int32)
    live = lax.dynamic_slice_in_dim(exit_layers, me * shard, shard, 1) > layer_index[0]

    def unpack(packed, values):
        spread = jnp.einsum("rct,rcd->rtd", pick, packed, preferred_element_type=F32)
        return jnp.where(live[:, :, None], spread.astype(BF16), values)

    project_share = project_share.reshape(group, -1, 3, wide).transpose(1, 2, 0, 3)
    devices = lax.axis_size("dp") * group
    index = lax.axis_index("dp").astype(jnp.int32) * group + me
    part = width // devices
    singles = lax.dynamic_slice(sums, (0, index * part), (6, part))
    high = up_share.shape[1] // devices
    at = index * high
    up_bias_share = lax.dynamic_slice(sums, (6 + at // width, at % width), (1, high))[0]
    at = index * part
    by_part = [
        lax.dynamic_slice(sums, (VECTORS + at // wide, k * wide + at % wide), (1, part))[0]
        for k in range(3)
    ]
    return (
        unpack(result, tokens),
        unpack(token_grad, upstream),
        singles[0],
        singles[1],
        project_share.reshape(-1, 3 * width),
        by_part[0],
        by_part[2],
        out_share,
        singles[2],
        singles[3],
        singles[4],
        up_share,
        up_bias_share,
        down_share,
        singles[5],
    )


def solution(mesh):
    rows = P("dp", "seq", None)
    shares = P(("dp", "seq"))
    wide_shares = P(("dp", "seq"), None)
    in_specs = (rows,) + (P(),) * 13 + (P("dp", None), P("dp", None), P(), rows)
    out_specs = (
        rows,
        rows,
        shares,
        shares,
        wide_shares,
        shares,
        shares,
        wide_shares,
        shares,
        shares,
        shares,
        wide_shares,
        shares,
        wide_shares,
        shares,
    )
    return jax.shard_map(
        per_device, mesh=mesh, in_specs=in_specs, out_specs=out_specs, check_vma=False
    )
```

```python
import functools
import math

import jax
import jax.numpy as jnp
from jax import lax
from jax.experimental import pallas as pl
from jax.experimental.pallas import tpu as pltpu
from jax.sharding import PartitionSpec as P

HEAD_DIM = 64
SCALE = HEAD_DIM**-0.5
TILE = 256
PAIR = 2 * TILE
NEG = -1e30
EPS = 1e-05
VMEM_LIMIT = 60 * 2**20
F32 = jnp.float32
BF16 = jnp.bfloat16

NT = (((1,), (1,)), ((), ()))
NN = (((1,), (0,)), ((), ()))
TN = (((0,), (0,)), ((), ()))


def dot(a, b, dims=NN):
    return lax.dot_general(a, b, dims, preferred_element_type=F32)


def any_spec():
    return pl.BlockSpec(memory_space=pltpu.VMEM)


def params(**kw):
    return pltpu.CompilerParams(vmem_limit_bytes=VMEM_LIMIT, **kw)


def centre_rows(x):
    centred = x - jnp.mean(x, axis=-1, keepdims=True)
    spread = jnp.mean(centred * centred, axis=-1, keepdims=True)
    rs = lax.rsqrt(spread + EPS)
    return centred * rs, rs


def smem():
    return pl.BlockSpec(memory_space=pltpu.SMEM)


def flip(index, mask, size=64):
    bit = 1
    out = index
    while bit < size:
        if not isinstance(mask, int):
            ours, theirs = (index // bit) % 2, (mask // bit) % 2
            out = out + bit * (theirs - 2 * ours * theirs)
        elif mask & bit:
            out = out + bit * (1 - 2 * ((index // bit) % 2))
        bit *= 2
    return out


def loop(first, last, body):
    def turn(i, _):
        body(i)
        return 0

    lax.fori_loop(first, last, turn, 0)


class Links:
    def __init__(self, send_sem, recv_sem):
        self.send_sem, self.recv_sem, self.used, self.sent = send_sem, recv_sem, 0, []

    def reserve(self, count):
        first, self.used = self.used, self.used + count
        return first

    def start(self, src, dst, slot, there, device, later=True):
        copy = pltpu.make_async_remote_copy(
            src_ref=src,
            dst_ref=dst,
            send_sem=self.send_sem.at[slot],
            recv_sem=self.recv_sem.at[there],
            device_id=device,
            device_id_type=pl.DeviceIdType.MESH,
        )
        copy.start()
        if later:
            self.sent.append(copy)

    def left(self, src, slot, device):
        pltpu.make_async_remote_copy(
            src_ref=src,
            dst_ref=src,
            send_sem=self.send_sem.at[slot],
            recv_sem=self.recv_sem.at[slot],
            device_id=device,
            device_id_type=pl.DeviceIdType.MESH,
        ).wait_send()

    def arrived(self, ref, slot, device):
        pltpu.make_async_remote_copy(
            src_ref=ref,
            dst_ref=ref,
            send_sem=self.send_sem.at[slot],
            recv_sem=self.recv_sem.at[slot],
            device_id=device,
            device_id_type=pl.DeviceIdType.MESH,
        ).wait_recv()

    def drain(self):
        for copy in self.sent:
            copy.wait_send()


def greet(seq_masks, dp_masks):
    me, dp = lax.axis_index("seq"), lax.axis_index("dp")
    barrier = pltpu.get_barrier_semaphore()
    others = [{"seq": flip(me, m)} for m in seq_masks] + [{"dp": flip(dp, m)} for m in dp_masks]
    for device in others:
        pl.semaphore_signal(barrier, inc=1, device_id=device, device_id_type=pl.DeviceIdType.MESH)
    pl.semaphore_wait(barrier, len(others))


class Grid:
    def __init__(self):
        self.dp, self.seq = lax.axis_size("dp"), lax.axis_size("seq")
        self.y = self.dp // 2
        self.x = min(self.y, self.seq)
        self.z = self.seq // self.x
        self.size = {"y": self.y, "x": self.x, "z": self.z}

    def device(self, axis, r):
        me, dp = lax.axis_index("seq"), lax.axis_index("dp")
        if axis == "y":
            return {"dp": flip(dp, 2 * r)}
        return {"seq": flip(me, self.mask(axis, r))}

    def mask(self, axis, r):
        return {"y": 0, "x": r, "z": r * self.x}[axis]


def row_copies(slots, packed, sem, first):
    rows = slots.shape[0]
    cap = packed.shape[0] // rows
    return [
        pltpu.make_async_copy(
            slots.at[r, pl.ds(0, cap)], packed.at[pl.ds(r * cap, cap)], sem.at[first + r]
        )
        for r in range(rows)
    ]


def put_rows(slots, r, cap, values):
    slots[r, :cap] = values.astype(slots.dtype)
    if cap < slots.shape[1]:
        slots[r, cap:] = jnp.zeros((slots.shape[1] - cap, slots.shape[2]), slots.dtype)


def total_of(first, others, kind):
    total = first.astype(F32)
    for other in others:
        total = total + other.astype(F32)
    return total.astype(kind)


def add_into(total, others):
    inner = total.shape[1]

    def one(k):
        i, j = k // inner, k % inner
        total[i, j] = total_of(total[i, j], [other[i, j] for other in others], total.dtype)

    loop(0, total.shape[0] * inner, one)


class Summed:
    def __init__(self, links, grid, axis, block, got):
        self.links, self.grid, self.axis, self.block, self.got = links, grid, axis, block, got
        self.size = grid.size[axis]
        self.slot = links.reserve(self.size - 1)

    def send(self):
        for r in range(1, self.size):
            slot = self.slot + r - 1
            self.links.start(
                self.block.at[r], self.got.at[r - 1], slot, slot, self.grid.device(self.axis, r)
            )

    def receive(self, store, kind=BF16):
        for r in range(1, self.size):
            self.links.arrived(
                self.got.at[r - 1], self.slot + r - 1, self.grid.device(self.axis, r)
            )
        inner = store.shape[1]

        def one(k):
            i, j = k // inner, k % inner
            others = [self.got[r - 1, i, j] for r in range(1, self.size)]
            store[i, j] = total_of(self.block[0, i, j], others, kind)

        if len(store.shape) == 4:
            loop(0, store.shape[0] * inner, one)
        else:
            store[...] = total_of(self.block[0], [self.got[r - 1] for r in range(1, self.size)], kind)

    def receive_last(self, store):
        for r in range(1, self.size):
            self.links.arrived(
                self.got.at[r - 1], self.slot + r - 1, self.grid.device(self.axis, r)
            )
        store[...] = total_of(self.block[0], [self.got[r - 1] for r in range(1, self.size)], F32)


class LineSum:
    def __init__(self, links, grid, block, right, left):
        self.links, self.grid, self.block = links, grid, block
        self.got = {1: right, -1: left}
        self.size = grid.z
        self.place = lax.axis_index("seq") // grid.x
        self.slot = {1: links.reserve(self.size), -1: links.reserve(self.size)}

    def next(self, way):
        return {"seq": lax.axis_index("seq") + way * self.grid.x}

    def copy(self, way, goal, src):
        slot = self.slot[way] + goal
        return pltpu.make_async_remote_copy(
            src_ref=src,
            dst_ref=self.got[way].at[goal],
            send_sem=self.links.send_sem.at[slot],
            recv_sem=self.links.recv_sem.at[slot],
            device_id=self.next(way),
            device_id_type=pl.DeviceIdType.MESH,
        )

    def source(self, way, goal, first):
        if first:
            return self.block.at[flip(self.place, goal)]
        return self.got[way].at[goal]

    def hop(self, k):
        for way, at in ((1, k), (-1, self.size - 1 - k)):
            goals = range(self.size - 1, at, -1) if way == 1 else range(at)

            @pl.when(self.place == at)
            def _(way=way, goals=goals):
                for goal in goals:
                    if k:
                        self.arrived(way, goal)
                        got = self.got[way]
                        own = self.block.at[flip(self.place, goal)]
                        for i in range(got.shape[1]):
                            got[goal, i] = total_of(own[i], [got[goal, i]], BF16)
                    self.copy(way, goal, self.source(way, goal, k == 0)).start()

    def arrived(self, way, goal):
        self.copy(way, goal, self.got[way].at[goal]).wait_recv()

    def finish(self, store, cols):
        store[:, cols] = self.block[0].astype(F32)
        for way, limit in ((1, self.place > 0), (-1, self.place < self.size - 1)):

            @pl.when(limit)
            def _(way=way):
                self.arrived(way, self.place)
                store[:, cols] = store[:, cols] + self.got[way][self.place].astype(F32)

        for way in (1, -1):
            for goal in range(self.size):

                @pl.when(self.place < goal if way == 1 else self.place > goal)
                def _(way=way, goal=goal):
                    self.copy(way, goal, self.got[way].at[goal]).wait_send()


class SlotSum:
    def __init__(self, links, grid, axis, slots, block, got, inner=False):
        self.links, self.grid, self.axis, self.got = links, grid, axis, got
        self.block = (lambda m, r: block.at[m, :, r]) if inner else (lambda m, r: block.at[m, r])
        self.size, self.slots = grid.size[axis], slots
        self.first = links.reserve(slots * (self.size - 1))

    def id(self, m, r):
        return self.first + m * (self.size - 1) + r - 1

    def send(self, m):
        for r in range(1, self.size):
            there = flip(m, self.grid.mask(self.axis, r), self.slots)
            self.links.start(
                self.block(m, r),
                self.got.at[there, r - 1],
                self.id(m, r),
                self.id(there, r),
                self.grid.device(self.axis, r),
                later=False,
            )

    def receive(self, m):
        for r in range(1, self.size):
            self.links.arrived(
                self.got.at[m, r - 1], self.id(m, r), self.grid.device(self.axis, r)
            )
        return total_of(
            self.block(m, 0)[...], [self.got[m, r - 1] for r in range(1, self.size)], F32
        )

    def drain(self, m):
        for r in range(1, self.size):
            self.links.left(self.block(m, r), self.id(m, r), self.grid.device(self.axis, r))


def split_weight(weight, group):
    width = weight.shape[0]
    wide = width // group
    if wide % 128 == 0:
        return weight
    return weight.reshape(width, 3, group, wide).transpose(1, 2, 0, 3)


def weight_view(weight, part, source, width, wide):
    if wide % 128 == 0:
        return weight.at[:, pl.ds(pl.multiple_of(part * width + source * wide, 128), wide)]
    return weight.at[part, source]


def only_head(block, head, heads):
    if heads == 1:
        return block
    lane = lax.broadcasted_iota(jnp.int32, block.shape, 1)
    return jnp.where(lane // HEAD_DIM == head, block, jnp.zeros_like(block))


def transposed(block):
    return block.astype(F32).T.astype(BF16)


def causal(size, offset):
    key = lax.broadcasted_iota(jnp.int32, (size, TILE), 0)
    query = lax.broadcasted_iota(jnp.int32, (size, TILE), 1)
    return key <= query + offset


def sweep(tiles, low_of, start, step, finish):
    def before(i, whole_blocks):
        low = low_of(i)
        return lax.fori_loop(
            low, whole_blocks, lambda b, c: step(i, b * PAIR, PAIR, None, c), start(i)
        )

    def even(i, half):
        finish(i, step(i, i * TILE, TILE, 0, before(i, half)))

    def odd(i, half):
        finish(i, step(i, half * PAIR, PAIR, TILE, before(i, half)))

    def both(half, _):
        even(2 * half, half)
        odd(2 * half + 1, half)
        return 0

    lax.fori_loop(0, tiles // 2, both, 0)
    if tiles % 2:
        even(tiles - 1, tiles // 2)


def span(at, size):
    return pl.ds(at if isinstance(at, int) else pl.multiple_of(at, TILE), size)


def blank_rest(used, *arrays):
    if used < arrays[0].shape[0]:
        for array in arrays:
            array[used:, :] = jnp.zeros((array.shape[0] - used, array.shape[1]), array.dtype)


def load_heads(me, cap, parts, q_s, k_s, v_s):
    wide = v_s.shape[1]
    blank_rest(parts.shape[0] * cap, q_s, k_s, v_s)
    for m in range(parts.shape[0]):
        here = pl.ds(pl.multiple_of((me ^ m) * cap, math.gcd(cap, 128)), cap)
        q_s[here, :] = parts[m, :, :wide] * SCALE
        k_s[here, :wide] = parts[m, :, wide : 2 * wide]
        v_s[here, :] = parts[m, :, 2 * wide :]


def documents(ids, docs):
    row = lax.broadcasted_iota(jnp.int32, (128, TILE), 0).astype(F32)
    unit = row + 1.0 == ids
    query = jnp.where(unit, 1.0, 0.0).astype(BF16)
    return query, jnp.where(unit | (row >= docs), 0.0, NEG)


def by_head(turned, heads):
    if heads == 1:
        return [turned]
    row = lax.broadcasted_iota(jnp.int32, turned.shape, 0) // HEAD_DIM
    return [jnp.where(row == h, turned, jnp.zeros_like(turned)) for h in range(heads)]


def query_rows(queries, ids, docs, heads):
    unit, _ = documents(ids, docs)
    turned = queries.astype(F32).T
    return tuple(
        jnp.concatenate([part.astype(BF16), unit], axis=0) for part in by_head(turned, heads)
    )


def key_documents(ids_ref, k_s, wide, docs):
    for t in range(ids_ref.shape[0]):
        _, keys = documents(ids_ref[t], docs)
        k_s[t * TILE : (t + 1) * TILE, wide:] = keys.T.astype(BF16)


def attend_row(heads, docs, tiles, ids, lse, q_s, k_s, v_s, vt_s, o_s, whole_s):
    for t in range(tiles):
        vt_s[:, t * TILE : (t + 1) * TILE] = transposed(v_s[t * TILE : (t + 1) * TILE, :])

    def start(i):
        blank = (
            jnp.full((1, TILE), NEG, F32),
            jnp.zeros((1, TILE), F32),
            jnp.zeros((HEAD_DIM, TILE), F32),
        )
        return query_rows(q_s[span(i * TILE, TILE), :], ids[i], docs, heads), (blank,) * heads

    def step(i, at, size, diagonal, carry):
        queries, states = carry
        there = span(at, size)
        keys = k_s[there, :]
        new = []
        for h in range(heads):
            top, total, acc = states[h]
            s = dot(keys, queries[h])
            if diagonal is not None:
                s = jnp.where(causal(size, diagonal), s, NEG)
            top2 = jnp.maximum(top, jnp.max(s, axis=0, keepdims=True))
            p = jnp.exp(s - top2)
            fade = jnp.exp(top - top2)
            total = total * fade + jnp.sum(p, axis=0, keepdims=True)
            vt = vt_s[h * HEAD_DIM : (h + 1) * HEAD_DIM, there]
            acc = acc * fade + dot(vt, p.astype(BF16))
            new.append((top2, total, acc))
        return queries, tuple(new)

    def finish(i, carry):
        pieces = []
        for h in range(heads):
            top, total, acc = carry[1][h]
            pieces.append(acc * (1.0 / total))
            lse[i, h : h + 1, :] = top + jnp.log(total)
        context = jnp.concatenate(pieces, axis=0).T
        whole_s[span(i * TILE, TILE), :] = context
        o_s[span(i * TILE, TILE), :] = context.astype(BF16)

    sweep(tiles, lambda i: 0, start, step, finish)


def first_kernel(wide, docs, *refs):
    x_hbm, g_hbm, gain_ref, shift_ref, weight, bias_ref, dw_hbm, ids_ref = refs[:8]
    normed_ref, heads_hbm, context_hbm, ctx_hbm, lse_ref, slope_hbm = refs[8:14]
    w_s, stage, landed, x_ref, g_ref, dw, slope, q_s, k_s, v_s, vt_s, o_s, whole_s = refs[14:27]
    send_sem, recv_sem, load_sem = refs[27:]
    group = lax.axis_size("seq")
    me = lax.axis_index("seq")
    width = x_ref.shape[1]
    rows, tiles = ids_ref.shape[0], ids_ref.shape[1]
    cap = x_ref.shape[0] // rows
    heads = wide // HEAD_DIM
    hidden = dw.shape[0]
    links = Links(send_sem, recv_sem)
    first, second = links.reserve(rows * group), links.reserve(rows * group)
    order = list(range(group - 1, 0, -1)) + [0]
    used = [0]

    def local(src, dst):
        copy = pltpu.make_async_copy(src, dst, load_sem.at[used[0]])
        used[0] += 1
        copy.start()
        return copy

    held_x = [local(x_hbm.at[r, pl.ds(0, cap)], x_ref.at[pl.ds(r * cap, cap)]) for r in range(rows)]
    held_w = {}
    for m in order:
        source = flip(me, m)
        held_w[m] = [
            local(weight_view(weight, part, source, width, wide), w_s.at[m, part])
            for part in range(3)
        ]
    held_g = [local(g_hbm.at[r, pl.ds(0, cap)], g_ref.at[pl.ds(r * cap, cap)]) for r in range(rows)]
    held_g.append(local(dw_hbm, dw))
    for copy in held_x:
        copy.wait()
    n, _ = centre_rows(x_ref[...].astype(F32))
    normed_ref[...] = (n * gain_ref[...] + shift_ref[...]).astype(BF16)
    greet(range(1, group), [])

    for r in range(rows):
        here = slice(r * cap, (r + 1) * cap)
        for m in order:
            if r == 0:
                for copy in held_w[m]:
                    copy.wait()
            joined = jnp.concatenate([w_s[m, part] for part in range(3)], axis=1)
            value = (dot(normed_ref[here, :], joined) + bias_ref[flip(me, m)]).astype(BF16)
            if m:
                stage[m, here, :] = value
                links.start(
                    stage.at[m, here],
                    landed.at[m, here],
                    first + r * group + m,
                    first + r * group + m,
                    {"seq": flip(me, m)},
                )
            else:
                landed[0, here, :] = value

    for copy in held_g:
        copy.wait()
    block = min(512, hidden)

    def before(f):
        at = pl.ds(pl.multiple_of(f * block, block), block)
        slope[:, at] = dot(g_ref[...], dw[at, :], NT).astype(BF16)

    loop(0, hidden // block, before)
    leaving = [local(slope, slope_hbm)]
    blank_rest(group * cap, q_s, k_s, v_s)
    for r in range(rows):
        here = slice(r * cap, (r + 1) * cap)
        for m in range(1, group):
            links.arrived(landed.at[m, here], first + r * group + m, {"seq": flip(me, m)})
        for m in range(group):
            there = pl.ds(pl.multiple_of(flip(me, m) * cap, math.gcd(cap, 128)), cap)
            q_s[there, :] = landed[m, here, :wide] * SCALE
            k_s[there, :wide] = landed[m, here, wide : 2 * wide]
            v_s[there, :] = landed[m, here, 2 * wide :]
        key_documents(ids_ref.at[r], k_s, wide, docs)
        attend_row(heads, docs, tiles, ids_ref.at[r], lse_ref.at[r], q_s, k_s, v_s, vt_s, o_s.at[r], whole_s.at[r])
        for m in order:
            src = o_s.at[r, pl.ds(pl.multiple_of(flip(me, m) * cap, math.gcd(cap, 128)), cap)]
            if m:
                links.start(
                    src,
                    ctx_hbm.at[m, here],
                    second + r * group + m,
                    second + r * group + m,
                    {"seq": flip(me, m)},
                )
            else:
                leaving.append(local(src, ctx_hbm.at[0, here]))
        leaving.append(local(whole_s.at[r], context_hbm.at[r]))
    leaving.append(local(landed, heads_hbm))
    for r in range(rows):
        here = slice(r * cap, (r + 1) * cap)
        for m in range(1, group):
            links.arrived(ctx_hbm.at[m, here], second + r * group + m, {"seq": flip(me, m)})
    links.drain()
    for copy in leaving:
        copy.wait()


def project_attend(branch, cap, docs, x, g, gain, shift, weight, bias_parts, dw, ids):
    slots, width = x.shape[0], x.shape[2]
    rows = slots * cap
    group = bias_parts.shape[0]
    wide = width // group
    cols = 3 * wide
    tiles = ids.shape[1]
    length = tiles * TILE
    heads = wide // HEAD_DIM
    hidden = dw.shape[0]
    here = any_spec()
    anywhere = pl.BlockSpec(memory_space=pl.ANY)
    shape = jax.ShapeDtypeStruct
    vmem = lambda dims, kind=BF16: pltpu.VMEM(dims, kind)
    pair = slots * heads * length * length // 2
    return pl.pallas_call(
        functools.partial(first_kernel, wide, docs),
        in_specs=[anywhere, anywhere, here, here, anywhere, here, anywhere, here],
        out_specs=[here, anywhere, anywhere, anywhere, here, anywhere],
        out_shape=[
            shape((rows, width), BF16),
            shape((group, rows, cols), BF16),
            shape((slots, length, wide), F32),
            shape((group, rows, wide), BF16),
            shape((slots, tiles, heads, TILE), F32),
            shape((rows, hidden), BF16),
        ],
        scratch_shapes=[
            vmem((group, 3, width, wide)),
            vmem((group, rows, cols)),
            vmem((group, rows, cols)),
            vmem((rows, width)),
            vmem((rows, width)),
            vmem((hidden, width)),
            vmem((rows, hidden)),
            vmem((length, wide)),
            vmem((length, wide + 128)),
            vmem((length, wide)),
            vmem((wide, length)),
            vmem((slots, length, wide)),
            vmem((slots, length, wide), F32),
            pltpu.SemaphoreType.DMA((2 * slots * group,)),
            pltpu.SemaphoreType.DMA((2 * slots * group,)),
            pltpu.SemaphoreType.DMA((4 * slots + 3 * group + 3,)),
        ],
        compiler_params=params(collective_id=3 * branch + 1, has_side_effects=True),
        cost_estimate=pl.CostEstimate(
            flops=2 * rows * width * (cols * group + hidden) + 4 * 256 * pair,
            bytes_accessed=2 * group * cols * (width + rows) + 2 * hidden * width,
            transcendentals=pair,
        ),
        name="project_attend",
    )(x, g, gain[None], shift[None], weight, bias_parts, dw, ids)


def attend_back_kernel(group, cap, tiles, heads, docs, sc_ref, *refs):
    parts, ctx, grads, ids_ref, lse_ref, out_ref = refs[:6]
    refs = refs[6:]
    q_s, k_s, v_s, kt_s, g_s, dq_s, dk_s, dv_s = refs
    wide = heads * HEAD_DIM
    me = sc_ref[0]
    row = pl.program_id(0)
    load_heads(me, cap, parts, q_s, k_s, v_s)
    key_documents(ids_ref.at[0], k_s, wide, docs)
    blank_rest(group * cap, g_s)
    for m in range(group):
        here = pl.ds(pl.multiple_of((me ^ m) * cap, math.gcd(cap, 128)), cap)
        g_s[here, :] = grads[m]
    for t in range(tiles):
        kt_s[:, t * TILE : (t + 1) * TILE] = transposed(k_s[t * TILE : (t + 1) * TILE, :wide])
    dk_s[...] = jnp.zeros_like(dk_s)
    dv_s[...] = jnp.zeros_like(dv_s)

    def start(i):
        at = span(i * TILE, TILE)
        queries = q_s[at, :]
        grad = g_s[at, :]
        product = (grad.astype(F32) * ctx[0, at, :]).T
        delta = tuple(
            jnp.sum(product[h * HEAD_DIM : (h + 1) * HEAD_DIM], axis=0, keepdims=True)
            for h in range(heads)
        )
        split_q = tuple(only_head(queries, h, heads) for h in range(heads))
        split_g = tuple(only_head(grad, h, heads) for h in range(heads))
        turned_q = query_rows(queries, ids_ref[0, i], docs, heads)
        turned_g = tuple(part.astype(BF16) for part in by_head(grad.astype(F32).T, heads))
        fixed = (split_q, split_g, turned_q, turned_g, delta)
        return fixed, tuple(jnp.zeros((HEAD_DIM, TILE), F32) for _ in range(heads))

    def step(i, at, size, diagonal, carry):
        fixed, sums = carry
        split_q, split_g, turned_q, turned_g, delta = fixed
        there = span(at, size)
        keys = k_s[there, :]
        values = v_s[there, :]
        new, ps, dss = [], [], []
        for h in range(heads):
            s = dot(keys, turned_q[h]) - lse_ref[0, i, h : h + 1, :]
            if diagonal is not None:
                s = jnp.where(causal(size, diagonal), s, NEG)
            p = jnp.exp(s)
            dp = dot(values, turned_g[h])
            ds = (p * (dp - delta[h])).astype(BF16)
            ps.append(p.astype(BF16))
            dss.append(ds)
            kt = kt_s[h * HEAD_DIM : (h + 1) * HEAD_DIM, there]
            new.append(sums[h] + dot(kt, ds))
        dv = dot(ps[0], split_g[0])
        dk = dot(dss[0], split_q[0])
        for h in range(1, heads):
            dv = dv + dot(ps[h], split_g[h])
            dk = dk + dot(dss[h], split_q[h])
        dv_s[there, :] += dv
        dk_s[there, :] += dk
        return fixed, tuple(new)

    def finish(i, carry):
        dq_s[span(i * TILE, TILE), :] = (jnp.concatenate(carry[1], axis=0).T * SCALE).astype(BF16)

    sweep(tiles, lambda i: sc_ref[1 + row * tiles + i], start, step, finish)
    for m in range(group):
        here = pl.ds(pl.multiple_of((me ^ m) * cap, math.gcd(cap, 128)), cap)
        out_ref[m, :, :wide] = dq_s[here, :]
        out_ref[m, :, wide : 2 * wide] = dk_s[here, :].astype(BF16)
        out_ref[m, :, 2 * wide :] = dv_s[here, :].astype(BF16)


def attend_back(scalars, parts, ctx, grads, ids, lse, docs, cap, heads):
    group, tokens, cols = parts.shape
    rows = tokens // cap
    tiles = pl.cdiv(group * cap, TILE)
    length = tiles * TILE
    wide = heads * HEAD_DIM
    deep = wide + 128
    pair = rows * heads * length * length // 2
    by_row = lambda r, sc: (0, r, 0)
    all_row = lambda r, sc: (r, 0, 0, 0)
    return pl.pallas_call(
        functools.partial(attend_back_kernel, group, cap, tiles, heads, docs),
        grid_spec=pltpu.PrefetchScalarGridSpec(
            num_scalar_prefetch=1,
            grid=(rows,),
            in_specs=[pl.BlockSpec((group, cap, cols), by_row)]
            + [pl.BlockSpec((1, length, wide), lambda r, sc: (r, 0, 0))]
            + [pl.BlockSpec((group, cap, wide), by_row)]
            + [pl.BlockSpec((1, tiles, 1, TILE), all_row)]
            + [pl.BlockSpec((1, tiles, heads, TILE), lambda r, sc: (r, 0, 0, 0))],
            out_specs=pl.BlockSpec((group, cap, cols), by_row),
            scratch_shapes=[
                pltpu.VMEM((length, wide), BF16),
                pltpu.VMEM((length, deep), BF16),
                pltpu.VMEM((length, wide), BF16),
                pltpu.VMEM((wide, length), BF16),
            ]
            + [pltpu.VMEM((length, wide), BF16)] * 2
            + [pltpu.VMEM((length, wide), F32)] * 2,
        ),
        out_shape=jax.ShapeDtypeStruct((group, rows * cap, cols), BF16),
        compiler_params=params(),
        cost_estimate=pl.CostEstimate(
            flops=10 * 256 * pair, bytes_accessed=20 * rows * length * wide, transcendentals=pair
        ),
        name="attend_back",
    )(scalars, parts, ctx, grads, ids, lse)


def norm_back(upper, n, rs, gain):
    e = upper * gain
    return rs * (
        e - jnp.mean(e, axis=-1, keepdims=True) - n * jnp.mean(e * n, axis=-1, keepdims=True)
    )


GELU_A = 0.7978845608028654
GELU_B = 0.044715


VECTORS = 10


def early_cols(cols, late):
    early = cols * 3 // 4
    return cols - early if late else early


def mid_kernel(wide, *refs):
    grid = Grid()
    group, ys, xs, zs = grid.seq, grid.y, grid.x, grid.z
    refs = list(refs)

    def take(n):
        out = refs[:n]
        del refs[:n]
        return out

    ctx_hbm, x_hbm, g_hbm, slope_hbm, ow_hbm, uw_hbm, dw_hbm, ob, gain, shift, ub, db = take(12)
    grads, result_ref, mg_ref, early = take(4)
    down_out, up_out, out_out = take(2 * ys), take(xs + ys), take(zs)
    gots = take(3)
    x_ref, g_ref, landed, ctx, ow, uw, dw, hid, rise, mid_s, n2_s, normed, attn, chunk = take(14)
    rings, loaded, lefts = take(3), take(3), take(6)
    send_sem, recv_sem, load_sem, ring_sem, got_sem = take(5)

    me, dp = lax.axis_index("seq"), lax.axis_index("dp")
    core, row = dp % 2, dp // 2
    links = Links(send_sem, recv_sem)
    tokens, width = x_ref.shape
    hidden = hid.shape[1]
    block = min(512, hidden)
    partner_core = {"dp": flip(dp, 1)}
    loads = [
        pltpu.make_async_copy(src, dst, load_sem.at[k])
        for k, (src, dst) in enumerate(
            ((ow_hbm, ow), (ctx_hbm, landed), (uw_hbm, uw), (slope_hbm, rise), (dw_hbm, dw))
        )
    ]
    held = row_copies(g_hbm, g_ref, load_sem, 5) + row_copies(x_hbm, x_ref, load_sem, 5 + x_hbm.shape[0])
    for copy in loads[:2] + held + loads[2:]:
        copy.start()
    greet(range(1, group), [1])
    for copy in held + loads[:2]:
        copy.wait()
    early[...] = jnp.zeros_like(early)
    early[5:6, :] = jnp.sum(g_ref[...].astype(F32), axis=0, keepdims=True)

    def lanes(f, size):
        return pl.ds(pl.multiple_of(f * size, size), size)

    for s in range(group):
        chunk[s] = landed[flip(me, s)]
    for s in range(group):
        ctx[:, s * wide : (s + 1) * wide] = chunk[s]
    mid = x_ref[...].astype(F32) + dot(ctx[...], ow[...]) + ob[...]
    mid_s[...] = mid
    n, _ = centre_rows(mid)
    normed[...] = (n * gain[...] + shift[...]).astype(BF16)
    n2_s[...] = jnp.zeros_like(n2_s)
    for copy in loads[2:4]:
        copy.wait()

    def through(f, _):
        here = lanes(f, block)
        u = dot(normed[...], uw[:, here]) + ub[:, here]
        square = u * u
        t = jnp.tanh(GELU_A * u * (1.0 + GELU_B * square))
        half = 0.5 * (1.0 + t)
        hid[:, here] = (u * half).astype(BF16)
        slope = half + 0.5 * GELU_A * u * (1.0 - t * t) * (1.0 + 3.0 * GELU_B * square)
        up = (rise[:, here].astype(F32) * slope).astype(BF16)
        rise[:, here] = up
        n2_s[...] += dot(up, uw[:, here], NT)
        return 0

    def ordered(ring, spot, total, parts, share, got):
        for s in range(parts):
            rel = flip(me % parts, s)
            piece = total[s * share : (s + 1) * share]
            if got is not None:
                piece = piece + got[rel % xs, rel // xs].astype(F32)
            ring[spot, rel % xs, rel // xs] = piece.astype(BF16)

    def outputs(item, o, z, cols, ring):
        if item == 0:
            first = down_out[0].shape[-1]
            for h, here in enumerate((slice(0, first), slice(first, width))):
                yield ring.at[:, :, :, here], down_out[2 * o + h].at[:, z]
        elif item == 1:
            first = up_out[0].shape[-1]
            if cols.start >= first:
                here = slice(cols.start - first, cols.stop - first)
                yield ring, up_out[xs + o].at[:, :, :, here]
            else:
                for x in range(xs):
                    yield ring.at[x], up_out[x].at[o, :, :, cols]
        else:
            for z in range(zs):
                yield ring.at[:, z], out_out[z].at[o]

    def weight_grad(item, a, b):
        share = a.shape[1] // (2 * ys * group)
        parts = min(group, max(256 // share, xs))
        sub = group // parts
        depth = parts // xs
        cols = b.shape[1]
        piece = min(1024, cols)
        pieces = cols // piece
        count = ys * sub * pieces
        ring, got, left_s = rings[item], loaded[item], lefts[2 * item : 2 * item + 2]
        spots = ring.shape[0] // 2
        slot = links.reserve(count)

        def unit(n):
            u = n // pieces
            return ys - 1 - u // sub, u % sub, n % pieces

        def start_of(c, n):
            o, k, _ = unit(n)
            at = (flip(row, o, ys) * 2 + flip(core, c, 2)) * group * share
            return at + flip(me // parts, k, sub) * parts * share

        def product(c, n):
            o, k, p = unit(n)
            left = left_s[c]

            @pl.when(p == 0)
            def _():
                at = pl.multiple_of(start_of(c, n), 128)
                left[...] = transposed(a[:, pl.ds(at, parts * share)])

            return dot(left[...], b[:, pl.ds(pl.multiple_of(p * piece, piece), piece)])

        def place(n):
            o, k, p = unit(n)
            columns = pl.ds(pl.multiple_of(p * piece, piece), piece)
            return (o, slice(None), pl.ds(k * depth, depth), slice(None), columns)

        def away(n):
            links.left(ring.at[n % spots], slot + n, partner_core)

        def send(n):
            @pl.when(n >= spots)
            def _():
                away(n - spots)

            ordered(ring, n % spots, product(1, n), parts, share, None)
            there = gots[item].at[place(n)]
            links.start(ring.at[n % spots], there, slot + n, slot + n, partner_core, later=False)

        def fetch(n):
            src = gots[item].at[place(n)]
            return pltpu.make_async_copy(src, got.at[n % 2], got_sem.at[2 * item + n % 2])

        def fetch_start(n):
            links.arrived(gots[item].at[place(n)], slot + n, partner_core)
            fetch(n).start()

        def written(n, act):
            for fixed in range(ys):
                for p in range(pieces):
                    o, k, q = unit(n)

                    @pl.when((o == fixed) & (q == p))
                    def _(fixed=fixed, p=p):
                        spot = spots + n % spots
                        z = pl.ds(k * depth, depth)
                        here = slice(p * piece, (p + 1) * piece)
                        copies = outputs(item, fixed, z, here, ring.at[spot])
                        for h, (src, dst) in enumerate(copies):
                            at = (item * spots + n % spots) * max(2, xs, zs) + h
                            act(pltpu.make_async_copy(src, dst, ring_sem.at[at]))

        def keep(n):
            @pl.when(n + 1 < count)
            def _():
                fetch_start(n + 1)

            @pl.when(n >= spots)
            def _():
                written(n - spots, lambda copy: copy.wait())

            total = product(0, n)
            fetch(n).wait()
            ordered(ring, spots + n % spots, total, parts, share, got.at[n % 2])
            written(n, lambda copy: copy.start())

        def rest(act):
            for n in range(max(0, count - spots), count):
                act(n)

        def finish():
            rest(lambda n: written(n, lambda copy: copy.wait()))

        return count, send, lambda: rest(away), fetch_start, keep, finish, start_of

    first_job = weight_grad(0, hid, g_ref)
    steps = hidden // block
    per = first_job[0] * 2 // steps

    def mine(i):
        c = 1 - 2 * i // steps
        f = first_job[6](c, (i % (steps // 2)) * per) // block
        through(f, 0)

        @pl.when(c == 1)
        def _():
            for k in range(per):
                first_job[1](i * per + k)

    loop(0, steps, mine)
    first_job[2]()
    n, rs = centre_rows(mid_s[...])
    n2 = n2_s[...]
    early[3:4, :] = jnp.sum(n2 * n, axis=0, keepdims=True)
    early[4:5, :] = jnp.sum(n2, axis=0, keepdims=True)
    mid_grad = g_ref[...].astype(F32) + norm_back(n2, n, rs, gain[...])
    mg_ref[...] = mid_grad
    attn[...] = mid_grad.astype(BF16)
    full = dot(attn[...], ow[...], NT).astype(BF16)
    for s in range(group):
        chunk[flip(me, s)] = full[:, s * wide : (s + 1) * wide]
    second = links.reserve(group)
    for m in range(group - 1, 0, -1):
        links.start(chunk.at[m], grads.at[m], second + m, second + m, {"seq": flip(me, m)})
    own = pltpu.make_async_copy(chunk.at[0], grads.at[0], load_sem.at[0])
    own.start()

    jobs = [first_job, weight_grad(1, normed, rise), weight_grad(2, ctx, attn)]
    for stage in range(1, len(jobs) + 1):
        new = jobs[stage] if stage < len(jobs) else None
        old = jobs[stage - 1]
        old[3](0)

        def turn(n, new=new, old=old):
            for job, act in ((new, 1), (old, 4)):
                if job:
                    if new and old and job[0] < max(new[0], old[0]):
                        pl.when(n < job[0])(lambda job=job, act=act: job[act](n))
                    else:
                        job[act](n)

        loop(0, max(job[0] for job in (new, old) if job), turn)
        if new:
            new[2]()
        old[5]()


    loads[4].wait()

    def finished(k):
        here = lanes(k, 256)
        mid_s[:, here] = mid_s[:, here] + (dot(hid[...], dw[:, here]) + db[:, here])

    loop(0, width // 256, finished)
    cap = tokens // result_ref.shape[0]
    for r in range(result_ref.shape[0]):
        put_rows(result_ref, r, cap, mid_s[r * cap : (r + 1) * cap, :])
    early[2:3, :] = jnp.sum(attn[...].astype(F32), axis=0, keepdims=True)
    for k in range(hidden // width):
        part = rise[:, k * width : (k + 1) * width].astype(F32)
        early[6 + k : 7 + k, :] = jnp.sum(part, axis=0, keepdims=True)
    for m in range(1, group):
        links.arrived(grads.at[m], second + m, {"seq": flip(me, m)})
    own.wait()
    links.drain()


def feed_forward(branch, cap, ctx, x, g, slope, ow, ob, gain, shift, uw, ub, dw, db):
    grid = Grid()
    group, ys, xs, zs = grid.seq, grid.y, grid.x, grid.z
    rows, width = x.shape[0] * cap, x.shape[2]
    wide = width // group
    hidden = uw.shape[1]
    here = any_spec()
    anywhere = pl.BlockSpec(memory_space=pl.ANY)
    shape = jax.ShapeDtypeStruct
    low, high = width // (grid.dp * group), hidden // (grid.dp * group)
    vectors = VECTORS + group
    vectors += -vectors % 8
    sums = [
        shape((ys, xs, zs, high, width), BF16),
        shape((ys, xs, zs, low, hidden), BF16),
        shape((ys, xs, zs, low, width), BF16),
    ]
    parts = lambda share: min(group, max(256 // share, xs))
    block = lambda share: (xs, parts(share) // xs, share, width)
    rings = [pltpu.VMEM((n,) + block(share), BF16) for n in (4, 2) for share in (high, low, low)]
    turned = [pltpu.VMEM((parts(s) * s, rows), BF16) for s in (high, low, low) for _ in range(2)]
    blocks = ys * (group // parts(high)) + ys * (hidden // width) + ys
    vmem = lambda dims, kind=BF16: pltpu.VMEM(dims, kind)
    return pl.pallas_call(
        functools.partial(mid_kernel, wide),
        in_specs=[anywhere] * 7 + [here] * 5,
        out_specs=[anywhere, here, here, here] + [anywhere] * (3 * ys + xs + zs + 3),
        out_shape=[
            shape((group, rows, wide), BF16),
            shape(x.shape, BF16),
            shape((rows, width), F32),
            shape((vectors, width), F32),
        ]
        + [shape((xs, zs, high, early_cols(width, k)), BF16) for _ in range(ys) for k in range(2)]
        + [shape((ys, zs, low, early_cols(hidden, 0)), BF16)] * xs
        + [shape((xs, zs, low, early_cols(hidden, 1)), BF16)] * ys
        + [shape((ys, xs, low, width), BF16)] * zs
        + sums,
        scratch_shapes=[
            vmem((rows, width)),
            vmem((rows, width)),
            vmem((group, rows, wide)),
            vmem((rows, width)),
            vmem((width, width)),
            vmem((width, hidden)),
            vmem((hidden, width)),
            vmem((rows, hidden)),
            vmem((rows, hidden)),
            vmem((rows, width), F32),
            vmem((rows, width), F32),
            vmem((rows, width)),
            vmem((rows, width)),
            vmem((group, rows, wide)),
        ]
        + rings
        + turned
        + [
            pltpu.SemaphoreType.DMA((2 * group + blocks,)),
            pltpu.SemaphoreType.DMA((2 * group + blocks,)),
            pltpu.SemaphoreType.DMA((5 + 2 * x.shape[0],)),
            pltpu.SemaphoreType.DMA((6 * max(2, xs, zs),)),
            pltpu.SemaphoreType.DMA((6,)),
        ],
        compiler_params=params(collective_id=3 * branch + 2, has_side_effects=True),
        cost_estimate=pl.CostEstimate(
            flops=8 * rows * width * width + 12 * rows * width * hidden,
            bytes_accessed=4 * width * width + 8 * width * hidden,
            transcendentals=rows * hidden,
        ),
        name="feed_forward",
    )(ctx, x, g, slope, ow, uw, dw, ob[None], gain[None], shift[None], ub[None], db[None])


def partner(axis, mask):
    return [(i, i ^ mask) for i in range(lax.axis_size(axis))]


def exchange(axis, blocks):
    grid = Grid()
    out = [blocks[0]]
    for r in range(1, grid.size[axis]):
        name, mask = ("dp", 2 * r) if axis == "y" else ("seq", grid.mask(axis, r))
        out.append(lax.ppermute(blocks[r], name, partner(name, mask)))
    return out


def item_counts(ys, xs, zs):
    return (ys - 1) + 5, (xs - 1) + 5, 7, 7, (zs - 1) + 4


def tail_kernel(wide, *refs):
    grid = Grid()
    group, ys, xs, zs = grid.seq, grid.y, grid.x, grid.z
    refs = list(refs)

    def take(n):
        out = refs[:n]
        del refs[:n]
        return out

    back, weight, normed_ref, x_hbm, mg_hbm, gain_ref, early_ref = take(7)
    down_in, down_rest = take(ys), take(ys)
    up_in, up_rest = take(xs), take(ys)
    out_in = take(zs)
    tg_ref, project_ref, down_ref, up_ref, out_ref, vec_ref = take(6)
    landed, w_s, x_s, mg_s, acc, turned, order = take(7)
    send_a, send_b, keep_a, keep_b, pair_a, pair_b = take(6)
    got_a1, got_b1, mid_a, mid_b, got_a2, got_b2, z_a, z_b, got_za, got_zb = take(10)
    items = [take(count) for count in item_counts(ys, xs, zs)]
    vec_s, vec_g = take(2)
    send_sem, recv_sem, load_sem = take(3)

    me, dp = lax.axis_index("seq"), lax.axis_index("dp")
    core, row = dp % 2, dp // 2
    links = Links(send_sem, recv_sem)
    tokens, width = normed_ref.shape
    share = project_ref.shape[1]
    partner_core = {"dp": flip(dp, 1)}
    loads = []

    def load(src, dst):
        copy = pltpu.make_async_copy(src, dst, load_sem.at[len(loads)])
        copy.start()
        loads.append(copy)
        return copy

    greet(range(1, group), [1] + [2 * r for r in range(1, ys)])

    first = links.reserve(group)
    for m in range(1, group):
        links.start(back.at[m], landed.at[m], first + m, first + m, {"seq": flip(me, m)})
    own = load(back.at[0], landed.at[0])
    down_a, up_a, down_b, up_b, out_a = items
    loaded = [
        [load(src, dst) for src, dst in zip(up_in, [up_a[xs - 1]] + up_a[: xs - 1])],
        [load(src, dst) for src, dst in zip(down_in, [down_a[ys - 1]] + down_a[: ys - 1])],
        [load(src, dst) for src, dst in zip(out_in, [out_a[zs - 1]] + out_a[: zs - 1])],
        [load(src, down_b[0].at[o]) for o, src in enumerate(down_rest)],
        [load(src, up_b[0].at[o]) for o, src in enumerate(up_rest)],
    ]

    cap = tokens // x_hbm.shape[0]
    own_x = [load(x_hbm.at[r, pl.ds(0, cap)], x_s.at[pl.ds(r * cap, cap)]) for r in range(x_hbm.shape[0])]
    own_mg = load(mg_hbm, mg_s)
    ahead = w_s.shape[0]
    weight_first = len(loads)

    def weight_copies(m):
        source = flip(me, m, group)
        return [
            pltpu.make_async_copy(
                weight_view(weight, part, source, width, wide),
                w_s.at[m % ahead, part],
                load_sem.at[weight_first + 3 * m + part],
            )
            for part in range(3)
        ]

    for m in range(ahead):
        for copy in weight_copies(m):
            copy.start()

    def summed(axis, block, got):
        return Summed(links, grid, axis, block, got)

    up_a1 = summed("y", up_a[xs - 1], up_a[xs])
    up_a2 = LineSum(links, grid, *up_a[xs + 1 :])
    down_a1 = summed("x", down_a[ys - 1], down_a[ys])
    down_a2 = LineSum(links, grid, *down_a[ys + 1 :])
    down_b1, down_b2 = summed("y", down_b[0], down_b[1]), summed("x", down_b[2], down_b[3])
    down_b3 = LineSum(links, grid, *down_b[4:])
    up_b1, up_b2 = summed("y", up_b[0], up_b[1]), summed("x", up_b[2], up_b[3])
    up_b3 = LineSum(links, grid, *up_b[4:])
    out_1 = summed("y", out_a[zs - 1], out_a[zs])
    out_2 = summed("x", out_a[zs + 1], out_a[zs + 2])
    lines = (up_a2, down_a2, up_b3, down_b3)
    for copies in loaded[3:]:
        for copy in copies:
            copy.wait()
    down_b1.send()
    up_b1.send()
    for copies, item, count, stage in (
        (loaded[0], up_a, xs, up_a1),
        (loaded[1], down_a, ys, down_a1),
        (loaded[2], out_a, zs, out_1),
    ):
        for copy in copies:
            copy.wait()
        add_into(item[count - 1], item[: count - 1])
        stage.send()

    for k in range(0, width, 256):
        turned[k : k + 256, :] = normed_ref[:, k : k + 256].astype(F32).T
    for c in range(2):
        for o in range(ys):

            def place(s, c=c, o=o):
                there = (flip(row, o) * 2 + flip(core, c)) * group + flip(me, s, group)
                rows = turned[pl.ds(pl.multiple_of(there * share, share), share), :]
                order[c, o, s % xs, s // xs] = rows.astype(BF16)

            loop(0, group, place)
    half = ys * group * share
    acc[...] = jnp.zeros_like(acc)
    vec_s[0] = early_ref[...]
    own.wait()

    pair_first = links.reserve(2 * group)
    a1 = SlotSum(links, grid, "y", group, keep_a, got_a1)
    a2 = SlotSum(links, grid, "x", group, mid_a, got_a2)
    b1 = SlotSum(links, grid, "x", group, keep_b, got_b1, inner=True)
    b2 = SlotSum(links, grid, "y", group, mid_b, got_b2)
    cut = 2 * wide

    def multiply(m):
        source = flip(me, m, group)

        @pl.when(m > 0)
        def _():
            links.arrived(landed.at[m], first + m, {"seq": source})

        for k, (send, keep, pair, cols) in enumerate(
            (
                (send_a, keep_a, pair_a, slice(0, cut)),
                (send_b, keep_b, pair_b, slice(cut, 3 * wide)),
            )
        ):
            grad = landed[m, :, cols]
            left = order[1].reshape(half, tokens)
            send[m] = dot(left, grad).reshape(send.shape[1:]).astype(BF16)
            slot = pair_first + 2 * m + k
            links.start(send.at[m], pair.at[m], slot, slot, partner_core, later=False)
            left = order[0].reshape(half, tokens)
            keep[m] = dot(left, grad).reshape(keep.shape[1:]).astype(BF16)
        block = landed[m]
        for copy in weight_copies(m):
            copy.wait()
        pieces = [w_s[m % ahead, part] for part in range(3)]
        acc[...] += dot(block, jnp.concatenate(pieces, axis=1), NT)

        @pl.when(m + ahead < group)
        def _():
            for copy in weight_copies(m + ahead):
                copy.start()

        sums = jnp.sum(block.astype(F32), axis=0, keepdims=True)
        vec_s[0, pl.ds(VECTORS + source, 1), : 3 * wide] = sums

    def paired(m):
        for k, (keep, pair, nxt) in enumerate(((keep_a, pair_a, a1), (keep_b, pair_b, b1))):
            links.arrived(pair.at[m], pair_first + 2 * m + k, partner_core)
            keep[m] = total_of(keep[m], [pair[m]], BF16)
            nxt.send(m)

    def second(m):
        mid_a[m] = a1.receive(m).astype(BF16)
        a2.send(m)
        mid_b[m] = b1.receive(m).astype(BF16)
        b2.send(m)

    def third(m):
        for block, stage in ((z_a, a2), (z_b, b2)):
            total = stage.receive(m).astype(BF16)
            for z in range(zs):
                block[z, m] = total[z]

    def input_grads():
        for copy in own_x:
            copy.wait()
        own_mg.wait()
        n, rs = centre_rows(x_s[...].astype(F32))
        n1 = acc[...]
        grad = mg_s[...] + norm_back(n1, n, rs, gain_ref[...])
        for r in range(tg_ref.shape[0]):
            put_rows(tg_ref, r, cap, grad[r * cap : (r + 1) * cap])
        vec_s[0, 0:1, :] = jnp.sum(n1 * n, axis=0, keepdims=True)
        vec_s[0, 1:2, :] = jnp.sum(n1, axis=0, keepdims=True)

    vec_first = links.reserve(1 + (ys - 1) + (xs - 1) + (zs - 1))
    hops = [[partner_core]]
    for axis in ("y", "x", "z"):
        hops.append([grid.device(axis, r) for r in range(1, grid.size[axis])])

    def vec_send(k):
        at = vec_first + sum(len(h) for h in hops[:k])
        for r, device in enumerate(hops[k]):
            links.start(vec_s.at[k], vec_g.at[at + r - vec_first], at + r, at + r, device)

    def vec_receive(k):
        at = vec_first + sum(len(h) for h in hops[:k])
        got = []
        for r, device in enumerate(hops[k]):
            links.arrived(vec_g.at[at + r - vec_first], at + r, device)
            got.append(vec_g[at + r - vec_first])
        total = total_of(vec_s[k], got, F32)
        if k + 1 < len(hops):
            vec_s[k + 1] = total
            vec_send(k + 1)
        else:
            vec_ref[...] = total

    def multiply_next(m):
        multiply(m)

        @pl.when(m > 0)
        def _():
            paired(m - 1)

    loop(0, group // 2 + 1, multiply_next)
    down_b1.receive(down_b[2])
    down_b2.send()
    loop(group // 2 + 1, group, multiply_next)
    paired(group - 1)
    down_a1.receive(down_a[ys + 1])
    down_a2.hop(0)
    up_b1.receive(up_b[2])
    up_b2.send()
    up_a1.receive(up_a[xs + 1])
    up_a2.hop(0)
    input_grads()
    vec_send(0)
    out_1.receive(out_a[zs + 1])
    out_2.send()
    down_b2.receive(down_b[4])
    down_b3.hop(0)
    for k in range(1, zs - 1):
        down_a2.hop(k)
        up_a2.hop(k)
    vec_receive(0)
    loop(0, group // 2, second)
    for k in range(1, zs - 1):
        down_b3.hop(k)
    loop(group // 2, group, second)
    vec_receive(1)
    up_b2.receive(up_b[4])
    up_b3.hop(0)
    loop(0, group // 2, third)
    for k in range(1, zs - 1):
        up_b3.hop(k)
    loop(group // 2, group, third)

    z_first = links.reserve(2 * (zs - 1))
    for r in range(1, zs):
        for k, (block, got) in enumerate(((z_a, got_za), (z_b, got_zb))):
            slot = z_first + 2 * (r - 1) + k
            links.start(block.at[r], got.at[r - 1], slot, slot, grid.device("z", r))
    vec_receive(2)
    cut_down, cut_up = early_cols(down_ref.shape[1], 0), early_cols(up_ref.shape[1], 0)
    out_2.receive_last(out_ref)
    up_a2.finish(up_ref, slice(0, cut_up))
    down_a2.finish(down_ref, slice(0, cut_down))
    up_b3.finish(up_ref, slice(cut_up, up_ref.shape[1]))
    down_b3.finish(down_ref, slice(cut_down, down_ref.shape[1]))
    vec_receive(3)
    for r in range(1, zs):
        for k, got in enumerate((got_za, got_zb)):
            links.arrived(got.at[r - 1], z_first + 2 * (r - 1) + k, grid.device("z", r))

    def share_of(m):
        source = flip(me, m, group)
        for block, got, cols in (
            (z_a, got_za, slice(0, cut)),
            (z_b, got_zb, slice(cut, 3 * wide)),
        ):
            others = [got[r - 1, flip(m, grid.mask("z", r), group)] for r in range(1, zs)]
            project_ref[source, :, cols] = total_of(block[0, m], others, F32)

    loop(0, group, share_of)

    def drain(m):
        for k, send in enumerate((send_a, send_b)):
            links.left(send.at[m], pair_first + 2 * m + k, partner_core)
        for stage in (a1, a2, b1, b2):
            stage.drain(m)

    loop(0, group, drain)
    links.drain()


def tail(branch, back, normed, weight, x, mid_grad, gain, early, down, up, out):
    grid = Grid()
    group, ys, xs, zs = grid.seq, grid.y, grid.x, grid.z
    rows, width = normed.shape
    wide = width // group
    shape = jax.ShapeDtypeStruct
    any_place = pl.BlockSpec(memory_space=pl.ANY)
    here = any_spec()
    share = width // (grid.dp * grid.seq)
    (down, down_rest), (up, up_rest) = down, up
    down_block, up_block, out_block = down[0].shape, up[0].shape, out[0].shape
    vmem = lambda dims, kind=BF16: pltpu.VMEM(tuple(dims), kind)
    a_full, b_full = (share, 2 * wide), (share, wide)
    copies = (
        group
        + 2 * group
        + 2 * group * (ys - 1)
        + 2 * group * (xs - 1)
        + 4 * (xs - 1)
        + 4 * (ys - 1)
        + 8 * zs
        + (1 + (ys - 1) + (xs - 1) + (zs - 1))
        + 2 * (zs - 1)
    )
    hops = 1 + (ys - 1) + (xs - 1) + (zs - 1)
    scratch = (
        [
            vmem((group, rows, 3 * wide)),
            vmem((min(4, group), 3, width, wide)),
            vmem((rows, width)),
            vmem((rows, width), F32),
            vmem((rows, width), F32),
            vmem((width, rows), F32),
            vmem((2, ys, xs, zs, share, rows)),
        ]
        + [vmem((group, ys, xs, zs) + a_full), vmem((group, ys, xs, zs) + b_full)] * 3
        + [
            vmem((group, ys - 1, xs, zs) + a_full),
            vmem((group, xs - 1, ys, zs) + b_full),
            vmem((group, xs, zs) + a_full),
            vmem((group, ys, zs) + b_full),
            vmem((group, xs - 1, zs) + a_full),
            vmem((group, ys - 1, zs) + b_full),
            vmem((zs, group) + a_full),
            vmem((zs, group) + b_full),
            vmem((zs - 1, group) + a_full),
            vmem((zs - 1, group) + b_full),
        ]
        + [vmem(down_block)] * ys
        + [vmem((xs - 1,) + down_block[1:])]
        + [vmem(down_block[1:])] * 3
        + [vmem(up_block)] * xs
        + [vmem((ys - 1,) + up_block[1:])]
        + [vmem(up_block[1:])] * 3
        + [
            vmem((ys,) + down_rest[0].shape),
            vmem((ys - 1,) + down_rest[0].shape),
            vmem(down_rest[0].shape),
            vmem((xs - 1,) + down_rest[0].shape[1:]),
        ]
        + [vmem(down_rest[0].shape[1:])] * 3
        + [
            vmem((ys,) + up_rest[0].shape),
            vmem((ys - 1,) + up_rest[0].shape),
            vmem(up_rest[0].shape),
            vmem((xs - 1,) + up_rest[0].shape[1:]),
        ]
        + [vmem(up_rest[0].shape[1:])] * 3
        + [vmem(out_block)] * zs
        + [
            vmem((ys - 1,) + out_block[1:]),
            vmem(out_block[1:]),
            vmem((xs - 1,) + out_block[2:]),
        ]
        + [
            vmem((4,) + early.shape, F32),
            vmem((hops,) + early.shape, F32),
            pltpu.SemaphoreType.DMA((copies,)),
            pltpu.SemaphoreType.DMA((copies,)),
            pltpu.SemaphoreType.DMA((2 + x.shape[0] + 3 * ys + xs + zs + 3 * group,)),
        ]
    )
    return pl.pallas_call(
        functools.partial(tail_kernel, wide),
        in_specs=[any_place, any_place, here, any_place, any_place, here, here]
        + [any_place] * (3 * ys + xs + zs),
        out_specs=[here] * 6,
        out_shape=[
            shape(x.shape, BF16),
            shape((group, share, 3 * wide), F32),
            shape((down_block[2], width), F32),
            shape((up_block[2], up_block[3] + up_rest[0].shape[3]), F32),
            shape(out_block[2:], F32),
            shape(early.shape, F32),
        ],
        scratch_shapes=scratch,
        compiler_params=params(collective_id=3 * branch + 3, has_side_effects=True),
        cost_estimate=pl.CostEstimate(
            flops=12 * rows * width * width, bytes_accessed=2**25, transcendentals=0
        ),
        name="tail",
    )(back, weight, normed, x, mid_grad, gain[None], early, *down, *down_rest, *up, *up_rest, *out)


def prepare_kernel(exit_ref, offsets, limit, tokens, upstream, x_ref, g_ref, pick_ref, ids_ref, most_ref, *scratch):
    rank_s, live_s, mine_s, got, send_sem, recv_sem = scratch
    rows, shard, _ = tokens.shape
    group = ids_ref.shape[1]
    docs = offsets.shape[1]
    dp, me = lax.axis_index("dp"), lax.axis_index("seq")
    others = lax.axis_size("dp") - 1
    links = Links(send_sem, recv_sem)
    for r in range(rows):
        for s in range(group):
            live = exit_ref[r : r + 1, s * shard : (s + 1) * shard] > limit[0]
            live_s[r * group + s : r * group + s + 1, :] = jnp.where(live, 1.0, 0.0)
    before = lax.broadcasted_iota(jnp.int32, (shard, shard), 0)
    after = lax.broadcasted_iota(jnp.int32, (shard, shard), 1)
    ones = jnp.where(before <= after, 1.0, 0.0).astype(BF16)
    rank = dot(live_s[...].astype(BF16), ones)
    rank_s[...] = jnp.where(live_s[...] > 0.0, rank - 1.0, -1.0)
    mine_s[...] = jnp.broadcast_to(jnp.max(rank), mine_s.shape)
    greet([], range(1, others + 1))
    for m in range(1, others + 1):
        links.start(mine_s, got.at[m - 1], m - 1, m - 1, {"dp": flip(dp, m)})
    slot = before.astype(F32)
    for r in range(rows):
        here = rank_s[pl.ds(r * group + me, 1), :]
        pick = jnp.where(slot == here, 1.0, 0.0).astype(BF16)
        pick_ref[r] = pick
        x_ref[r] = dot(pick, tokens[r]).astype(BF16)
        g_ref[r] = dot(pick, upstream[r]).astype(BF16)
    seat = lax.broadcasted_iota(jnp.int32, (group, shard), 1)
    place = seat + shard * lax.broadcasted_iota(jnp.int32, (group, shard), 0)
    for r in range(rows):
        live = live_s[r * group : (r + 1) * group, :]
        ids = jnp.ones((group, shard), F32)
        for j in range(1, docs):
            ahead = jnp.where(place < offsets[r, j], live, 0.0)
            ahead = jnp.sum(ahead, axis=1, keepdims=True)
            ids = ids + jnp.where(seat.astype(F32) >= ahead, 1.0, 0.0)
        used = jnp.sum(live, axis=1, keepdims=True)
        ids = jnp.where(seat.astype(F32) < used, ids, 0.0)
        for s in range(group):
            ids_ref[r, s] = ids[s : s + 1]
    most = mine_s[...]
    for m in range(1, others + 1):
        links.arrived(got.at[m - 1], m - 1, {"dp": flip(dp, m)})
        most = jnp.maximum(most, got[m - 1])
    most_ref[...] = most
    links.drain()


def prepare(exit_layers, doc_offsets, layer_index, tokens, upstream):
    others = lax.axis_size("dp") - 1
    group = lax.axis_size("seq")
    rows, shard, width = tokens.shape
    shape = jax.ShapeDtypeStruct
    here, scalar = any_spec(), smem()
    return pl.pallas_call(
        prepare_kernel,
        in_specs=[here, scalar, scalar, here, here],
        out_specs=[here] * 5,
        out_shape=[
            shape(tokens.shape, BF16),
            shape(tokens.shape, BF16),
            shape((rows, shard, shard), BF16),
            shape((rows, group, 1, shard), F32),
            shape((8, 128), F32),
        ],
        scratch_shapes=[
            pltpu.VMEM((rows * group, shard), F32),
            pltpu.VMEM((rows * group, shard), F32),
            pltpu.VMEM((8, 128), F32),
            pltpu.VMEM((others, 8, 128), F32),
            pltpu.SemaphoreType.DMA((others,)),
            pltpu.SemaphoreType.DMA((others,)),
        ],
        compiler_params=params(collective_id=0, has_side_effects=True),
        name="prepare",
    )(exit_layers, doc_offsets, layer_index, tokens, upstream)


def layer(
    branch,
    cap,
    docs,
    x,
    g,
    ids,
    first_gain,
    first_shift,
    project_weight,
    query_bias,
    value_bias,
    output_weight,
    output_bias,
    second_gain,
    second_shift,
    up_weight,
    up_bias,
    down_weight,
    down_bias,
):
    group = lax.axis_size("seq")
    rows, shard, width = x.shape
    wide = width // group
    heads = wide // HEAD_DIM
    me = lax.axis_index("seq").astype(jnp.int32)
    tiles = pl.cdiv(group * cap, TILE)
    ids = ids[:, :, 0, :cap].reshape(rows, group * cap)
    ids = jnp.pad(ids, ((0, 0), (0, tiles * TILE - group * cap))).reshape(rows, tiles, 1, TILE)
    last = jnp.max(ids[:, :, 0], axis=2)
    first = jnp.min(jnp.where(ids == 0, docs + 1, ids)[:, :, 0], axis=2)
    number = jnp.arange(tiles, dtype=jnp.int32)
    needed = (last[:, None, :] >= first[:, :, None]) & (number < number[:, None])
    low = jnp.min(jnp.where(needed, number, number[:, None]), axis=2) // 2
    scalars = jnp.concatenate([me[None], low.reshape(-1)])
    biases = jnp.stack([query_bias, jnp.zeros_like(query_bias), value_bias])
    bias_parts = biases.reshape(3, group, wide).transpose(1, 0, 2).reshape(group, 1, 3 * wide)

    weight = split_weight(project_weight, group)
    normed, head_parts, context, ctx_parts, lse, slope = project_attend(
        branch, cap, docs, x, g, first_gain, first_shift, weight, bias_parts, down_weight, ids
    )
    grad_parts, result, middle_grad, early, *halves = feed_forward(
        branch,
        cap,
        ctx_parts,
        x,
        g,
        slope,
        output_weight,
        output_bias,
        second_gain,
        second_shift,
        up_weight,
        up_bias,
        down_weight,
        down_bias,
    )
    ys, xs = Grid().y, Grid().x
    down, up, out = halves[: 2 * ys], halves[2 * ys : 3 * ys + xs], halves[3 * ys + xs : -3]
    down_parts = exchange("y", down[0::2]), down[1::2]
    up_parts = exchange("x", up[:xs]), up[xs:]
    out_parts = exchange("z", out)
    back = attend_back(
        scalars, head_parts, context, grad_parts, ids, lse, docs, cap, heads
    )
    token_grad, project_share, down_share, up_share, out_share, sums = tail(
        branch, back, normed, weight, x, middle_grad, first_gain, early, down_parts, up_parts, out_parts
    )
    return (result, token_grad, project_share, out_share, up_share, down_share, sums)


CAPS = (12, 11, 13, 10, 16)


def per_device(tokens, *args):
    *weights, doc_offsets, exit_layers, layer_index, upstream = args
    rows, shard, width = tokens.shape
    group = lax.axis_size("seq")
    wide = width // group
    docs = doc_offsets.shape[1]
    x, g, pick, ids, most = prepare(exit_layers, doc_offsets, layer_index, tokens, upstream)
    caps = list(dict.fromkeys(pl.cdiv(shard * k, 256) * 16 for k in CAPS))
    count = jnp.maximum(most[0, 0], 1.0)
    branch = sum(
        jnp.where((count <= cap) & (count > max([0] + [c for c in caps if c < cap])), k, 0)
        for k, cap in enumerate(caps)
    )
    steps = [functools.partial(layer, k, cap, docs) for k, cap in enumerate(caps)]
    result, token_grad, project_share, out_share, up_share, down_share, sums = lax.switch(
        branch, steps, x, g, ids, *weights
    )
    me = lax.axis_index("seq").astype(jnp.int32)
    live = lax.dynamic_slice_in_dim(exit_layers, me * shard, shard, 1) > layer_index[0]

    def unpack(packed, values):
        spread = jnp.einsum("rct,rcd->rtd", pick, packed, preferred_element_type=F32)
        return jnp.where(live[:, :, None], spread.astype(BF16), values)

    project_share = project_share.reshape(group, -1, 3, wide).transpose(1, 2, 0, 3)
    devices = lax.axis_size("dp") * group
    index = lax.axis_index("dp").astype(jnp.int32) * group + me
    part = width // devices
    singles = lax.dynamic_slice(sums, (0, index * part), (6, part))
    high = up_share.shape[1] // devices
    at = index * high
    up_bias_share = lax.dynamic_slice(sums, (6 + at // width, at % width), (1, high))[0]
    at = index * part
    by_part = [
        lax.dynamic_slice(sums, (VECTORS + at // wide, k * wide + at % wide), (1, part))[0]
        for k in range(3)
    ]
    return (
        unpack(result, tokens),
        unpack(token_grad, upstream),
        singles[0],
        singles[1],
        project_share.reshape(-1, 3 * width),
        by_part[0],
        by_part[2],
        out_share,
        singles[2],
        singles[3],
        singles[4],
        up_share,
        up_bias_share,
        down_share,
        singles[5],
    )


def solution(mesh):
    rows = P("dp", "seq", None)
    shares = P(("dp", "seq"))
    wide_shares = P(("dp", "seq"), None)
    in_specs = (rows,) + (P(),) * 13 + (P("dp", None), P("dp", None), P(), rows)
    out_specs = (
        rows,
        rows,
        shares,
        shares,
        wide_shares,
        shares,
        shares,
        wide_shares,
        shares,
        shares,
        shares,
        wide_shares,
        shares,
        wide_shares,
        shares,
    )
    return jax.shard_map(
        per_device, mesh=mesh, in_specs=in_specs, out_specs=out_specs, check_vma=False
    )
```
